32 devices in a mesh: fsdp: 8 (over z, x), tensor: 4 (over y, core).
Axes of the slice: x: 2, y: 2, z: 4, core: 2. Of those that a mesh axis runs over, the one named last changes fastest.
Arguments:
- momentum: float32 [1920, 6144], P('fsdp', 'tensor'), may hold values from -100 to 100
- gradient: bfloat16 [1920, 6144], P('fsdp', 'tensor'), may hold values from -3 to 3
- right_basis: float32 [6144, 512], P('tensor'), may hold values from -0.078125 to 0.078125
Outputs:
- update: bfloat16 [1920, 6144], P('fsdp', 'tensor')
- new_momentum: float32 [1920, 6144], P('fsdp', 'tensor')
- left_scaled: float32 [1920, 512], P('fsdp')
- next_basis: float32 [6144, 512], P(('tensor', 'fsdp'))
The draws below stay inside these ranges and needn't reach their ends.
All inputs are finite; a program needn't handle non-finite values.
Results may differ from the reference program's by a relative error of at most 0.001.
Values sent between devices are 32-bit elements; how exact they have to be, the bound alone decides.
No kernel may reach another device: no remote copies, remote signals or barrier semaphores. Data moves between devices by JAX's collectives and lax.ppermute only.
A program may use at most 64 MiB of HBM per device.

```python
import math
import jax
import jax.numpy as jnp
from jax import lax

RANK = 512
N = 6144
M = 1920


def draw_momentum(key, part):
    key_noise, key_rows, key_cols = jax.random.split(key, 3)
    rising = jnp.exp(math.log(3.0) * jnp.arange(M, dtype=jnp.float32) / M)
    col_rising = jnp.exp(math.log(3.0) * jnp.arange(N, dtype=jnp.float32) / N)
    col_scale = col_rising * jnp.exp(jax.random.uniform(key_cols, (N,), jnp.float32, 0.0, math.log(10.0)))
    row_scale = jnp.exp(jax.random.uniform(key_rows, (M,), jnp.float32, 0.0, math.log(10.0)))
    noise = jnp.clip(jax.random.normal(key_noise, (M, N), jnp.float32), -4.0, 4.0)
    return 0.02 * (rising * row_scale)[:, None] * col_scale[None, :] * noise


def block_levels(own_key, dims, cuts, smallest, top_value):
    level, own = 1.0, jax.random.fold_in(own_key, 6)
    for axis_at, shards_of in cuts:
        draws = jnp.exp(jax.random.uniform(jax.random.fold_in(own, axis_at), (shards_of,), jnp.float32, smallest / len(cuts), top_value / len(cuts)))
        level = level * jnp.repeat(draws, dims[axis_at] // shards_of).reshape([-1 if axis == axis_at else 1 for axis in range(len(dims))])
    return level


def gaussian(stream_key, dims, deviation, bound, pieces=(), held_as=jnp.bfloat16):
    factor_of = block_levels(stream_key, dims, pieces, -0.22, 0.18) if pieces else 1.0
    entries = jax.random.normal(stream_key, dims, jnp.float32) * deviation * factor_of
    return jnp.minimum(jnp.maximum(entries, -bound), bound).astype(held_as)


def setup_inputs(seed: int = 0) -> dict:
    arg_keys = jax.random.split(jax.random.key(seed), 4)
    return {
        "momentum": draw_momentum(jax.random.fold_in(arg_keys[3], 71), 0),
        "gradient": gaussian(arg_keys[1], (M, N), 0.5, 3.0, ((0, 8), (1, 4))),
        "right_basis": gaussian(arg_keys[2], (N, RANK), N ** -0.5, 0.078125, ((0, 4),), jnp.float32),
    }


def reference(momentum, gradient, right_basis):
    highest = lax.Precision.HIGHEST
    summed = momentum + gradient.astype(jnp.float32)
    left_raw = jnp.dot(summed, right_basis, precision=highest)
    gram = jnp.dot(left_raw.T, left_raw, precision=highest)
    factor_lower = jnp.linalg.cholesky(gram)
    left = jax.scipy.linalg.solve_triangular(factor_lower, left_raw.T, lower=True).T
    right_factor = jnp.dot(summed.T, left, precision=highest)
    column_norm = jnp.sqrt(lax.optimization_barrier(jnp.sum(right_factor * right_factor, axis=0)) + 1e-06)
    next_basis = right_factor / column_norm[None, :]
    scaled_left = left * (math.sqrt(M / N) / column_norm)[None, :]
    update = jnp.dot(scaled_left, right_factor.T, precision=highest).astype(jnp.bfloat16)
    product = jnp.dot(left, right_factor.T, precision=highest)
    new_momentum = summed - 0.5 * product
    return (update, new_momentum, left * math.sqrt(M), next_basis)
```

```python
import functools
import math

import jax
import jax.numpy as jnp
from jax import lax
from jax.experimental import pallas as pl
from jax.experimental.pallas import tpu as pltpu
from jax.sharding import PartitionSpec as P

epsilon = 1e-06
highest = lax.Precision.HIGHEST
lanes = 128
panel = 8
square = 4


def dot(a, b, contract=((1,), (0,))):
    return lax.dot_general(
        a, b, (contract, ((), ())), precision=highest, preferred_element_type=jnp.float32
    )


def factor_block(block):
    size = block.shape[0]
    lane = lax.broadcasted_iota(jnp.int32, (panel, size), 1)
    row = lax.broadcasted_iota(jnp.int32, (panel, size), 0)
    for first in range(0, size, panel):
        count = size - first
        now = block[first:, :]
        columns = [
            jnp.broadcast_to(now[:, first + k : first + k + 1], (count, size)) for k in range(panel)
        ]
        inside = (lane >= first) & (lane < first + panel)
        head = jnp.where(inside, jnp.where(lane - first == row, 1.0, 0.0), now[:panel])
        tail = None
        if count > panel:
            lane_below = lax.broadcasted_iota(jnp.int32, (count - panel, size), 1)
            inside_below = (lane_below >= first) & (lane_below < first + panel)
            tail = jnp.where(inside_below, 0.0, now[panel:])
        for j in range(panel):
            inverse = lax.rsqrt(columns[j][j : j + 1, :])
            multiplier = columns[j] * inverse
            for k in range(j + 1, panel):
                columns[k] = columns[k] - multiplier * (columns[k][j : j + 1, :] * inverse)
            pivot = head[j : j + 1, :] * inverse
            below = jnp.where(row > j, head - multiplier[:panel] * pivot, head)
            head = jnp.where(row == j, pivot, below)
            if tail is not None:
                tail = tail - multiplier[panel:] * pivot
        block[first : first + panel, :] = head
        if tail is not None:
            block[first + panel :, :] = tail


def inverse_factor_kernel(gram_ref, out_ref, work, block):
    size = gram_ref.shape[0]
    count = size // lanes
    work[...] = gram_ref[...]
    row = lax.broadcasted_iota(jnp.int32, (lanes, lanes), 0)
    lower = row >= lax.broadcasted_iota(jnp.int32, (lanes, lanes), 1)
    column_block = lax.broadcasted_iota(jnp.int32, (lanes, size), 1) // lanes

    def step(b, carry):
        own_rows = pl.ds(pl.multiple_of(b * lanes, lanes), lanes)
        block[...] = work[own_rows, own_rows]
        factor_block(block)
        inverse = jnp.where(lower, block[...], 0.0)
        own = column_block == b
        work[own_rows, :] = dot(inverse, jnp.where(own, 0.0, work[own_rows, :]))
        work[own_rows, own_rows] = inverse
        out_ref[own_rows, :] = jnp.where(column_block <= b, work[own_rows, :], 0.0)

        def update(i, carry):
            rows = pl.ds(pl.multiple_of(i * lanes, lanes), lanes)
            change = dot(work[own_rows, rows], work[own_rows, :], ((0,), (0,)))
            work[rows, :] = jnp.where(own, 0.0, work[rows, :]) - change
            return carry

        return lax.fori_loop(b + 1, count, update, carry)

    lax.fori_loop(0, count, step, 0)


def inverse_factor(gram):
    size = gram.shape[0]
    return pl.pallas_call(
        inverse_factor_kernel,
        out_shape=jax.ShapeDtypeStruct((size, size), jnp.float32),
        scratch_shapes=[
            pltpu.VMEM((size, size), jnp.float32),
            pltpu.VMEM((lanes, lanes), jnp.float32),
        ],
        compiler_params=pltpu.CompilerParams(vmem_limit_bytes=32 * 2**20),
        cost_estimate=pl.CostEstimate(
            flops=12 * size**3, bytes_accessed=8 * size * size, transcendentals=size
        ),
        name="inverse_factor",
    )(gram)


def share_norms(right_rows):
    squares = lax.psum(jnp.sum(right_rows * right_rows, axis=0), ("fsdp", "tensor"))
    return jnp.sqrt(squares + epsilon)


def any_mesh(momentum, gradient, right_basis):
    summed = momentum + gradient.astype(jnp.float32)
    left_raw = lax.psum(dot(summed, right_basis), "tensor")
    gram = lax.psum(dot(left_raw, left_raw, ((0,), (0,))), "fsdp")
    inverse = inverse_factor(gram)
    left = dot(left_raw, inverse, ((1,), (1,)))
    total_rows = left.shape[0] * lax.axis_size("fsdp")
    total_cols = summed.shape[1] * lax.axis_size("tensor")
    raw_rows = lax.psum_scatter(
        dot(summed, left_raw, ((0,), (0,))), "fsdp", scatter_dimension=0, tiled=True
    )
    right_rows = dot(raw_rows, inverse, ((1,), (1,)))
    column_norm = share_norms(right_rows)
    scaled_left = left * (math.sqrt(total_rows / total_cols) / column_norm)[None, :]
    raw = lax.all_gather(raw_rows, "fsdp", axis=0, tiled=True)
    product = dot(dot(left, inverse), raw, ((1,), (1,)))
    update = dot(dot(scaled_left, inverse), raw, ((1,), (1,))).astype(jnp.bfloat16)
    new_momentum = summed - 0.5 * product
    return (update, new_momentum, left * math.sqrt(total_rows), right_rows / column_norm[None, :])


def swap(value, axis, flip):
    return lax.ppermute(value, axis, [(i, i ^ flip) for i in range(lax.axis_size(axis))])


def split_kernel(place, momentum, gradient, *pieces):
    width = pieces[0].shape[1]
    for k, piece in enumerate(pieces):
        at = pl.ds(pl.multiple_of((place[0] ^ k) * width, lanes), width)
        piece[...] = momentum[:, at] + gradient[:, at].astype(jnp.float32)


def split_sum(place, momentum, gradient):
    rows, cols = momentum.shape
    return pl.pallas_call(
        split_kernel,
        out_shape=[jax.ShapeDtypeStruct((rows, cols // square), jnp.float32)] * square,
        in_specs=[
            pl.BlockSpec(memory_space=pltpu.SMEM),
            pl.BlockSpec(memory_space=pltpu.VMEM),
            pl.BlockSpec(memory_space=pltpu.VMEM),
        ],
        compiler_params=pltpu.CompilerParams(vmem_limit_bytes=32 * 2**20),
        cost_estimate=pl.CostEstimate(
            flops=rows * cols, bytes_accessed=10 * rows * cols, transcendentals=0
        ),
        name="split_sum",
    )(place, momentum, gradient)


def ordered(bit, mine, other):
    first = jnp.where(bit == 0, mine, other)
    second = jnp.where(bit == 0, other, mine)
    return jnp.concatenate([first, second], axis=0)


def in_squares(momentum, gradient, right_basis):
    device = lax.axis_index("fsdp")
    place = device % square
    tensor = lax.axis_index("tensor")
    core, plane = tensor % 2, tensor // 2
    rows, cols = momentum.shape
    rank = right_basis.shape[1]
    half, width = rows // 2, cols // square
    total_rows = rows * lax.axis_size("fsdp")
    total_cols = cols * lax.axis_size("tensor")

    pieces = split_sum(place.reshape(1), momentum, gradient)
    columns = [pieces[0]] + [swap(pieces[k], "fsdp", k) for k in range(1, square)]

    summed = momentum + gradient.astype(jnp.float32)
    part = dot(summed, right_basis)
    sent = lax.dynamic_slice_in_dim(part, (1 - core) * half, half, 0)
    kept = lax.dynamic_slice_in_dim(part, core * half, half, 0)
    mine = kept + swap(sent, "tensor", 1)
    mine = mine + swap(mine, "tensor", 2)
    in_square = jnp.concatenate(
        [mine] + [swap(mine, "fsdp", k) for k in range(1, square)], axis=0
    )
    other = swap(in_square, "tensor", 1)

    part_gram = dot(in_square, in_square, ((0,), (0,)))
    count = rank // lanes
    blocks = [(i, j) for j in range(count) for i in range(j, count)]
    stack = jnp.concatenate(
        [part_gram[i * lanes : (i + 1) * lanes, j * lanes : (j + 1) * lanes] for i, j in blocks], axis=0
    )
    share = stack.shape[0] // 4
    sent = lax.dynamic_slice_in_dim(stack, (2 * plane + 1 - core) * share, share, 0)
    kept = lax.dynamic_slice_in_dim(stack, (2 * plane + core) * share, share, 0)
    quarter = kept + swap(sent, "tensor", 1)
    quarter = quarter + swap(quarter, "fsdp", square)
    over_cores = ordered(core, quarter, swap(quarter, "tensor", 1))
    stack = ordered(plane, over_cores, swap(over_cores, "tensor", 2))
    found = {}
    for at, (i, j) in enumerate(blocks):
        block = stack[at * lanes : (at + 1) * lanes]
        found[i, j] = block
        found[j, i] = block if i == j else block.T
    gram = jnp.concatenate(
        [jnp.concatenate([found[i, j] for j in range(count)], axis=1) for i in range(count)], axis=0
    )

    square_rows = jnp.concatenate(
        [ordered(core, in_square[k * half : (k + 1) * half], other[k * half : (k + 1) * half]) for k in range(square)],
        axis=0,
    )
    part_raw = dot(jnp.concatenate(columns, axis=0), square_rows, ((0,), (0,)))
    step = lanes
    raw = jnp.zeros((cols, rank), jnp.float32)
    own = []
    for at in range(0, width, step):
        share_raw = part_raw[at : at + step]
        share_raw = share_raw + swap(share_raw, "fsdp", square)
        own.append(share_raw)
        for k in range(square):
            block = share_raw if k == 0 else swap(share_raw, "fsdp", k)
            raw = lax.dynamic_update_slice_in_dim(raw, block, (place ^ k) * width + at, 0)
    own = jnp.concatenate(own, axis=0)

    inverse = inverse_factor(gram)
    left_raw = square_rows[:rows]
    left = dot(left_raw, inverse, ((1,), (1,)))
    norm_rows = lax.dynamic_slice_in_dim(own, (device // square) * (width // 2), width // 2, 0)
    norm_rows = dot(norm_rows, inverse, ((1,), (1,)))
    squares = jnp.sum(norm_rows * norm_rows, axis=0, keepdims=True)
    for axis in ("tensor", "fsdp"):
        flip = 1
        while flip < lax.axis_size(axis):
            squares = squares + swap(squares, axis, flip)
            flip *= 2
    column_norm = jnp.sqrt(squares + epsilon)
    scaled_left = left * (math.sqrt(total_rows / total_cols) / column_norm)
    planes = dot(jnp.concatenate([left, scaled_left], axis=0), inverse)

    both = dot(planes, raw, ((1,), (1,)))
    new_momentum = summed - 0.5 * both[:rows]
    update = both[rows:].astype(jnp.bfloat16)
    out_rows = cols // lax.axis_size("fsdp")
    right_rows = dot(
        lax.dynamic_slice_in_dim(raw, device * out_rows, out_rows, 0), inverse, ((1,), (1,))
    )
    return (update, new_momentum, left * math.sqrt(total_rows), right_rows / column_norm)


def on_device(momentum, gradient, right_basis):
    rows, cols = momentum.shape
    pairs = lax.axis_size("fsdp") == 2 * square and lax.axis_size("tensor") == 4
    aligned = rows % 16 == 0 and cols % (square * lanes) == 0 and right_basis.shape[1] % lanes == 0
    plan = in_squares if pairs and aligned else any_mesh
    return plan(momentum, gradient, right_basis)


def solution(mesh):
    in_specs = (P("fsdp", "tensor"), P("fsdp", "tensor"), P("tensor", None))
    out_specs = (
        P("fsdp", "tensor"),
        P("fsdp", "tensor"),
        P("fsdp", None),
        P(("tensor", "fsdp"), None),
    )
    return jax.shard_map(
        on_device, mesh=mesh, in_specs=in_specs, out_specs=out_specs, check_vma=False
    )
```

```python
import functools
import math

import jax
import jax.numpy as jnp
from jax import lax
from jax.experimental import pallas as pl
from jax.experimental.pallas import tpu as pltpu
from jax.sharding import PartitionSpec as P

epsilon = 1e-06
highest = lax.Precision.HIGHEST
lanes = 128
panel = 8
square = 4


def dot(a, b, contract=((1,), (0,))):
    return lax.dot_general(
        a, b, (contract, ((), ())), precision=highest, preferred_element_type=jnp.float32
    )


vmem = pl.BlockSpec(memory_space=pltpu.VMEM)
smem = pl.BlockSpec(memory_space=pltpu.SMEM)
anywhere = pl.BlockSpec(memory_space=pl.ANY)


def kernel(body, out_shape, in_specs, scratch, name):
    return pl.pallas_call(
        body,
        out_shape=out_shape,
        in_specs=in_specs,
        scratch_shapes=scratch,
        compiler_params=pltpu.CompilerParams(vmem_limit_bytes=32 * 2**20),
        cost_estimate=pl.CostEstimate(flops=0, bytes_accessed=0, transcendentals=0),
        name=name,
    )


def shape(*dims, dtype=jnp.float32):
    return jax.ShapeDtypeStruct(dims, dtype)


def factor_block(block):
    size = block.shape[0]
    lane = lax.broadcasted_iota(jnp.int32, (panel, size), 1)
    row = lax.broadcasted_iota(jnp.int32, (panel, size), 0)
    for first in range(0, size, panel):
        count = size - first
        now = block[first:, :]
        columns = [
            jnp.broadcast_to(now[:, first + k : first + k + 1], (count, size)) for k in range(panel)
        ]
        inside = (lane >= first) & (lane < first + panel)
        head = jnp.where(inside, jnp.where(lane - first == row, 1.0, 0.0), now[:panel])
        tail = None
        if count > panel:
            lane_below = lax.broadcasted_iota(jnp.int32, (count - panel, size), 1)
            inside_below = (lane_below >= first) & (lane_below < first + panel)
            tail = jnp.where(inside_below, 0.0, now[panel:])
        for j in range(panel):
            inverse = lax.rsqrt(columns[j][j : j + 1, :])
            multiplier = columns[j] * inverse
            for k in range(j + 1, panel):
                columns[k] = columns[k] - multiplier * (columns[k][j : j + 1, :] * inverse)
            pivot = head[j : j + 1, :] * inverse
            below = jnp.where(row > j, head - multiplier[:panel] * pivot, head)
            head = jnp.where(row == j, pivot, below)
            if tail is not None:
                tail = tail - multiplier[panel:] * pivot
        block[first : first + panel, :] = head
        if tail is not None:
            block[first + panel :, :] = tail


def place_gram(bits, shares, work):
    size = work.shape[0]
    count = size // lanes
    core, plane = bits[0], bits[1]
    stack = shares.pop()
    share = shares[0].shape[0]
    for flip_plane in range(2):
        for flip_core in range(2):
            at = pl.multiple_of(((plane ^ flip_plane) * 2 + (core ^ flip_core)) * share, 8)
            stack[pl.ds(at, share), :] = shares[flip_plane * 2 + flip_core][...]
    at = 0
    for j in range(count):
        for i in range(j, count):
            block = stack[at * lanes : (at + 1) * lanes, :]
            work[j * lanes : (j + 1) * lanes, i * lanes : (i + 1) * lanes] = block.T
            at += 1


def factor_step(b, work, out, block):
    size = work.shape[0]
    count = size // lanes
    row = lax.broadcasted_iota(jnp.int32, (lanes, lanes), 0)
    lower = row >= lax.broadcasted_iota(jnp.int32, (lanes, lanes), 1)
    rows = slice(b * lanes, (b + 1) * lanes)
    past = (b + 1) * lanes
    block[...] = work[rows, rows]
    factor_block(block)
    inverse = jnp.where(lower, block[...], 0.0)
    out[:, rows] = inverse
    if b:
        out[:, : b * lanes] = dot(inverse, work[rows, : b * lanes])
    if past < size:
        out[:, past:] = jnp.zeros((lanes, size - past), jnp.float32)
        upper = dot(inverse, work[rows, past:])
        own = out[:, :past]
        for i in range(b + 1, count):
            at = (i - b - 1) * lanes
            left = upper[:, at : at + lanes]
            below = slice(i * lanes, (i + 1) * lanes)
            work[below, i * lanes :] = work[below, i * lanes :] - dot(left, upper[:, at:], ((0,), (0,)))
            change = dot(left, own, ((0,), (0,)))
            if b:
                work[below, : b * lanes] = work[below, : b * lanes] - change[:, : b * lanes]
            work[below, b * lanes : past] = -change[:, b * lanes :]


def whole_kernel(gram, out, work, block):
    work[...] = gram[...]
    for b in range(work.shape[0] // lanes):
        factor_step(b, work, out.at[b * lanes : (b + 1) * lanes], block)


def inverse_factor(gram):
    size = gram.shape[0]
    return kernel(
        whole_kernel,
        jax.ShapeDtypeStruct((size, size), jnp.float32),
        [vmem],
        [pltpu.VMEM((size, size), jnp.float32), pltpu.VMEM((lanes, lanes), jnp.float32)],
        "inverse_factor",
    )(gram)


def first_kernel(bits, a, b, c, d, token, out, work, stack, block):
    place_gram(bits, [a, b, c, d, stack], work)
    factor_step(0, work, out, block)


def first_step(bits, shares, size, token):
    blocks = sum(x.shape[0] for x in shares)
    return kernel(
        first_kernel,
        [
            jax.ShapeDtypeStruct((lanes, size), jnp.float32),
            jax.ShapeDtypeStruct((size, size), jnp.float32),
        ],
        [smem] + [vmem] * 4 + [anywhere],
        [pltpu.VMEM((blocks, lanes), jnp.float32), pltpu.VMEM((lanes, lanes), jnp.float32)],
        "factor_first",
    )(bits, *shares, token)


def later_kernel(b, before, token, out, work, block):
    work[...] = before[...]
    factor_step(b, work, out, block)


def later_step(b, work, token):
    size = work.shape[0]
    return kernel(
        functools.partial(later_kernel, b),
        [
            jax.ShapeDtypeStruct((lanes, size), jnp.float32),
            jax.ShapeDtypeStruct((size, size), jnp.float32),
        ],
        [vmem, anywhere],
        [pltpu.VMEM((lanes, lanes), jnp.float32)],
        "factor_later",
    )(work, token)


def share_norms(right_rows):
    squares = lax.psum(jnp.sum(right_rows * right_rows, axis=0), ("fsdp", "tensor"))
    return jnp.sqrt(squares + epsilon)


def any_mesh(momentum, gradient, right_basis):
    summed = momentum + gradient.astype(jnp.float32)
    left_raw = lax.psum(dot(summed, right_basis), "tensor")
    gram = lax.psum(dot(left_raw, left_raw, ((0,), (0,))), "fsdp")
    inverse = inverse_factor(gram)
    left = dot(left_raw, inverse, ((1,), (1,)))
    total_rows = left.shape[0] * lax.axis_size("fsdp")
    total_cols = summed.shape[1] * lax.axis_size("tensor")
    raw_rows = lax.psum_scatter(
        dot(summed, left_raw, ((0,), (0,))), "fsdp", scatter_dimension=0, tiled=True
    )
    right_rows = dot(raw_rows, inverse, ((1,), (1,)))
    column_norm = share_norms(right_rows)
    scaled_left = left * (math.sqrt(total_rows / total_cols) / column_norm)[None, :]
    raw = lax.all_gather(raw_rows, "fsdp", axis=0, tiled=True)
    product = dot(dot(left, inverse), raw, ((1,), (1,)))
    update = dot(dot(scaled_left, inverse), raw, ((1,), (1,))).astype(jnp.bfloat16)
    new_momentum = summed - 0.5 * product
    return (update, new_momentum, left * math.sqrt(total_rows), right_rows / column_norm[None, :])


def swap(value, axis, flip):
    return lax.ppermute(value, axis, [(i, i ^ flip) for i in range(lax.axis_size(axis))])


def split_kernel(bits, momentum, gradient, *pieces):
    width = pieces[0].shape[1]
    for k, piece in enumerate(pieces):
        at = pl.ds(pl.multiple_of((bits[2] ^ k) * width, lanes), width)
        piece[...] = momentum[:, at] + gradient[:, at].astype(jnp.float32)


def part_left_kernel(bits, basis, *refs):
    pieces, (sent, kept, total) = refs[:square], refs[square:]
    width = pieces[0].shape[1]
    half = sent.shape[0]
    for k, piece in enumerate(pieces):
        rows = pl.ds(pl.multiple_of((bits[2] ^ k) * width, lanes), width)
        part = dot(piece[...], basis[rows, :])
        total[...] = part if k == 0 else total[...] + part
    sent[...] = total[pl.ds(pl.multiple_of((1 - bits[0]) * half, 8), half), :]
    kept[...] = total[pl.ds(pl.multiple_of(bits[0] * half, 8), half), :]


def gram_kernel(bits, *refs):
    rows, (in_square, sent, kept, stack) = refs[:square], refs[square:]
    half, rank = rows[0].shape
    share = sent.shape[0]
    for k, part in enumerate(rows):
        in_square[k * half : (k + 1) * half, :] = part[...]
    at = 0
    for first in range(0, rank, lanes):
        left, right = in_square[:, first:], in_square[:, first : first + lanes]
        stack[at : at + rank - first, :] = dot(left, right, ((0,), (0,)))
        at += rank - first
    sent[...] = stack[pl.ds(pl.multiple_of((2 * bits[1] + 1 - bits[0]) * share, 8), share), :]
    kept[...] = stack[pl.ds(pl.multiple_of((2 * bits[1] + bits[0]) * share, 8), share), :]


def raw_kernel(bits, in_square, other, *refs):
    columns, pieces, (left, right) = refs[:square], refs[square:-2], refs[-2:]
    rows = columns[0].shape[0]
    half = rows // 2
    for k in range(square):
        own = slice(k * half, (k + 1) * half)
        left[k * rows : (k + 1) * rows, :] = columns[k][...]
        right[pl.ds(pl.multiple_of(k * rows + bits[0] * half, 8), half), :] = in_square[own, :]
        right[pl.ds(pl.multiple_of(k * rows + (1 - bits[0]) * half, 8), half), :] = other[own, :]
    step = pieces[0].shape[0]
    raw = dot(left[...], right[...], ((0,), (0,)))
    for at, piece in enumerate(pieces):
        piece[...] = raw[at * step : (at + 1) * step]


def left_kernel(bits, in_square, other, *refs):
    count = refs[-2].shape[0] // lanes
    inverses, refs = refs[:count], refs[count:]
    own, (left, squares, inverse, rows) = refs[:-4], refs[-4:]
    half = left.shape[0] // 2
    for b, part in enumerate(inverses):
        inverse[b * lanes : (b + 1) * lanes, :] = part[...]
    rows[pl.ds(pl.multiple_of(bits[0] * half, 8), half), :] = in_square[:half, :]
    rows[pl.ds(pl.multiple_of((1 - bits[0]) * half, 8), half), :] = other[:half, :]
    total = None
    for part in own:
        right = dot(part[...], inverse[...], ((1,), (1,)))
        part_total = jnp.sum(right * right, axis=0, keepdims=True)
        total = part_total if total is None else total + part_total
    squares[...] = total
    left[...] = dot(rows[...], inverse[...], ((1,), (1,)))


def plane_kernel(scale, left, inverse, left_scaled, plane):
    left_scaled[...] = left[...] * scale
    plane[...] = dot(left[...], inverse[...])


def last_kernel(factor, steps, bits, squares, left, inverse, plane, *refs):
    pieces, refs = refs[:square], refs[square:]
    raws, (new_momentum, update, next_basis, raw, planes) = refs[: square * steps], refs[square * steps :]
    rows, width = pieces[0].shape
    step = raws[0].shape[0]
    column_norm = jnp.sqrt(squares[...] + epsilon)
    planes[:rows, :] = plane[...]
    planes[rows:, :] = dot(left[...] * (factor / column_norm), inverse[...])
    for k in range(square):
        first = (bits[2] ^ k) * width
        new_momentum[:, pl.ds(pl.multiple_of(first, lanes), width)] = pieces[k][...]
        for i in range(steps):
            raw[pl.ds(pl.multiple_of(first + i * step, lanes), step), :] = raws[i * square + k][...]
    cols, chunk = raw.shape[0], raw.shape[1]
    for first in range(0, cols, chunk):
        at = slice(first, min(first + chunk, cols))
        both = dot(planes[...], raw[at, :], ((1,), (1,)))
        new_momentum[:, at] = new_momentum[:, at] - 0.5 * both[:rows]
        update[:, at] = both[rows:].astype(jnp.bfloat16)
    count = next_basis.shape[0]
    own = raw[pl.ds(pl.multiple_of(bits[3] * count, 8), count), :]
    next_basis[...] = dot(own, inverse[...], ((1,), (1,))) / column_norm


def in_squares(momentum, gradient, right_basis):
    device = lax.axis_index("fsdp")
    tensor = lax.axis_index("tensor")
    bits = jnp.stack([tensor % 2, tensor // 2, device % square, device]).astype(jnp.int32)
    rows, cols = momentum.shape
    rank = right_basis.shape[1]
    half, width = rows // 2, cols // square
    total_rows = rows * lax.axis_size("fsdp")
    total_cols = cols * lax.axis_size("tensor")

    pieces = kernel(split_kernel, [shape(rows, width)] * square, [smem, vmem, vmem], [], "split_sum")(
        bits, momentum, gradient
    )
    columns = [pieces[0]] + [swap(pieces[k], "fsdp", k) for k in range(1, square)]

    sent, kept = kernel(
        part_left_kernel,
        [shape(half, rank)] * 2,
        [smem] + [vmem] * (1 + square),
        [pltpu.VMEM((rows, rank), jnp.float32)],
        "part_left",
    )(bits, right_basis, *pieces)
    mine = kept + swap(sent, "tensor", 1)
    mine = mine + swap(mine, "tensor", 2)
    gathered = [mine] + [swap(mine, "fsdp", k) for k in range(1, square)]

    count = rank // lanes
    stacked = count * (count + 1) // 2 * lanes
    share = stacked // 4
    in_square, sent, kept = kernel(
        gram_kernel,
        [shape(square * half, rank), shape(share, lanes), shape(share, lanes)],
        [smem] + [vmem] * square,
        [pltpu.VMEM((stacked, lanes), jnp.float32)],
        "part_gram",
    )(bits, *gathered)
    other = swap(in_square, "tensor", 1)
    quarter = kept + swap(sent, "tensor", 1)
    quarter = quarter + swap(quarter, "fsdp", square)
    over_planes = swap(quarter, "tensor", 2)
    shares = [quarter, swap(quarter, "tensor", 1), over_planes, swap(over_planes, "tensor", 1)]

    steps = width // lanes
    parts = kernel(
        raw_kernel,
        [shape(lanes, rank)] * steps,
        [smem] + [vmem] * (2 + square),
        [
            pltpu.VMEM((square * rows, width), jnp.float32),
            pltpu.VMEM((square * rows, rank), jnp.float32),
        ],
        "part_raw",
    )(bits, in_square, other, *columns)
    own, raws = [], []
    for part in parts:
        part = part + swap(part, "fsdp", square)
        own.append(part)
        raws += [part] + [swap(part, "fsdp", k) for k in range(1, square)]

    factors = []
    out, work = first_step(bits, shares, rank, parts[0])
    factors.append(out)
    for b in range(1, count):
        out, work = later_step(b, work, own[min(b // 2, len(own) - 1)])
        factors.append(out)

    left, squares, inverse = kernel(
        left_kernel,
        [shape(rows, rank), shape(1, rank), shape(rank, rank)],
        [smem] + [vmem] * (2 + count + steps),
        [pltpu.VMEM((rows, rank), jnp.float32)],
        "left",
    )(bits, in_square, other, *factors, *own)
    for axis, last in (("tensor", lax.axis_size("tensor")), ("fsdp", square)):
        flip = 1
        while flip < last:
            squares = squares + swap(squares, axis, flip)
            flip *= 2
    left_scaled, plane = kernel(
        functools.partial(plane_kernel, math.sqrt(total_rows)),
        [shape(rows, rank)] * 2,
        [vmem] * 2,
        [],
        "plane",
    )(left, inverse)

    new_momentum, update, next_basis = kernel(
        functools.partial(last_kernel, math.sqrt(total_rows / total_cols), steps),
        [
            shape(rows, cols),
            shape(rows, cols, dtype=jnp.bfloat16),
            shape(cols // lax.axis_size("fsdp"), rank),
        ],
        [smem] + [vmem] * (4 + square + square * steps),
        [pltpu.VMEM((cols, rank), jnp.float32), pltpu.VMEM((2 * rows, rank), jnp.float32)],
        "last",
    )(bits, squares, left, inverse, plane, *pieces, *raws)
    return (update, new_momentum, left_scaled, next_basis)


def on_device(momentum, gradient, right_basis):
    rows, cols = momentum.shape
    pairs = lax.axis_size("fsdp") == 2 * square and lax.axis_size("tensor") == 4
    aligned = rows % 16 == 0 and cols % (square * lanes) == 0 and right_basis.shape[1] % lanes == 0
    plan = in_squares if pairs and aligned else any_mesh
    return plan(momentum, gradient, right_basis)


def solution(mesh):
    in_specs = (P("fsdp", "tensor"), P("fsdp", "tensor"), P("tensor", None))
    out_specs = (
        P("fsdp", "tensor"),
        P("fsdp", "tensor"),
        P("fsdp", None),
        P(("tensor", "fsdp"), None),
    )
    return jax.shard_map(
        on_device, mesh=mesh, in_specs=in_specs, out_specs=out_specs, check_vma=False
    )
```

```python
import functools
import math

import jax
import jax.numpy as jnp
from jax import lax
from jax.experimental import pallas as pl
from jax.experimental.pallas import tpu as pltpu
from jax.sharding import PartitionSpec as P

epsilon = 1e-06
highest = lax.Precision.HIGHEST
lanes = 128
panel = 8
square = 4


def dot(a, b, contract=((1,), (0,))):
    return lax.dot_general(
        a, b, (contract, ((), ())), precision=highest, preferred_element_type=jnp.float32
    )


vmem = pl.BlockSpec(memory_space=pltpu.VMEM)
smem = pl.BlockSpec(memory_space=pltpu.SMEM)
anywhere = pl.BlockSpec(memory_space=pl.ANY)


def kernel(body, out_shape, in_specs, scratch, name):
    return pl.pallas_call(
        body,
        out_shape=out_shape,
        in_specs=in_specs,
        scratch_shapes=scratch,
        compiler_params=pltpu.CompilerParams(vmem_limit_bytes=32 * 2**20),
        cost_estimate=pl.CostEstimate(flops=0, bytes_accessed=0, transcendentals=0),
        name=name,
    )


def shape(*dims, dtype=jnp.float32):
    return jax.ShapeDtypeStruct(dims, dtype)


def factor_block(block):
    size = block.shape[0]
    lane = lax.broadcasted_iota(jnp.int32, (panel, size), 1)
    row = lax.broadcasted_iota(jnp.int32, (panel, size), 0)
    for first in range(0, size, panel):
        count = size - first
        now = block[first:, :]
        columns = [
            jnp.broadcast_to(now[:, first + k : first + k + 1], (count, size)) for k in range(panel)
        ]
        inside = (lane >= first) & (lane < first + panel)
        head = jnp.where(inside, jnp.where(lane - first == row, 1.0, 0.0), now[:panel])
        tail = None
        if count > panel:
            lane_below = lax.broadcasted_iota(jnp.int32, (count - panel, size), 1)
            inside_below = (lane_below >= first) & (lane_below < first + panel)
            tail = jnp.where(inside_below, 0.0, now[panel:])
        for j in range(panel):
            inverse = lax.rsqrt(columns[j][j : j + 1, :])
            multiplier = columns[j] * inverse
            for k in range(j + 1, panel):
                columns[k] = columns[k] - multiplier * (columns[k][j : j + 1, :] * inverse)
            pivot = head[j : j + 1, :] * inverse
            below = jnp.where(row > j, head - multiplier[:panel] * pivot, head)
            head = jnp.where(row == j, pivot, below)
            if tail is not None:
                tail = tail - multiplier[panel:] * pivot
        block[first : first + panel, :] = head
        if tail is not None:
            block[first + panel :, :] = tail


def place_gram(bits, shares, work):
    size = work.shape[0]
    count = size // lanes
    core, plane = bits[0], bits[1]
    stack = shares.pop()
    share = shares[0].shape[0]
    for flip_plane in range(2):
        for flip_core in range(2):
            at = pl.multiple_of(((plane ^ flip_plane) * 2 + (core ^ flip_core)) * share, 8)
            stack[pl.ds(at, share), :] = shares[flip_plane * 2 + flip_core][...]
    at = 0
    for j in range(count):
        for i in range(j, count):
            block = stack[at * lanes : (at + 1) * lanes, :]
            work[j * lanes : (j + 1) * lanes, i * lanes : (i + 1) * lanes] = block.T
            at += 1


def factor_step(b, work, out, block):
    size = work.shape[0]
    count = size // lanes
    row = lax.broadcasted_iota(jnp.int32, (lanes, lanes), 0)
    lower = row >= lax.broadcasted_iota(jnp.int32, (lanes, lanes), 1)
    rows = slice(b * lanes, (b + 1) * lanes)
    past = (b + 1) * lanes
    block[...] = work[rows, rows]
    factor_block(block)
    inverse = jnp.where(lower, block[...], 0.0)
    out[:, rows] = inverse
    if b:
        out[:, : b * lanes] = dot(inverse, work[rows, : b * lanes])
    if past < size:
        out[:, past:] = jnp.zeros((lanes, size - past), jnp.float32)
        upper = dot(inverse, work[rows, past:])
        own = out[:, :past]
        for i in range(b + 1, count):
            at = (i - b - 1) * lanes
            left = upper[:, at : at + lanes]
            below = slice(i * lanes, (i + 1) * lanes)
            work[below, i * lanes :] = work[below, i * lanes :] - dot(left, upper[:, at:], ((0,), (0,)))
            change = dot(left, own, ((0,), (0,)))
            if b:
                work[below, : b * lanes] = work[below, : b * lanes] - change[:, : b * lanes]
            work[below, b * lanes : past] = -change[:, b * lanes :]


def whole_kernel(gram, out, work, block):
    work[...] = gram[...]
    for b in range(work.shape[0] // lanes):
        factor_step(b, work, out.at[b * lanes : (b + 1) * lanes], block)


def inverse_factor(gram):
    size = gram.shape[0]
    return kernel(
        whole_kernel,
        jax.ShapeDtypeStruct((size, size), jnp.float32),
        [vmem],
        [pltpu.VMEM((size, size), jnp.float32), pltpu.VMEM((lanes, lanes), jnp.float32)],
        "inverse_factor",
    )(gram)


def first_kernel(bits, a, b, c, d, out, work, stack, block):
    place_gram(bits, [a, b, c, d, stack], work)
    factor_step(0, work, out, block)


def first_step(bits, shares, size):
    blocks = sum(x.shape[0] for x in shares)
    return kernel(
        first_kernel,
        [shape(lanes, size), shape(size, size)],
        [smem] + [vmem] * 4,
        [pltpu.VMEM((blocks, lanes), jnp.float32), pltpu.VMEM((lanes, lanes), jnp.float32)],
        "factor_first",
    )(bits, *shares)


def later_kernel(b, before, out, work, block):
    work[...] = before[...]
    factor_step(b, work, out, block)


def later_step(b, work):
    size = work.shape[0]
    return kernel(
        functools.partial(later_kernel, b),
        [shape(lanes, size), shape(size, size)],
        [vmem],
        [pltpu.VMEM((lanes, lanes), jnp.float32)],
        "factor_later",
    )(work)


def share_norms(right_rows):
    squares = lax.psum(jnp.sum(right_rows * right_rows, axis=0), ("fsdp", "tensor"))
    return jnp.sqrt(squares + epsilon)


def any_mesh(momentum, gradient, right_basis):
    summed = momentum + gradient.astype(jnp.float32)
    left_raw = lax.psum(dot(summed, right_basis), "tensor")
    gram = lax.psum(dot(left_raw, left_raw, ((0,), (0,))), "fsdp")
    inverse = inverse_factor(gram)
    left = dot(left_raw, inverse, ((1,), (1,)))
    total_rows = left.shape[0] * lax.axis_size("fsdp")
    total_cols = summed.shape[1] * lax.axis_size("tensor")
    raw_rows = lax.psum_scatter(
        dot(summed, left_raw, ((0,), (0,))), "fsdp", scatter_dimension=0, tiled=True
    )
    right_rows = dot(raw_rows, inverse, ((1,), (1,)))
    column_norm = share_norms(right_rows)
    scaled_left = left * (math.sqrt(total_rows / total_cols) / column_norm)[None, :]
    raw = lax.all_gather(raw_rows, "fsdp", axis=0, tiled=True)
    product = dot(dot(left, inverse), raw, ((1,), (1,)))
    update = dot(dot(scaled_left, inverse), raw, ((1,), (1,))).astype(jnp.bfloat16)
    new_momentum = summed - 0.5 * product
    return (update, new_momentum, left * math.sqrt(total_rows), right_rows / column_norm[None, :])


def swap(value, axis, flip):
    return lax.ppermute(value, axis, [(i, i ^ flip) for i in range(lax.axis_size(axis))])


def split_kernel(bits, momentum, gradient, *pieces):
    width = pieces[0].shape[1]
    for k, piece in enumerate(pieces):
        at = pl.ds(pl.multiple_of((bits[2] ^ k) * width, lanes), width)
        piece[...] = momentum[:, at] + gradient[:, at].astype(jnp.float32)


def part_left_kernel(bits, basis, *refs):
    pieces, (sent, kept, total) = refs[:square], refs[square:]
    width = pieces[0].shape[1]
    half = sent.shape[0]
    for k, piece in enumerate(pieces):
        rows = pl.ds(pl.multiple_of((bits[2] ^ k) * width, lanes), width)
        part = dot(piece[...], basis[rows, :])
        total[...] = part if k == 0 else total[...] + part
    sent[...] = total[pl.ds(pl.multiple_of((1 - bits[0]) * half, 8), half), :]
    kept[...] = total[pl.ds(pl.multiple_of(bits[0] * half, 8), half), :]


def add_kernel(*refs):
    refs[-1][...] = refs[0][...] + refs[1][...]


def add_after(a, b, *tokens):
    return kernel(
        add_kernel, shape(*a.shape), [vmem] * 2 + [anywhere] * len(tokens), [], "add_after"
    )(a, b, *tokens)


def gram_kernel(bits, *refs):
    parts, (sent, kept, rows, stack) = refs[:square], refs[square:]
    half, rank = parts[0].shape
    share = sent.shape[0]
    for k, part in enumerate(parts):
        rows[k * half : (k + 1) * half, :] = part[...]
    at = 0
    for first in range(0, rank, lanes):
        left, right = rows[:, first:], rows[:, first : first + lanes]
        stack[at : at + rank - first, :] = dot(left, right, ((0,), (0,)))
        at += rank - first
    for out, core in ((kept, bits[0]), (sent, 1 - bits[0])):
        index = (2 * bits[1] + core) * square + bits[2]
        out[...] = stack[pl.ds(pl.multiple_of(index * share, 8), share), :]


def order_kernel(bits, *refs):
    out = refs[-1]
    share = refs[0].shape[0]
    for k in range(square):
        out[pl.ds(pl.multiple_of((bits[2] ^ k) * share, 8), share), :] = refs[k][...]


def raw_kernel(bits, *refs):
    mine, others, columns = refs[:square], refs[square : 2 * square], refs[2 * square : 3 * square]
    sent, kept, left, right, raw = refs[3 * square :]
    rows = columns[0].shape[0]
    half = rows // 2
    for k in range(square):
        left[k * rows : (k + 1) * rows, :] = columns[k][...]
        right[pl.ds(pl.multiple_of(k * rows + bits[0] * half, 8), half), :] = mine[k][...]
        right[pl.ds(pl.multiple_of(k * rows + (1 - bits[0]) * half, 8), half), :] = others[k][...]
    raw[...] = dot(left[...], right[...], ((0,), (0,)))
    count = kept.shape[0]
    kept[...] = raw[pl.ds(pl.multiple_of(bits[4] * count, 8), count), :]
    sent[...] = raw[pl.ds(pl.multiple_of((1 - bits[4]) * count, 8), count), :]


def left_kernel(scale, bits, mine, other, *refs):
    inverses, (left, left_scaled, inverse, rows) = refs[:-4], refs[-4:]
    half = mine.shape[0]
    for b, part in enumerate(inverses):
        inverse[b * lanes : (b + 1) * lanes, :] = part[...]
    rows[pl.ds(pl.multiple_of(bits[0] * half, 8), half), :] = mine[...]
    rows[pl.ds(pl.multiple_of((1 - bits[0]) * half, 8), half), :] = other[...]
    left[...] = dot(rows[...], inverse[...], ((1,), (1,)))
    left_scaled[...] = left[...] * scale


def norm_kernel(own, received, inverse, *refs):
    out = refs[-1]
    count = own.shape[0]
    total = jnp.zeros((1, own.shape[1]), jnp.float32)
    for part in (own, received):
        right = dot(part[...], inverse[...], ((1,), (1,)))
        total = total + jnp.sum(right * right, axis=0, keepdims=True)
    out[:count, :] = received[...]
    row = lax.broadcasted_iota(jnp.int32, (8, own.shape[1]), 0)
    out[count:, :] = jnp.where(row == 0, total, 0.0)


def momentum_kernel(bits, left, inverse, *refs):
    pieces, own, received = refs[:square], refs[square : 2 * square], refs[2 * square : 3 * square]
    new_momentum, raw, plane = refs[3 * square :]
    rows, width = pieces[0].shape
    half = own[0].shape[0]
    plane[...] = dot(left[...], inverse[...])
    for k in range(square):
        first = (bits[2] ^ k) * width
        new_momentum[:, pl.ds(pl.multiple_of(first, lanes), width)] = pieces[k][...]
        at = pl.multiple_of(first + bits[4] * half, 8)
        raw[pl.ds(at, half), :] = own[k][...]
        at = pl.multiple_of(first + (1 - bits[4]) * half, 8)
        raw[pl.ds(at, half), :] = received[k][:half, :]
    cols, chunk = raw.shape
    for first in range(0, cols, chunk):
        at = slice(first, min(first + chunk, cols))
        new_momentum[:, at] = new_momentum[:, at] - 0.5 * dot(plane[...], raw[at, :], ((1,), (1,)))


def update_kernel(factor, bits, squares, left, inverse, raw, update, next_basis, plane):
    column_norm = jnp.sqrt(squares[...] + epsilon)
    plane[...] = dot(left[...] * (factor / column_norm), inverse[...])
    cols, chunk = raw.shape
    for first in range(0, cols, chunk):
        at = slice(first, min(first + chunk, cols))
        update[:, at] = dot(plane[...], raw[at, :], ((1,), (1,))).astype(jnp.bfloat16)
    count = next_basis.shape[0]
    own = raw[pl.ds(pl.multiple_of(bits[3] * count, 8), count), :]
    next_basis[...] = dot(own, inverse[...], ((1,), (1,))) / column_norm


def in_squares(momentum, gradient, right_basis):
    device = lax.axis_index("fsdp")
    tensor = lax.axis_index("tensor")
    bits = jnp.stack([tensor % 2, tensor // 2, device % square, device, device // square])
    bits = bits.astype(jnp.int32)
    rows, cols = momentum.shape
    rank = right_basis.shape[1]
    half, width = rows // 2, cols // square
    total_rows = rows * lax.axis_size("fsdp")
    total_cols = cols * lax.axis_size("tensor")

    pieces = kernel(split_kernel, [shape(rows, width)] * square, [smem, vmem, vmem], [], "split_sum")(
        bits, momentum, gradient
    )
    columns = [pieces[0]] + [swap(pieces[k], "fsdp", k) for k in range(1, square)]

    sent, kept = kernel(
        part_left_kernel,
        [shape(half, rank)] * 2,
        [smem] + [vmem] * (1 + square),
        [pltpu.VMEM((rows, rank), jnp.float32)],
        "part_left",
    )(bits, right_basis, *pieces)
    mine = kept + swap(sent, "tensor", 1)
    mine = add_after(mine, swap(mine, "tensor", 2), *columns[1:])
    gathered = [mine] + [swap(mine, "fsdp", k) for k in range(1, square)]
    others = [swap(part, "tensor", 1) for part in gathered]

    sent, kept = kernel(
        raw_kernel,
        [shape(width // 2, rank)] * 2,
        [smem] + [vmem] * (3 * square),
        [
            pltpu.VMEM((square * rows, width), jnp.float32),
            pltpu.VMEM((square * rows, rank), jnp.float32),
            pltpu.VMEM((width, rank), jnp.float32),
        ],
        "part_raw",
    )(bits, *gathered, *others, *columns)
    own = kept + swap(sent, "fsdp", square)

    count = rank // lanes
    stacked = count * (count + 1) // 2 * lanes
    share = stacked // (4 * square)
    sent, kept = kernel(
        gram_kernel,
        [shape(share, lanes)] * 2,
        [smem] + [vmem] * square,
        [pltpu.VMEM((square * half, rank), jnp.float32), pltpu.VMEM((stacked, lanes), jnp.float32)],
        "part_gram",
    )(bits, *gathered)
    part = kept + swap(sent, "tensor", 1)
    part = part + swap(part, "fsdp", square)
    quarter = kernel(
        order_kernel, shape(square * share, lanes), [smem] + [vmem] * square, [], "order"
    )(bits, part, *[swap(part, "fsdp", k) for k in range(1, square)])
    over_planes = swap(quarter, "tensor", 2)
    shares = [quarter, swap(quarter, "tensor", 1), over_planes, swap(over_planes, "tensor", 1)]

    factors = []
    out, work = first_step(bits, shares, rank)
    factors.append(out)
    for b in range(1, count):
        out, work = later_step(b, work)
        factors.append(out)
    left, left_scaled, inverse = kernel(
        functools.partial(left_kernel, math.sqrt(total_rows)),
        [shape(rows, rank), shape(rows, rank), shape(rank, rank)],
        [smem] + [vmem] * (2 + count),
        [pltpu.VMEM((rows, rank), jnp.float32)],
        "left",
    )(bits, mine, others[0], *factors)

    received = swap(own, "fsdp", square)
    own_rows = [own] + [swap(own, "fsdp", k) for k in range(1, square)]
    with_norms = kernel(
        norm_kernel,
        shape(width // 2 + 8, rank),
        [vmem] * 3 + [anywhere] * (square - 1),
        [],
        "norms",
    )(own, received, inverse, *own_rows[1:])
    received_rows = [with_norms] + [swap(with_norms, "fsdp", k) for k in range(1, square)]
    squares = sum(part[width // 2 : width // 2 + 1] for part in received_rows)
    squares = squares + swap(squares, "tensor", 1)
    squares = squares + swap(squares, "tensor", 2)

    new_momentum, raw = kernel(
        momentum_kernel,
        [shape(rows, cols), shape(cols, rank)],
        [smem] + [vmem] * (2 + 3 * square),
        [pltpu.VMEM((rows, rank), jnp.float32)],
        "new_momentum",
    )(bits, left, inverse, *pieces, *own_rows, *received_rows)
    update, next_basis = kernel(
        functools.partial(update_kernel, math.sqrt(total_rows / total_cols)),
        [shape(rows, cols, dtype=jnp.bfloat16), shape(cols // lax.axis_size("fsdp"), rank)],
        [smem] + [vmem] * 4,
        [pltpu.VMEM((rows, rank), jnp.float32)],
        "update",
    )(bits, squares, left, inverse, raw)
    return (update, new_momentum, left_scaled, next_basis)


def on_device(momentum, gradient, right_basis):
    rows, cols = momentum.shape
    pairs = lax.axis_size("fsdp") == 2 * square and lax.axis_size("tensor") == 4
    aligned = rows % 16 == 0 and cols % (square * lanes) == 0 and right_basis.shape[1] % lanes == 0
    plan = in_squares if pairs and aligned else any_mesh
    return plan(momentum, gradient, right_basis)


def solution(mesh):
    in_specs = (P("fsdp", "tensor"), P("fsdp", "tensor"), P("tensor", None))
    out_specs = (
        P("fsdp", "tensor"),
        P("fsdp", "tensor"),
        P("fsdp", None),
        P(("tensor", "fsdp"), None),
    )
    return jax.shard_map(
        on_device, mesh=mesh, in_specs=in_specs, out_specs=out_specs, check_vma=False
    )
```

```python
import functools
import math

import jax
import jax.numpy as jnp
from jax import lax
from jax.experimental import pallas as pl
from jax.experimental.pallas import tpu as pltpu
from jax.sharding import PartitionSpec as P

epsilon = 1e-06
highest = lax.Precision.HIGHEST
lanes = 128
panel = 8
square = 4


def dot(a, b, contract=((1,), (0,))):
    return lax.dot_general(
        a, b, (contract, ((), ())), precision=highest, preferred_element_type=jnp.float32
    )


vmem = pl.BlockSpec(memory_space=pltpu.VMEM)
smem = pl.BlockSpec(memory_space=pltpu.SMEM)
anywhere = pl.BlockSpec(memory_space=pl.ANY)


def kernel(body, out_shape, in_specs, scratch, name, cost=0):
    return pl.pallas_call(
        body,
        out_shape=out_shape,
        in_specs=in_specs,
        scratch_shapes=scratch,
        compiler_params=pltpu.CompilerParams(vmem_limit_bytes=32 * 2**20),
        cost_estimate=pl.CostEstimate(flops=0, bytes_accessed=cost, transcendentals=0),
        name=name,
    )


def shape(*dims, dtype=jnp.float32):
    return jax.ShapeDtypeStruct(dims, dtype)


def split(value):
    high = value.astype(jnp.bfloat16)
    return high, (value - high.astype(jnp.float32)).astype(jnp.bfloat16)


def dot_three(a, b):
    a_high, a_low = split(a)
    b_high, b_low = split(b)
    return lax.dot_general(
        jnp.concatenate([a_high, a_high, a_low], axis=1),
        jnp.concatenate([b_high, b_low, b_high], axis=1),
        (((1,), (1,)), ((), ())),
        preferred_element_type=jnp.float32,
    )


def factor_block(block):
    size = block.shape[0]
    lane = lax.broadcasted_iota(jnp.int32, (panel, size), 1)
    row = lax.broadcasted_iota(jnp.int32, (panel, size), 0)
    for first in range(0, size, panel):
        count = size - first
        now = block[first:, :]
        columns = [
            jnp.broadcast_to(now[:, first + k : first + k + 1], (count, size)) for k in range(panel)
        ]
        inside = (lane >= first) & (lane < first + panel)
        head = jnp.where(inside, jnp.where(lane - first == row, 1.0, 0.0), now[:panel])
        tail = None
        if count > panel:
            lane_below = lax.broadcasted_iota(jnp.int32, (count - panel, size), 1)
            inside_below = (lane_below >= first) & (lane_below < first + panel)
            tail = jnp.where(inside_below, 0.0, now[panel:])
        for j in range(panel):
            inverse = lax.rsqrt(columns[j][j : j + 1, :])
            multiplier = columns[j] * inverse
            for k in range(j + 1, panel):
                columns[k] = columns[k] - multiplier * (columns[k][j : j + 1, :] * inverse)
            pivot = head[j : j + 1, :] * inverse
            below = jnp.where(row > j, head - multiplier[:panel] * pivot, head)
            head = jnp.where(row == j, pivot, below)
            if tail is not None:
                tail = tail - multiplier[panel:] * pivot
        block[first : first + panel, :] = head
        if tail is not None:
            block[first + panel :, :] = tail


def place_gram(bits, shares, work):
    size = work.shape[0]
    count = size // lanes
    core, plane = bits[0], bits[1]
    stack = shares.pop()
    share = shares[0].shape[0]
    for flip_plane in range(2):
        for flip_core in range(2):
            at = pl.multiple_of(((plane ^ flip_plane) * 2 + (core ^ flip_core)) * share, 8)
            stack[pl.ds(at, share), :] = shares[flip_plane * 2 + flip_core][...]
    at = 0
    for j in range(count):
        for i in range(j, count):
            block = stack[at * lanes : (at + 1) * lanes, :]
            work[j * lanes : (j + 1) * lanes, i * lanes : (i + 1) * lanes] = block.T
            at += 1


def factor_step(b, work, out, block):
    size = work.shape[0]
    count = size // lanes
    row = lax.broadcasted_iota(jnp.int32, (lanes, lanes), 0)
    lower = row >= lax.broadcasted_iota(jnp.int32, (lanes, lanes), 1)
    rows = slice(b * lanes, (b + 1) * lanes)
    past = (b + 1) * lanes
    block[...] = work[rows, rows]
    factor_block(block)
    inverse = jnp.where(lower, block[...], 0.0)
    out[:, rows] = inverse
    if b:
        out[:, : b * lanes] = dot(inverse, work[rows, : b * lanes])
    if past < size:
        out[:, past:] = jnp.zeros((lanes, size - past), jnp.float32)
        upper = dot(inverse, work[rows, past:])
        own = out[:, :past]
        for i in range(b + 1, count):
            at = (i - b - 1) * lanes
            left = upper[:, at : at + lanes]
            below = slice(i * lanes, (i + 1) * lanes)
            work[below, i * lanes :] = work[below, i * lanes :] - dot(left, upper[:, at:], ((0,), (0,)))
            change = dot(left, own, ((0,), (0,)))
            if b:
                work[below, : b * lanes] = work[below, : b * lanes] - change[:, : b * lanes]
            work[below, b * lanes : past] = -change[:, b * lanes :]


def whole_kernel(gram, out, work, block):
    work[...] = gram[...]
    for b in range(work.shape[0] // lanes):
        factor_step(b, work, out.at[b * lanes : (b + 1) * lanes], block)


def inverse_factor(gram):
    size = gram.shape[0]
    return kernel(
        whole_kernel,
        jax.ShapeDtypeStruct((size, size), jnp.float32),
        [vmem],
        [pltpu.VMEM((size, size), jnp.float32), pltpu.VMEM((lanes, lanes), jnp.float32)],
        "inverse_factor",
    )(gram)


def first_kernel(bits, a, b, c, d, out, work, stack, block):
    place_gram(bits, [a, b, c, d, stack], work)
    factor_step(0, work, out, block)


def first_step(bits, shares, size):
    blocks = sum(x.shape[0] for x in shares)
    return kernel(
        first_kernel,
        [shape(lanes, size), shape(size, size)],
        [smem] + [vmem] * 4,
        [pltpu.VMEM((blocks, lanes), jnp.float32), pltpu.VMEM((lanes, lanes), jnp.float32)],
        "factor_first",
    )(bits, *shares)


def later_kernel(b, before, token, out, work, block):
    work[...] = before[...]
    factor_step(b, work, out, block)


def later_step(b, work, token):
    size = work.shape[0]
    return kernel(
        functools.partial(later_kernel, b),
        [shape(lanes, size), shape(size, size)],
        [vmem, anywhere],
        [pltpu.VMEM((lanes, lanes), jnp.float32)],
        "factor_later",
    )(work, token)


def share_norms(right_rows):
    squares = lax.psum(jnp.sum(right_rows * right_rows, axis=0), ("fsdp", "tensor"))
    return jnp.sqrt(squares + epsilon)


def any_mesh(momentum, gradient, right_basis):
    summed = momentum + gradient.astype(jnp.float32)
    left_raw = lax.psum(dot(summed, right_basis), "tensor")
    gram = lax.psum(dot(left_raw, left_raw, ((0,), (0,))), "fsdp")
    inverse = inverse_factor(gram)
    left = dot(left_raw, inverse, ((1,), (1,)))
    total_rows = left.shape[0] * lax.axis_size("fsdp")
    total_cols = summed.shape[1] * lax.axis_size("tensor")
    raw_rows = lax.psum_scatter(
        dot(summed, left_raw, ((0,), (0,))), "fsdp", scatter_dimension=0, tiled=True
    )
    right_rows = dot(raw_rows, inverse, ((1,), (1,)))
    column_norm = share_norms(right_rows)
    scaled_left = left * (math.sqrt(total_rows / total_cols) / column_norm)[None, :]
    raw = lax.all_gather(raw_rows, "fsdp", axis=0, tiled=True)
    product = dot(dot(left, inverse), raw, ((1,), (1,)))
    update = dot(dot(scaled_left, inverse), raw, ((1,), (1,))).astype(jnp.bfloat16)
    new_momentum = summed - 0.5 * product
    return (update, new_momentum, left * math.sqrt(total_rows), right_rows / column_norm[None, :])


def swap(value, axis, flip):
    return lax.ppermute(value, axis, [(i, i ^ flip) for i in range(lax.axis_size(axis))])


def split_kernel(bits, momentum, gradient, *pieces):
    width = pieces[0].shape[1]
    for k, piece in enumerate(pieces):
        at = pl.ds(pl.multiple_of((bits[2] ^ k) * width, lanes), width)
        piece[...] = momentum[:, at] + gradient[:, at].astype(jnp.float32)


def part_left_kernel(bits, basis, *refs):
    pieces, (sent, kept, total) = refs[:square], refs[square:]
    width = pieces[0].shape[1]
    half = sent.shape[0]
    for k, piece in enumerate(pieces):
        rows = pl.ds(pl.multiple_of((bits[2] ^ k) * width, lanes), width)
        part = dot(piece[...], basis[rows, :])
        total[...] = part if k == 0 else total[...] + part
    sent[...] = total[pl.ds(pl.multiple_of((1 - bits[0]) * half, 8), half), :]
    kept[...] = total[pl.ds(pl.multiple_of(bits[0] * half, 8), half), :]


def add_kernel(*refs):
    refs[-1][...] = refs[0][...] + refs[1][...]


def add_after(a, b, *tokens):
    return kernel(
        add_kernel, shape(*a.shape), [vmem] * 2 + [anywhere] * len(tokens), [], "add_after"
    )(a, b, *tokens)


def gram_kernel(bits, *refs):
    parts, (sent, kept, rows, stack) = refs[:square], refs[square:]
    half, rank = parts[0].shape
    share = sent.shape[0]
    for k, part in enumerate(parts):
        rows[k * half : (k + 1) * half, :] = part[...]
    at = 0
    for first in range(0, rank, lanes):
        left, right = rows[:, first:], rows[:, first : first + lanes]
        stack[at : at + rank - first, :] = dot(left, right, ((0,), (0,)))
        at += rank - first
    for out, core in ((kept, bits[0]), (sent, 1 - bits[0])):
        index = (2 * bits[1] + core) * square + bits[2]
        out[...] = stack[pl.ds(pl.multiple_of(index * share, 8), share), :]


def order_kernel(bits, *refs):
    out = refs[-1]
    share = refs[0].shape[0]
    for k in range(square):
        out[pl.ds(pl.multiple_of((bits[2] ^ k) * share, 8), share), :] = refs[k][...]


def raw_kernel(bits, token, *refs):
    mine, others, columns = refs[:square], refs[square : 2 * square], refs[2 * square : 3 * square]
    sent, kept, left, right, raw = refs[3 * square :]
    rows = columns[0].shape[0]
    half = rows // 2
    for k in range(square):
        left[k * rows : (k + 1) * rows, :] = columns[k][...]
        right[pl.ds(pl.multiple_of(k * rows + bits[0] * half, 8), half), :] = mine[k][...]
        right[pl.ds(pl.multiple_of(k * rows + (1 - bits[0]) * half, 8), half), :] = others[k][...]
    raw[...] = dot(left[...], right[...], ((0,), (0,)))
    count = kept.shape[0]
    kept[...] = raw[pl.ds(pl.multiple_of(bits[4] * count, 8), count), :]
    sent[...] = raw[pl.ds(pl.multiple_of((1 - bits[4]) * count, 8), count), :]


def left_kernel(scale, bits, mine, other, *refs):
    inverses, (left, left_scaled, inverse, rows) = refs[:-4], refs[-4:]
    half = mine.shape[0]
    for b, part in enumerate(inverses):
        inverse[b * lanes : (b + 1) * lanes, :] = part[...]
    rows[pl.ds(pl.multiple_of(bits[0] * half, 8), half), :] = mine[...]
    rows[pl.ds(pl.multiple_of((1 - bits[0]) * half, 8), half), :] = other[...]
    left[...] = dot(rows[...], inverse[...], ((1,), (1,)))
    left_scaled[...] = left[...] * scale


def norm_kernel(own, received, inverse, *refs):
    own_right, out = refs[-2:]
    count = own.shape[0]
    own_right[...] = dot(own[...], inverse[...], ((1,), (1,)))
    right = dot(received[...], inverse[...], ((1,), (1,)))
    out[:count, :] = right
    total = jnp.sum(right * right, axis=0, keepdims=True)
    total = total + jnp.sum(own_right[...] * own_right[...], axis=0, keepdims=True)
    row = lax.broadcasted_iota(jnp.int32, (8, own.shape[1]), 0)
    out[count:, :] = jnp.where(row == 0, total, 0.0)


def own_kernel(left, inverse, own_right, *refs):
    rows, (rights, products) = refs[:-2], refs[-2:]
    count = own_right.shape[0]
    for k in range(square):
        if k == 0:
            right = own_right[...]
        else:
            right = dot(rows[k - 1][...], inverse[...], ((1,), (1,)))
        rights[k * count : (k + 1) * count, :] = right
    for k in range(square):
        products[k] = dot_three(left[...], rights[k * count : (k + 1) * count, :])


def momentum_kernel(bits, left, products, *refs):
    pieces, received = refs[:square], refs[square : 2 * square]
    new_momentum = refs[-1]
    width = pieces[0].shape[1]
    half = width // 2
    for k in range(square):
        at = pl.ds(pl.multiple_of((bits[2] ^ k) * width, lanes), width)
        other = dot_three(left[...], received[k][:half, :])
        lower = jnp.concatenate([products[k], other], axis=1)
        upper = jnp.concatenate([other, products[k]], axis=1)
        new_momentum[:, at] = pieces[k][...] - 0.5 * jnp.where(bits[4] == 0, lower, upper)


def squares_kernel(row, *refs):
    total = refs[0][row : row + 1, :]
    for part in refs[1:square]:
        total = total + part[row : row + 1, :]
    refs[-1][...] = total


def update_kernel(factor, bits, squares, left, rights, *refs):
    received, (update, next_basis, right) = refs[:square], refs[square:]
    rows = left.shape[0]
    cols = update.shape[1]
    width = cols // square
    half = width // 2
    inverse_norm = 1.0 / jnp.sqrt(squares[...] + epsilon)
    for k in range(square):
        at = pl.multiple_of(k * width + bits[4] * half, 8)
        right[pl.ds(at, half), :] = rights[k * half : (k + 1) * half, :]
        at = pl.multiple_of(k * width + (1 - bits[4]) * half, 8)
        right[pl.ds(at, half), :] = received[k][:half, :]
    scaled = left[...] * (factor * inverse_norm)
    for k in range(0, square, 2):
        both = dot_three(scaled, right[k * width : (k + 2) * width, :]).astype(jnp.bfloat16)
        for i in range(2):
            at = pl.ds(pl.multiple_of((bits[2] ^ (k + i)) * width, lanes), width)
            update[:, at] = both[:, i * width : (i + 1) * width]
    count = next_basis.shape[0]
    place = ((bits[3] // 2) ^ bits[2]) * width + (bits[3] % 2) * half
    own = right[pl.ds(pl.multiple_of(place, 8), count), :]
    next_basis[...] = own / jnp.sqrt(squares[...] + epsilon)


def in_squares(momentum, gradient, right_basis):
    device = lax.axis_index("fsdp")
    tensor = lax.axis_index("tensor")
    bits = jnp.stack([tensor % 2, tensor // 2, device % square, device, device // square])
    bits = bits.astype(jnp.int32)
    rows, cols = momentum.shape
    rank = right_basis.shape[1]
    half, width = rows // 2, cols // square
    total_rows = rows * lax.axis_size("fsdp")
    total_cols = cols * lax.axis_size("tensor")

    pieces = kernel(split_kernel, [shape(rows, width)] * square, [smem, vmem, vmem], [], "split_sum")(
        bits, momentum, gradient
    )
    columns = [pieces[0]] + [swap(pieces[k], "fsdp", k) for k in range(1, square)]

    sent, kept = kernel(
        part_left_kernel,
        [shape(half, rank)] * 2,
        [smem] + [vmem] * (1 + square),
        [pltpu.VMEM((rows, rank), jnp.float32)],
        "part_left",
    )(bits, right_basis, *pieces)
    mine = kept + swap(sent, "tensor", 1)
    mine = add_after(mine, swap(mine, "tensor", 2), *columns[1:])
    gathered = [mine] + [swap(mine, "fsdp", k) for k in range(1, square)]
    others = [swap(part, "tensor", 1) for part in gathered]

    count = rank // lanes
    stacked = count * (count + 1) // 2 * lanes
    share = stacked // (4 * square)
    gram_sent, gram_kept = kernel(
        gram_kernel,
        [shape(share, lanes)] * 2,
        [smem] + [vmem] * square,
        [pltpu.VMEM((square * half, rank), jnp.float32), pltpu.VMEM((stacked, lanes), jnp.float32)],
        "part_gram",
    )(bits, *gathered)
    part = gram_kept + swap(gram_sent, "tensor", 1)

    sent, kept = kernel(
        raw_kernel,
        [shape(width // 2, rank)] * 2,
        [smem, anywhere] + [vmem] * (3 * square),
        [
            pltpu.VMEM((square * rows, width), jnp.float32),
            pltpu.VMEM((square * rows, rank), jnp.float32),
            pltpu.VMEM((width, rank), jnp.float32),
        ],
        "part_raw",
    )(bits, part, *gathered, *others, *columns)

    part = part + swap(part, "fsdp", square)
    quarter = kernel(
        order_kernel, shape(square * share, lanes), [smem] + [vmem] * square, [], "order"
    )(bits, part, *[swap(part, "fsdp", k) for k in range(1, square)])
    over_planes = swap(quarter, "tensor", 2)
    shares = [quarter, swap(quarter, "tensor", 1), over_planes, swap(over_planes, "tensor", 1)]

    factors = []
    out, work = first_step(bits, shares, rank)
    factors.append(out)
    token = out
    for b in range(1, count):
        if b == (count + 1) // 2:
            own = add_after(kept, swap(sent, "fsdp", square), out)
            token = own
        out, work = later_step(b, work, token)
        factors.append(out)
    left, left_scaled, inverse = kernel(
        functools.partial(left_kernel, math.sqrt(total_rows)),
        [shape(rows, rank), shape(rows, rank), shape(rank, rank)],
        [smem] + [vmem] * (2 + count),
        [pltpu.VMEM((rows, rank), jnp.float32)],
        "left",
    )(bits, mine, others[0], *factors)

    received = swap(own, "fsdp", square)
    own_rows = [own] + [swap(own, "fsdp", k) for k in range(1, square)]
    own_right, with_norms = kernel(
        norm_kernel,
        [shape(width // 2, rank), shape(width // 2 + 8, rank)],
        [vmem] * 3 + [anywhere] * (square - 1),
        [],
        "norms",
    )(own, received, inverse, *own_rows[1:])
    received_rows = [with_norms] + [swap(with_norms, "fsdp", k) for k in range(1, square)]
    rights, products = kernel(
        own_kernel,
        [shape(square * (width // 2), rank), shape(square, rows, width // 2)],
        [vmem] * (2 + square),
        [],
        "own_part",
        cost=2**24,
    )(left, inverse, own_right, *own_rows[1:])
    squares = kernel(
        functools.partial(squares_kernel, width // 2),
        shape(1, rank),
        [vmem] * square + [anywhere],
        [],
        "squares",
    )(*received_rows, products)
    squares = squares + swap(squares, "tensor", 1)
    squares = squares + swap(squares, "tensor", 2)

    new_momentum = kernel(
        momentum_kernel,
        shape(rows, cols),
        [smem] + [vmem] * (2 + 2 * square),
        [],
        "new_momentum",
        cost=2**22,
    )(bits, left, products, *pieces, *received_rows)
    update, next_basis = kernel(
        functools.partial(update_kernel, math.sqrt(total_rows / total_cols)),
        [shape(rows, cols, dtype=jnp.bfloat16), shape(cols // lax.axis_size("fsdp"), rank)],
        [smem] + [vmem] * (3 + square),
        [pltpu.VMEM((cols, rank), jnp.float32)],
        "update",
    )(bits, squares, left, rights, *received_rows)
    return (update, new_momentum, left_scaled, next_basis)


def on_device(momentum, gradient, right_basis):
    rows, cols = momentum.shape
    pairs = lax.axis_size("fsdp") == 2 * square and lax.axis_size("tensor") == 4
    aligned = rows % 16 == 0 and cols % (square * lanes) == 0 and right_basis.shape[1] % lanes == 0
    plan = in_squares if pairs and aligned else any_mesh
    return plan(momentum, gradient, right_basis)


def solution(mesh):
    in_specs = (P("fsdp", "tensor"), P("fsdp", "tensor"), P("tensor", None))
    out_specs = (
        P("fsdp", "tensor"),
        P("fsdp", "tensor"),
        P("fsdp", None),
        P(("tensor", "fsdp"), None),
    )
    return jax.shard_map(
        on_device, mesh=mesh, in_specs=in_specs, out_specs=out_specs, check_vma=False
    )
```

```python
import functools
import math

import jax
import jax.numpy as jnp
from jax import lax
from jax.experimental import pallas as pl
from jax.experimental.pallas import tpu as pltpu
from jax.sharding import PartitionSpec as P

epsilon = 1e-06
highest = lax.Precision.HIGHEST
lanes = 128
panel = 8
square = 4


def dot(a, b, contract=((1,), (0,))):
    return lax.dot_general(
        a, b, (contract, ((), ())), precision=highest, preferred_element_type=jnp.float32
    )


vmem = pl.BlockSpec(memory_space=pltpu.VMEM)
smem = pl.BlockSpec(memory_space=pltpu.SMEM)
anywhere = pl.BlockSpec(memory_space=pl.ANY)


def kernel(body, out_shape, in_specs, scratch, name, cost=0):
    return pl.pallas_call(
        body,
        out_shape=out_shape,
        in_specs=in_specs,
        scratch_shapes=scratch,
        compiler_params=pltpu.CompilerParams(vmem_limit_bytes=32 * 2**20),
        cost_estimate=pl.CostEstimate(flops=0, bytes_accessed=cost, transcendentals=0),
        name=name,
    )


def shape(*dims, dtype=jnp.float32):
    return jax.ShapeDtypeStruct(dims, dtype)


def split(value):
    high = value.astype(jnp.bfloat16)
    return high, (value - high.astype(jnp.float32)).astype(jnp.bfloat16)


def three_left(value):
    high, low = split(value)
    return jnp.concatenate([high, high, low], axis=1)


def three_right(value):
    high, low = split(value)
    return jnp.concatenate([high, low, high], axis=1)


def dot_three(a, b):
    return lax.dot_general(a, b, (((1,), (1,)), ((), ())), preferred_element_type=jnp.float32)


def factor_block(block):
    size = block.shape[0]
    lane = lax.broadcasted_iota(jnp.int32, (panel, size), 1)
    row = lax.broadcasted_iota(jnp.int32, (panel, size), 0)
    for first in range(0, size, panel):
        count = size - first
        now = block[first:, :]
        columns = [
            jnp.broadcast_to(now[:, first + k : first + k + 1], (count, size)) for k in range(panel)
        ]
        inside = (lane >= first) & (lane < first + panel)
        head = jnp.where(inside, jnp.where(lane - first == row, 1.0, 0.0), now[:panel])
        tail = None
        if count > panel:
            lane_below = lax.broadcasted_iota(jnp.int32, (count - panel, size), 1)
            inside_below = (lane_below >= first) & (lane_below < first + panel)
            tail = jnp.where(inside_below, 0.0, now[panel:])
        for j in range(panel):
            inverse = lax.rsqrt(columns[j][j : j + 1, :])
            multiplier = columns[j] * inverse
            for k in range(j + 1, panel):
                columns[k] = columns[k] - multiplier * (columns[k][j : j + 1, :] * inverse)
            pivot = head[j : j + 1, :] * inverse
            below = jnp.where(row > j, head - multiplier[:panel] * pivot, head)
            head = jnp.where(row == j, pivot, below)
            if tail is not None:
                tail = tail - multiplier[panel:] * pivot
        block[first : first + panel, :] = head
        if tail is not None:
            block[first + panel :, :] = tail


def place_gram(bits, shares, work):
    size = work.shape[0]
    count = size // lanes
    core, plane = bits[0], bits[1]
    stack = shares.pop()
    share = shares[0].shape[0]
    for flip_plane in range(2):
        for flip_core in range(2):
            at = pl.multiple_of(((plane ^ flip_plane) * 2 + (core ^ flip_core)) * share, 8)
            stack[pl.ds(at, share), :] = shares[flip_plane * 2 + flip_core][...]
    at = 0
    for j in range(count):
        for i in range(j, count):
            block = stack[at * lanes : (at + 1) * lanes, :]
            work[j * lanes : (j + 1) * lanes, i * lanes : (i + 1) * lanes] = block.T
            at += 1


def factor_step(b, work, out, block):
    size = work.shape[0]
    count = size // lanes
    row = lax.broadcasted_iota(jnp.int32, (lanes, lanes), 0)
    lower = row >= lax.broadcasted_iota(jnp.int32, (lanes, lanes), 1)
    rows = slice(b * lanes, (b + 1) * lanes)
    past = (b + 1) * lanes
    block[...] = work[rows, rows]
    factor_block(block)
    inverse = jnp.where(lower, block[...], 0.0)
    out[:, rows] = inverse
    if b:
        out[:, : b * lanes] = dot(inverse, work[rows, : b * lanes])
    if past < size:
        out[:, past:] = jnp.zeros((lanes, size - past), jnp.float32)
        upper = dot(inverse, work[rows, past:])
        own = out[:, :past]
        for i in range(b + 1, count):
            at = (i - b - 1) * lanes
            left = upper[:, at : at + lanes]
            below = slice(i * lanes, (i + 1) * lanes)
            work[below, i * lanes :] = work[below, i * lanes :] - dot(left, upper[:, at:], ((0,), (0,)))
            change = dot(left, own, ((0,), (0,)))
            if b:
                work[below, : b * lanes] = work[below, : b * lanes] - change[:, : b * lanes]
            work[below, b * lanes : past] = -change[:, b * lanes :]


def whole_kernel(gram, out, work, block):
    work[...] = gram[...]
    for b in range(work.shape[0] // lanes):
        factor_step(b, work, out.at[b * lanes : (b + 1) * lanes], block)


def inverse_factor(gram):
    size = gram.shape[0]
    return kernel(
        whole_kernel,
        jax.ShapeDtypeStruct((size, size), jnp.float32),
        [vmem],
        [pltpu.VMEM((size, size), jnp.float32), pltpu.VMEM((lanes, lanes), jnp.float32)],
        "inverse_factor",
    )(gram)


def first_kernel(bits, a, b, c, d, out, work, stack, block):
    place_gram(bits, [a, b, c, d, stack], work)
    factor_step(0, work, out, block)


def first_step(bits, shares, size):
    blocks = sum(x.shape[0] for x in shares)
    return kernel(
        first_kernel,
        [shape(lanes, size), shape(size, size)],
        [smem] + [vmem] * 4,
        [pltpu.VMEM((blocks, lanes), jnp.float32), pltpu.VMEM((lanes, lanes), jnp.float32)],
        "factor_first",
    )(bits, *shares)


def later_kernel(b, before, token, out, work, block):
    work[...] = before[...]
    factor_step(b, work, out, block)


def later_step(b, work, token):
    size = work.shape[0]
    return kernel(
        functools.partial(later_kernel, b),
        [shape(lanes, size), shape(size, size)],
        [vmem, anywhere],
        [pltpu.VMEM((lanes, lanes), jnp.float32)],
        "factor_later",
    )(work, token)


def share_norms(right_rows):
    squares = lax.psum(jnp.sum(right_rows * right_rows, axis=0), ("fsdp", "tensor"))
    return jnp.sqrt(squares + epsilon)


def any_mesh(momentum, gradient, right_basis):
    summed = momentum + gradient.astype(jnp.float32)
    left_raw = lax.psum(dot(summed, right_basis), "tensor")
    gram = lax.psum(dot(left_raw, left_raw, ((0,), (0,))), "fsdp")
    inverse = inverse_factor(gram)
    left = dot(left_raw, inverse, ((1,), (1,)))
    total_rows = left.shape[0] * lax.axis_size("fsdp")
    total_cols = summed.shape[1] * lax.axis_size("tensor")
    raw_rows = lax.psum_scatter(
        dot(summed, left_raw, ((0,), (0,))), "fsdp", scatter_dimension=0, tiled=True
    )
    right_rows = dot(raw_rows, inverse, ((1,), (1,)))
    column_norm = share_norms(right_rows)
    scaled_left = left * (math.sqrt(total_rows / total_cols) / column_norm)[None, :]
    raw = lax.all_gather(raw_rows, "fsdp", axis=0, tiled=True)
    product = dot(dot(left, inverse), raw, ((1,), (1,)))
    update = dot(dot(scaled_left, inverse), raw, ((1,), (1,))).astype(jnp.bfloat16)
    new_momentum = summed - 0.5 * product
    return (update, new_momentum, left * math.sqrt(total_rows), right_rows / column_norm[None, :])


def swap(value, axis, flip):
    return lax.ppermute(value, axis, [(i, i ^ flip) for i in range(lax.axis_size(axis))])


def split_kernel(bits, momentum, gradient, *pieces):
    width = pieces[0].shape[1]
    for k, piece in enumerate(pieces):
        at = pl.ds(pl.multiple_of((bits[2] ^ k) * width, lanes), width)
        piece[...] = momentum[:, at] + gradient[:, at].astype(jnp.float32)


def part_left_kernel(bits, basis, *refs):
    pieces, (sent, kept, total) = refs[:square], refs[square:]
    width = pieces[0].shape[1]
    half = sent.shape[0]
    for k, piece in enumerate(pieces):
        rows = pl.ds(pl.multiple_of((bits[2] ^ k) * width, lanes), width)
        part = dot(piece[...], basis[rows, :])
        total[...] = part if k == 0 else total[...] + part
    sent[...] = total[pl.ds(pl.multiple_of((1 - bits[0]) * half, 8), half), :]
    kept[...] = total[pl.ds(pl.multiple_of(bits[0] * half, 8), half), :]


def core_add_kernel(bits, kept, both, out):
    half = kept.shape[0]
    out[...] = kept[...] + both[pl.ds(pl.multiple_of((1 - bits[0]) * half, 8), half), :]


def add_kernel(*refs):
    refs[-1][...] = refs[0][...] + refs[1][...]


def add_after(a, b, *tokens):
    return kernel(
        add_kernel, shape(*a.shape), [vmem] * 2 + [anywhere] * len(tokens), [], "add_after"
    )(a, b, *tokens)


def gram_kernel(bits, *refs):
    parts, (sent, kept, rows, stack) = refs[:square], refs[square:]
    half, rank = parts[0].shape
    share = sent.shape[0]
    for k, part in enumerate(parts):
        rows[k * half : (k + 1) * half, :] = part[...]
    at = 0
    for first in range(0, rank, 2 * lanes):
        last = min(first + 2 * lanes, rank)
        product = dot(rows[:, first:], rows[:, first:last], ((0,), (0,)))
        for j in range(0, last - first, lanes):
            stack[at : at + rank - first - j, :] = product[j:, j : j + lanes]
            at += rank - first - j
    for out, core in ((kept, bits[0]), (sent, 1 - bits[0])):
        index = (2 * bits[1] + core) * 2 + bits[2] % 2
        out[...] = stack[pl.ds(pl.multiple_of(index * share, 8), share), :]


def order_kernel(bits, *refs):
    out = refs[-1]
    share = refs[0].shape[0]
    for k in range(2):
        out[pl.ds(pl.multiple_of((bits[2] % 2 ^ k) * share, 8), share), :] = refs[k][...]


def raw_kernel(bits, token, *refs):
    mine, others, columns = refs[:square], refs[square : 2 * square], refs[2 * square : 3 * square]
    sent, kept, left, right, raw = refs[3 * square :]
    rows = columns[0].shape[0]
    half = rows // 2
    for k in range(square):
        left[k * rows : (k + 1) * rows, :] = columns[k][...]
        right[pl.ds(pl.multiple_of(k * rows + bits[0] * half, 8), half), :] = mine[k][...]
        right[pl.ds(pl.multiple_of(k * rows + (1 - bits[0]) * half, 8), half), :] = others[k][...]
    raw[...] = dot(left[...], right[...], ((0,), (0,)))
    count = kept.shape[0]
    kept[...] = raw[pl.ds(pl.multiple_of(bits[4] * count, 8), count), :]
    sent[...] = raw[pl.ds(pl.multiple_of((1 - bits[4]) * count, 8), count), :]


def left_kernel(scale, bits, mine, other, *refs):
    inverses, (left, left_scaled, inverse, rows) = refs[:-4], refs[-4:]
    half = mine.shape[0]
    for b, part in enumerate(inverses):
        inverse[b * lanes : (b + 1) * lanes, :] = part[...]
    rows[pl.ds(pl.multiple_of(bits[0] * half, 8), half), :] = mine[...]
    rows[pl.ds(pl.multiple_of((1 - bits[0]) * half, 8), half), :] = other[...]
    left[...] = dot(rows[...], inverse[...], ((1,), (1,)))
    left_scaled[...] = left[...] * scale


def norm_kernel(own, received, inverse, *refs):
    own_right, out = refs[-2:]
    count = own.shape[0]
    own_right[...] = dot(own[...], inverse[...], ((1,), (1,)))
    right = dot(received[...], inverse[...], ((1,), (1,)))
    out[:count, :] = right
    total = jnp.sum(right * right, axis=0, keepdims=True)
    total = total + jnp.sum(own_right[...] * own_right[...], axis=0, keepdims=True)
    row = lax.broadcasted_iota(jnp.int32, (8, own.shape[1]), 0)
    out[count:, :] = jnp.where(row == 0, total, 0.0)


def own_kernel(left, inverse, own_right, *refs):
    rows, (rights, splits, products) = refs[:-3], refs[-3:]
    count = own_right.shape[0]
    rights[:count, :] = own_right[...]
    for k in range(1, square):
        right = dot(rows[k - 1][...], inverse[...], ((1,), (1,)))
        rights[k * count : (k + 1) * count, :] = right
    splits[...] = three_right(rights[...])
    product = dot_three(three_left(left[...]), splits[...])
    for k in range(square):
        products[k] = product[:, k * count : (k + 1) * count]


def momentum_kernel(bits, left, products, *refs):
    pieces, received = refs[:square], refs[square : 2 * square]
    new_momentum, splits = refs[-2:]
    width = pieces[0].shape[1]
    half = width // 2
    for k in range(square):
        splits[k * half : (k + 1) * half, :] = three_right(received[k][:half, :])
    product = dot_three(three_left(left[...]), splits[...])
    for k in range(square):
        at = pl.ds(pl.multiple_of((bits[2] ^ k) * width, lanes), width)
        other = product[:, k * half : (k + 1) * half]
        lower = jnp.concatenate([products[k], other], axis=1)
        upper = jnp.concatenate([other, products[k]], axis=1)
        new_momentum[:, at] = pieces[k][...] - 0.5 * jnp.where(bits[4] == 0, lower, upper)


def squares_kernel(row, *refs):
    total = refs[0][row : row + 1, :]
    for part in refs[1:square]:
        total = total + part[row : row + 1, :]
    refs[-1][...] = total


def update_kernel(factor, bits, squares, left, rights, own_splits, splits, *refs):
    received, (update, next_basis) = refs[:square], refs[square:]
    half = next_basis.shape[0]
    width = 2 * half
    norm = jnp.sqrt(squares[...] + epsilon)
    scaled = three_left(left[...] * (factor / norm))
    mine = dot_three(scaled, own_splits[...])
    other = dot_three(scaled, splits[...])
    for k in range(square):
        at = pl.ds(pl.multiple_of((bits[2] ^ k) * width, lanes), width)
        parts = slice(k * half, (k + 1) * half)
        lower = jnp.concatenate([mine[:, parts], other[:, parts]], axis=1)
        upper = jnp.concatenate([other[:, parts], mine[:, parts]], axis=1)
        update[:, at] = jnp.where(bits[4] == 0, lower, upper).astype(jnp.bfloat16)
    for k in range(square):

        @pl.when((bits[3] // 2) ^ bits[2] == k)
        def _():
            mine_rows = rights[k * half : (k + 1) * half, :]
            rows = jnp.where(bits[3] % 2 == bits[4], mine_rows, received[k][:half, :])
            next_basis[...] = rows / norm


def in_squares(momentum, gradient, right_basis):
    device = lax.axis_index("fsdp")
    tensor = lax.axis_index("tensor")
    bits = jnp.stack([tensor % 2, tensor // 2, device % square, device, device // square])
    bits = bits.astype(jnp.int32)
    rows, cols = momentum.shape
    rank = right_basis.shape[1]
    half, width = rows // 2, cols // square
    total_rows = rows * lax.axis_size("fsdp")
    total_cols = cols * lax.axis_size("tensor")

    pieces = kernel(split_kernel, [shape(rows, width)] * square, [smem, vmem, vmem], [], "split_sum")(
        bits, momentum, gradient
    )
    columns = [pieces[0]] + [swap(pieces[k], "fsdp", k) for k in range(1, square)]

    sent, kept = kernel(
        part_left_kernel,
        [shape(half, rank)] * 2,
        [smem] + [vmem] * (1 + square),
        [pltpu.VMEM((rows, rank), jnp.float32)],
        "part_left",
    )(bits, right_basis, *pieces)
    cores = [[i, i + 1] for i in range(0, lax.axis_size("tensor"), 2)]
    both = lax.all_gather(sent, "tensor", axis=0, tiled=True, axis_index_groups=cores)
    mine = kernel(core_add_kernel, shape(half, rank), [smem, vmem, vmem], [], "core_add")(
        bits, kept, both
    )
    mine = add_after(mine, swap(mine, "tensor", 2), *columns[1:])
    gathered = [mine] + [swap(mine, "fsdp", k) for k in range(1, square)]
    others = [swap(part, "tensor", 1) for part in gathered]

    count = rank // lanes
    stacked = count * (count + 1) // 2 * lanes
    share = stacked // 8
    gram_sent, gram_kept = kernel(
        gram_kernel,
        [shape(share, lanes)] * 2,
        [smem] + [vmem] * square,
        [pltpu.VMEM((square * half, rank), jnp.float32), pltpu.VMEM((stacked, lanes), jnp.float32)],
        "part_gram",
    )(bits, *gathered)
    part = gram_kept + swap(gram_sent, "tensor", 1)

    sent, kept = kernel(
        raw_kernel,
        [shape(width // 2, rank)] * 2,
        [smem, anywhere] + [vmem] * (3 * square),
        [
            pltpu.VMEM((square * rows, width), jnp.float32),
            pltpu.VMEM((square * rows, rank), jnp.float32),
            pltpu.VMEM((width, rank), jnp.float32),
        ],
        "part_raw",
    )(bits, part, *gathered, *others, *columns)

    part = add_after(part, swap(part, "fsdp", square), kept)
    quarter = kernel(
        order_kernel, shape(2 * share, lanes), [smem] + [vmem] * 2, [], "order"
    )(bits, part, swap(part, "fsdp", 1))
    over_planes = swap(quarter, "tensor", 2)
    shares = [quarter, swap(quarter, "tensor", 1), over_planes, swap(over_planes, "tensor", 1)]

    factors = []
    out, work = first_step(bits, shares, rank)
    factors.append(out)
    token = out
    for b in range(1, count):
        if b == (count + 1) // 2:
            own = add_after(kept, swap(sent, "fsdp", square), out)
            token = own
        out, work = later_step(b, work, token)
        factors.append(out)
    left, left_scaled, inverse = kernel(
        functools.partial(left_kernel, math.sqrt(total_rows)),
        [shape(rows, rank), shape(rows, rank), shape(rank, rank)],
        [smem] + [vmem] * (2 + count),
        [pltpu.VMEM((rows, rank), jnp.float32)],
        "left",
    )(bits, mine, others[0], *factors)

    received = swap(own, "fsdp", square)
    own_rows = [own] + [swap(own, "fsdp", k) for k in range(1, square)]
    own_right, with_norms = kernel(
        norm_kernel,
        [shape(width // 2, rank), shape(width // 2 + 8, rank)],
        [vmem] * 3 + [anywhere] * (square - 1),
        [],
        "norms",
    )(own, received, inverse, *own_rows[1:])
    received_rows = [with_norms] + [swap(with_norms, "fsdp", k) for k in range(1, square)]
    rights, own_splits, products = kernel(
        own_kernel,
        [
            shape(cols // 2, rank),
            shape(cols // 2, 3 * rank, dtype=jnp.bfloat16),
            shape(square, rows, width // 2),
        ],
        [vmem] * (2 + square),
        [],
        "own_part",
        cost=2**24,
    )(left, inverse, own_right, *own_rows[1:])
    squares = kernel(
        functools.partial(squares_kernel, width // 2),
        shape(1, rank),
        [vmem] * square + [anywhere],
        [],
        "squares",
    )(*received_rows, products)
    squares = squares + swap(squares, "tensor", 1)
    squares = squares + swap(squares, "tensor", 2)

    new_momentum, splits = kernel(
        momentum_kernel,
        [shape(rows, cols), shape(cols // 2, 3 * rank, dtype=jnp.bfloat16)],
        [smem] + [vmem] * (2 + 2 * square),
        [],
        "new_momentum",
        cost=2**22,
    )(bits, left, products, *pieces, *received_rows)
    update, next_basis = kernel(
        functools.partial(update_kernel, math.sqrt(total_rows / total_cols)),
        [shape(rows, cols, dtype=jnp.bfloat16), shape(cols // lax.axis_size("fsdp"), rank)],
        [smem] + [vmem] * (5 + square),
        [],
        "update",
    )(bits, squares, left, rights, own_splits, splits, *received_rows)
    return (update, new_momentum, left_scaled, next_basis)


def on_device(momentum, gradient, right_basis):
    rows, cols = momentum.shape
    pairs = lax.axis_size("fsdp") == 2 * square and lax.axis_size("tensor") == 4
    aligned = rows % 16 == 0 and cols % (square * lanes) == 0 and right_basis.shape[1] % lanes == 0
    plan = in_squares if pairs and aligned else any_mesh
    return plan(momentum, gradient, right_basis)


def solution(mesh):
    in_specs = (P("fsdp", "tensor"), P("fsdp", "tensor"), P("tensor", None))
    out_specs = (
        P("fsdp", "tensor"),
        P("fsdp", "tensor"),
        P("fsdp", None),
        P(("tensor", "fsdp"), None),
    )
    return jax.shard_map(
        on_device, mesh=mesh, in_specs=in_specs, out_specs=out_specs, check_vma=False
    )
```

```python
import functools
import math

import jax
import jax.numpy as jnp
from jax import lax
from jax.experimental import pallas as pl
from jax.experimental.pallas import tpu as pltpu
from jax.sharding import PartitionSpec as P

epsilon = 1e-06
highest = lax.Precision.HIGHEST
lanes = 128
panel = 8
square = 4


def dot(a, b, contract=((1,), (0,))):
    return lax.dot_general(
        a, b, (contract, ((), ())), precision=highest, preferred_element_type=jnp.float32
    )


vmem = pl.BlockSpec(memory_space=pltpu.VMEM)
smem = pl.BlockSpec(memory_space=pltpu.SMEM)
anywhere = pl.BlockSpec(memory_space=pl.ANY)


def kernel(body, out_shape, in_specs, scratch, name, cost=0, out_specs=None):
    extra = {} if out_specs is None else {"out_specs": out_specs}
    return pl.pallas_call(
        body,
        out_shape=out_shape,
        **extra,
        in_specs=in_specs,
        scratch_shapes=scratch,
        compiler_params=pltpu.CompilerParams(vmem_limit_bytes=32 * 2**20),
        cost_estimate=pl.CostEstimate(flops=0, bytes_accessed=cost, transcendentals=0),
        name=name,
    )


def shape(*dims, dtype=jnp.float32):
    return jax.ShapeDtypeStruct(dims, dtype)


def split(value):
    high = value.astype(jnp.bfloat16)
    return high, (value - high.astype(jnp.float32)).astype(jnp.bfloat16)


def three_left(value):
    high, low = split(value)
    return jnp.concatenate([high, high, low], axis=1)


def three_right(value):
    high, low = split(value)
    return jnp.concatenate([high, low, high], axis=1)


def dot_three(a, b):
    return lax.dot_general(a, b, (((1,), (1,)), ((), ())), preferred_element_type=jnp.float32)


def factor_block(block):
    size = block.shape[0]
    lane = lax.broadcasted_iota(jnp.int32, (panel, size), 1)
    row = lax.broadcasted_iota(jnp.int32, (panel, size), 0)
    for first in range(0, size, panel):
        count = size - first
        now = block[first:, :]
        columns = [
            jnp.broadcast_to(now[:, first + k : first + k + 1], (count, size)) for k in range(panel)
        ]
        inside = (lane >= first) & (lane < first + panel)
        head = jnp.where(inside, jnp.where(lane - first == row, 1.0, 0.0), now[:panel])
        tail = None
        if count > panel:
            lane_below = lax.broadcasted_iota(jnp.int32, (count - panel, size), 1)
            inside_below = (lane_below >= first) & (lane_below < first + panel)
            tail = jnp.where(inside_below, 0.0, now[panel:])
        for j in range(panel):
            inverse = lax.rsqrt(columns[j][j : j + 1, :])
            multiplier = columns[j] * inverse
            for k in range(j + 1, panel):
                columns[k] = columns[k] - multiplier * (columns[k][j : j + 1, :] * inverse)
            pivot = head[j : j + 1, :] * inverse
            below = jnp.where(row > j, head - multiplier[:panel] * pivot, head)
            head = jnp.where(row == j, pivot, below)
            if tail is not None:
                tail = tail - multiplier[panel:] * pivot
        block[first : first + panel, :] = head
        if tail is not None:
            block[first + panel :, :] = tail


def place_gram(bits, shares, work):
    size = work.shape[0]
    count = size // lanes
    core, plane = bits[0], bits[1]
    stack = shares.pop()
    share = shares[0].shape[0]
    for flip_plane in range(2):
        for flip_core in range(2):
            at = pl.multiple_of(((plane ^ flip_plane) * 2 + (core ^ flip_core)) * share, 8)
            stack[pl.ds(at, share), :] = shares[flip_plane * 2 + flip_core][...]
    at = 0
    for j in range(count):
        for i in range(j, count):
            block = stack[at * lanes : (at + 1) * lanes, :]
            work[j * lanes : (j + 1) * lanes, i * lanes : (i + 1) * lanes] = block.T
            at += 1


def factor_step(b, work, out, block):
    size = work.shape[0]
    count = size // lanes
    row = lax.broadcasted_iota(jnp.int32, (lanes, lanes), 0)
    lower = row >= lax.broadcasted_iota(jnp.int32, (lanes, lanes), 1)
    rows = slice(b * lanes, (b + 1) * lanes)
    past = (b + 1) * lanes
    block[...] = work[rows, rows]
    factor_block(block)
    inverse = jnp.where(lower, block[...], 0.0)
    out[:, rows] = inverse
    if b:
        out[:, : b * lanes] = dot(inverse, work[rows, : b * lanes])
    if past < size:
        out[:, past:] = jnp.zeros((lanes, size - past), jnp.float32)
        upper = dot(inverse, work[rows, past:])
        own = out[:, :past]
        for i in range(b + 1, count):
            at = (i - b - 1) * lanes
            left = upper[:, at : at + lanes]
            below = slice(i * lanes, (i + 1) * lanes)
            work[below, i * lanes :] = work[below, i * lanes :] - dot(left, upper[:, at:], ((0,), (0,)))
            change = dot(left, own, ((0,), (0,)))
            if b:
                work[below, : b * lanes] = work[below, : b * lanes] - change[:, : b * lanes]
            work[below, b * lanes : past] = -change[:, b * lanes :]


def whole_kernel(gram, out, work, block):
    work[...] = gram[...]
    for b in range(work.shape[0] // lanes):
        factor_step(b, work, out.at[b * lanes : (b + 1) * lanes], block)


def inverse_factor(gram):
    size = gram.shape[0]
    return kernel(
        whole_kernel,
        jax.ShapeDtypeStruct((size, size), jnp.float32),
        [vmem],
        [pltpu.VMEM((size, size), jnp.float32), pltpu.VMEM((lanes, lanes), jnp.float32)],
        "inverse_factor",
    )(gram)


def first_kernel(bits, a, b, c, d, out, work, stack, block):
    place_gram(bits, [a, b, c, d, stack], work)
    factor_step(0, work, out, block)


def first_step(bits, shares, size):
    blocks = sum(x.shape[0] for x in shares)
    return kernel(
        first_kernel,
        [shape(lanes, size), shape(size, size)],
        [smem] + [vmem] * 4,
        [pltpu.VMEM((blocks, lanes), jnp.float32), pltpu.VMEM((lanes, lanes), jnp.float32)],
        "factor_first",
    )(bits, *shares)


def later_kernel(b, before, token, out, work, block):
    work[...] = before[...]
    factor_step(b, work, out, block)


def later_step(b, work, token):
    size = work.shape[0]
    return kernel(
        functools.partial(later_kernel, b),
        [shape(lanes, size), shape(size, size)],
        [vmem, anywhere],
        [pltpu.VMEM((lanes, lanes), jnp.float32)],
        "factor_later",
    )(work, token)


def share_norms(right_rows):
    squares = lax.psum(jnp.sum(right_rows * right_rows, axis=0), ("fsdp", "tensor"))
    return jnp.sqrt(squares + epsilon)


def any_mesh(momentum, gradient, right_basis):
    summed = momentum + gradient.astype(jnp.float32)
    left_raw = lax.psum(dot(summed, right_basis), "tensor")
    gram = lax.psum(dot(left_raw, left_raw, ((0,), (0,))), "fsdp")
    inverse = inverse_factor(gram)
    left = dot(left_raw, inverse, ((1,), (1,)))
    total_rows = left.shape[0] * lax.axis_size("fsdp")
    total_cols = summed.shape[1] * lax.axis_size("tensor")
    raw_rows = lax.psum_scatter(
        dot(summed, left_raw, ((0,), (0,))), "fsdp", scatter_dimension=0, tiled=True
    )
    right_rows = dot(raw_rows, inverse, ((1,), (1,)))
    column_norm = share_norms(right_rows)
    scaled_left = left * (math.sqrt(total_rows / total_cols) / column_norm)[None, :]
    raw = lax.all_gather(raw_rows, "fsdp", axis=0, tiled=True)
    product = dot(dot(left, inverse), raw, ((1,), (1,)))
    update = dot(dot(scaled_left, inverse), raw, ((1,), (1,))).astype(jnp.bfloat16)
    new_momentum = summed - 0.5 * product
    return (update, new_momentum, left * math.sqrt(total_rows), right_rows / column_norm[None, :])


def swap(value, axis, flip):
    return lax.ppermute(value, axis, [(i, i ^ flip) for i in range(lax.axis_size(axis))])


def split_kernel(bits, momentum, gradient, *pieces):
    width = pieces[0].shape[1]
    for k, piece in enumerate(pieces):
        at = pl.ds(pl.multiple_of((bits[2] ^ k) * width, lanes), width)
        piece[...] = momentum[:, at] + gradient[:, at].astype(jnp.float32)


def part_left_kernel(bits, basis, *refs):
    pieces, (sent, kept, total) = refs[:square], refs[square:]
    width = pieces[0].shape[1]
    half = sent.shape[0]
    for k, piece in enumerate(pieces):
        rows = pl.ds(pl.multiple_of((bits[2] ^ k) * width, lanes), width)
        part = dot(piece[...], basis[rows, :])
        total[...] = part if k == 0 else total[...] + part
    sent[...] = total[pl.ds(pl.multiple_of((1 - bits[0]) * half, 8), half), :]
    kept[...] = total[pl.ds(pl.multiple_of(bits[0] * half, 8), half), :]


def core_add_kernel(bits, kept, both, out):
    half = kept.shape[0]
    out[...] = kept[...] + both[pl.ds(pl.multiple_of((1 - bits[0]) * half, 8), half), :]


def add_kernel(*refs):
    refs[-1][...] = refs[0][...] + refs[1][...]


def add_after(a, b, *tokens):
    return kernel(
        add_kernel, shape(*a.shape), [vmem] * 2 + [anywhere] * len(tokens), [], "add_after"
    )(a, b, *tokens)


def gram_kernel(bits, *refs):
    parts, (sent, kept, rows, stack) = refs[:square], refs[square:]
    half, rank = parts[0].shape
    share = sent.shape[0]
    for k, part in enumerate(parts):
        rows[k * half : (k + 1) * half, :] = part[...]
    at = 0
    for first in range(0, rank, 2 * lanes):
        last = min(first + 2 * lanes, rank)
        product = dot(rows[:, first:], rows[:, first:last], ((0,), (0,)))
        for j in range(0, last - first, lanes):
            stack[at : at + rank - first - j, :] = product[j:, j : j + lanes]
            at += rank - first - j
    for out, core in ((kept, bits[0]), (sent, 1 - bits[0])):
        index = (2 * bits[1] + core) * 2 + bits[2] % 2
        out[...] = stack[pl.ds(pl.multiple_of(index * share, 8), share), :]


def raw_kernel(bits, token, *refs):
    mine, others, columns = refs[:square], refs[square : 2 * square], refs[2 * square : 3 * square]
    sent, kept, left, right, raw = refs[3 * square :]
    rows = columns[0].shape[0]
    half = rows // 2
    for k in range(square):
        left[k * rows : (k + 1) * rows, :] = columns[k][...]
        right[pl.ds(pl.multiple_of(k * rows + bits[0] * half, 8), half), :] = mine[k][...]
        right[pl.ds(pl.multiple_of(k * rows + (1 - bits[0]) * half, 8), half), :] = others[k][...]
    raw[...] = dot(left[...], right[...], ((0,), (0,)))
    count = kept.shape[0]
    kept[...] = raw[pl.ds(pl.multiple_of(bits[4] * count, 8), count), :]
    sent[...] = raw[pl.ds(pl.multiple_of((1 - bits[4]) * count, 8), count), :]


def left_kernel(scale, bits, mine, other, own, *refs):
    inverses, (left, left_scaled, inverse, own_right, rows) = refs[:-5], refs[-5:]
    half = mine.shape[0]
    for b, part in enumerate(inverses):
        inverse[b * lanes : (b + 1) * lanes, :] = part[...]
    rows[pl.ds(pl.multiple_of(bits[0] * half, 8), half), :] = mine[...]
    rows[pl.ds(pl.multiple_of((1 - bits[0]) * half, 8), half), :] = other[...]
    left[...] = dot(rows[...], inverse[...], ((1,), (1,)))
    left_scaled[...] = left[...] * scale
    own_right[...] = dot(own[...], inverse[...], ((1,), (1,)))


def norm_kernel(own_right, received, inverse, one, two, out):
    count = own_right.shape[0]
    right = dot(received[...], inverse[...], ((1,), (1,)))
    out[:count, :] = right
    total = jnp.sum(right * right, axis=0, keepdims=True)
    total = total + jnp.sum(own_right[...] * own_right[...], axis=0, keepdims=True)
    row = lax.broadcasted_iota(jnp.int32, (8, own_right.shape[1]), 0)
    out[count:, :] = jnp.where(row == 0, total, 0.0)


def own_kernel(left, inverse, own_right, *refs):
    rows, (rights, splits, products) = refs[:-3], refs[-3:]
    count = own_right.shape[0]
    rights[:count, :] = own_right[...]
    for k, part in enumerate(rows):
        at = slice((k + 1) * count, (k + 2) * count)
        rights[at, :] = dot(part[...], inverse[...], ((1,), (1,)))
    splits[...] = three_right(rights[...])
    product = dot_three(three_left(left[...]), splits[...])
    for k in range(len(rows) + 1):
        products[k] = product[:, k * count : (k + 1) * count]


def diagonal_kernel(left, inverse, first, second, right, splits, product):
    middle = first.shape[0]
    right[:middle, :] = dot(first[...], inverse[...], ((1,), (1,)))
    right[middle:, :] = dot(second[...], inverse[...], ((1,), (1,)))
    splits[...] = three_right(right[...])
    product[...] = dot_three(three_left(left[...]), splits[...])


def momentum_kernel(bits, left, products, last_product, *refs):
    pieces, received = refs[:square], refs[square : 2 * square]
    new_momentum, splits, ready, sent = refs[-4:]
    width = pieces[0].shape[1]
    half = width // 2
    scaled = three_left(left[...])
    copies = []
    for k in range(square):
        parts = slice(k * half, (k + 1) * half)
        splits[parts, :] = three_right(received[k][:half, :])
        if k % 2 == 0:
            continue
        both = dot_three(scaled, splits[(k - 1) * half : (k + 1) * half, :])
        for i in (k - 1, k):
            other = both[:, (i - k + 1) * half : (i - k + 2) * half]
            mine = products[i] if i < square - 1 else last_product[...]
            lower = jnp.concatenate([mine, other], axis=1)
            upper = jnp.concatenate([other, mine], axis=1)
            ready[i] = pieces[i][...] - 0.5 * jnp.where(bits[4] == 0, lower, upper)
            at = pl.ds(pl.multiple_of((bits[2] ^ i) * width, lanes), width)
            copies.append(pltpu.make_async_copy(ready.at[i], new_momentum.at[:, at], sent.at[i]))
            copies[i].start()
    for copy in copies:
        copy.wait()


def squares_kernel(row, *refs):
    total = refs[0][row : row + 1, :]
    for part in refs[1:square]:
        total = total + part[row : row + 1, :]
    refs[-1][...] = total


def update_kernel(factor, bits, squares, left, rights, last_right, own_splits, last_split, splits, *refs):
    received, (update, next_basis, ready, basis_ready, sent) = refs[:square], refs[square:]
    half = basis_ready.shape[0]
    width = 2 * half
    norm = jnp.sqrt(squares[...] + epsilon)
    for k in range(square):

        @pl.when((bits[3] // 2) ^ bits[2] == k)
        def _():
            mine_rows = rights[k * half : (k + 1) * half, :] if k < square - 1 else last_right[...]
            rows = jnp.where(bits[3] % 2 == bits[4], mine_rows, received[k][:half, :])
            basis_ready[...] = rows / norm

    copies = [pltpu.make_async_copy(basis_ready, next_basis, sent.at[square])]
    copies[0].start()
    scaled = three_left(left[...] * (factor / norm))
    for k in range(square):
        parts = slice(k * half, (k + 1) * half)
        mine = dot_three(scaled, own_splits[parts, :] if k < square - 1 else last_split[...])
        other = dot_three(scaled, splits[parts, :])
        lower = jnp.concatenate([mine, other], axis=1)
        upper = jnp.concatenate([other, mine], axis=1)
        ready[k] = jnp.where(bits[4] == 0, lower, upper).astype(jnp.bfloat16)
        at = pl.ds(pl.multiple_of((bits[2] ^ k) * width, lanes), width)
        copy = pltpu.make_async_copy(ready.at[k], update.at[:, at], sent.at[k])
        copy.start()
        copies.append(copy)
    for copy in copies:
        copy.wait()


def in_squares(momentum, gradient, right_basis):
    device = lax.axis_index("fsdp")
    tensor = lax.axis_index("tensor")
    bits = jnp.stack([tensor % 2, tensor // 2, device % square, device, device // square])
    bits = bits.astype(jnp.int32)
    rows, cols = momentum.shape
    rank = right_basis.shape[1]
    half, width = rows // 2, cols // square
    total_rows = rows * lax.axis_size("fsdp")
    total_cols = cols * lax.axis_size("tensor")

    pieces = kernel(split_kernel, [shape(rows, width)] * square, [smem, vmem, vmem], [], "split_sum")(
        bits, momentum, gradient
    )
    columns = [pieces[0]] + [swap(pieces[k], "fsdp", k) for k in range(1, square)]

    sent, kept = kernel(
        part_left_kernel,
        [shape(half, rank)] * 2,
        [smem] + [vmem] * (1 + square),
        [pltpu.VMEM((rows, rank), jnp.float32)],
        "part_left",
    )(bits, right_basis, *pieces)
    cores = [[i, i + 1] for i in range(0, lax.axis_size("tensor"), 2)]
    both = lax.all_gather(sent, "tensor", axis=0, tiled=True, axis_index_groups=cores)
    mine = kernel(core_add_kernel, shape(half, rank), [smem, vmem, vmem], [], "core_add")(
        bits, kept, both
    )
    mine = add_after(mine, swap(mine, "tensor", 2), *columns[1:])
    gathered = [mine] + [swap(mine, "fsdp", k) for k in range(1, square)]
    others = [swap(part, "tensor", 1) for part in gathered]

    count = rank // lanes
    stacked = count * (count + 1) // 2 * lanes
    share = stacked // 8
    gram_sent, gram_kept = kernel(
        gram_kernel,
        [shape(share, lanes)] * 2,
        [smem] + [vmem] * square,
        [pltpu.VMEM((square * half, rank), jnp.float32), pltpu.VMEM((stacked, lanes), jnp.float32)],
        "part_gram",
    )(bits, *gathered)
    part = gram_kept + swap(gram_sent, "tensor", 1)

    sent, kept = kernel(
        raw_kernel,
        [shape(width // 2, rank)] * 2,
        [smem, anywhere] + [vmem] * (3 * square),
        [
            pltpu.VMEM((square * rows, width), jnp.float32),
            pltpu.VMEM((square * rows, rank), jnp.float32),
            pltpu.VMEM((width, rank), jnp.float32),
        ],
        "part_raw",
    )(bits, part, *gathered, *others, *columns)

    part = add_after(part, swap(part, "fsdp", square), kept)
    chips = [[i, i + 1] for i in range(0, lax.axis_size("fsdp"), 2)]
    quarter = lax.all_gather(part, "fsdp", axis=0, tiled=True, axis_index_groups=chips)
    over_planes = swap(quarter, "tensor", 2)
    shares = [quarter, swap(quarter, "tensor", 1), over_planes, swap(over_planes, "tensor", 1)]

    factors = []
    out, work = first_step(bits, shares, rank)
    factors.append(out)
    token = out
    for b in range(1, count):
        if b == (count + 1) // 2:
            own = add_after(kept, swap(sent, "fsdp", square), out)
            token = own
        out, work = later_step(b, work, token)
        factors.append(out)
    left, left_scaled, inverse, own_right = kernel(
        functools.partial(left_kernel, math.sqrt(total_rows)),
        [shape(rows, rank), shape(rows, rank), shape(rank, rank), shape(width // 2, rank)],
        [smem] + [vmem] * (3 + count),
        [pltpu.VMEM((rows, rank), jnp.float32)],
        "left",
    )(bits, mine, others[0], own, *factors)

    received = swap(own, "fsdp", square)
    beside = [swap(own, "fsdp", k) for k in (1, 2)]
    with_norms = kernel(
        norm_kernel, shape(width // 2 + 8, rank), [vmem] * 3 + [anywhere] * 2, [], "norms"
    )(own_right, received, inverse, *beside)
    received_rows = [with_norms] + [swap(with_norms, "fsdp", k) for k in range(1, square)]
    middle = width // 4
    diagonal = [swap(beside[1][:middle], "fsdp", 1), swap(beside[0][middle:], "fsdp", 2)]
    rights, own_splits, products = kernel(
        own_kernel,
        [
            shape(3 * (width // 2), rank),
            shape(3 * (width // 2), 3 * rank, dtype=jnp.bfloat16),
            shape(3, rows, width // 2),
        ],
        [vmem] * 5,
        [],
        "own_part",
        cost=2**24,
    )(left, inverse, own_right, *beside)
    last_right, last_split, last_product = kernel(
        diagonal_kernel,
        [
            shape(width // 2, rank),
            shape(width // 2, 3 * rank, dtype=jnp.bfloat16),
            shape(rows, width // 2),
        ],
        [vmem] * 4,
        [],
        "diagonal_part",
        cost=2**22,
    )(left, inverse, *diagonal)
    squares = kernel(
        functools.partial(squares_kernel, width // 2),
        shape(1, rank),
        [vmem] * square + [anywhere] * 2,
        [],
        "squares",
    )(*received_rows, products, last_product)
    squares = squares + swap(squares, "tensor", 1)
    squares = squares + swap(squares, "tensor", 2)

    new_momentum, splits = kernel(
        momentum_kernel,
        [shape(rows, cols), shape(cols // 2, 3 * rank, dtype=jnp.bfloat16)],
        [smem] + [vmem] * (3 + 2 * square),
        [pltpu.VMEM((square, rows, width), jnp.float32), pltpu.SemaphoreType.DMA((square,))],
        "new_momentum",
        cost=2**22,
        out_specs=[anywhere, vmem],
    )(bits, left, products, last_product, *pieces, *received_rows)
    update, next_basis = kernel(
        functools.partial(update_kernel, math.sqrt(total_rows / total_cols)),
        [shape(rows, cols, dtype=jnp.bfloat16), shape(cols // lax.axis_size("fsdp"), rank)],
        [smem] + [vmem] * (7 + square),
        [
            pltpu.VMEM((square, rows, width), jnp.bfloat16),
            pltpu.VMEM((width // 2, rank), jnp.float32),
            pltpu.SemaphoreType.DMA((square + 1,)),
        ],
        "update",
        out_specs=[anywhere, anywhere],
    )(bits, squares, left, rights, last_right, own_splits, last_split, splits, *received_rows)
    return (update, new_momentum, left_scaled, next_basis)


def on_device(momentum, gradient, right_basis):
    rows, cols = momentum.shape
    pairs = lax.axis_size("fsdp") == 2 * square and lax.axis_size("tensor") == 4
    aligned = rows % 16 == 0 and cols % (square * lanes) == 0 and right_basis.shape[1] % lanes == 0
    plan = in_squares if pairs and aligned else any_mesh
    return plan(momentum, gradient, right_basis)


def solution(mesh):
    in_specs = (P("fsdp", "tensor"), P("fsdp", "tensor"), P("tensor", None))
    out_specs = (
        P("fsdp", "tensor"),
        P("fsdp", "tensor"),
        P("fsdp", None),
        P(("tensor", "fsdp"), None),
    )
    return jax.shard_map(
        on_device, mesh=mesh, in_specs=in_specs, out_specs=out_specs, check_vma=False
    )
```

```python
import functools
import math

import jax
import jax.numpy as jnp
from jax import lax
from jax.experimental import pallas as pl
from jax.experimental.pallas import tpu as pltpu
from jax.sharding import PartitionSpec as P

epsilon = 1e-06
highest = lax.Precision.HIGHEST
lanes = 128
panel = 8
square = 4


def dot(a, b, contract=((1,), (0,))):
    return lax.dot_general(
        a, b, (contract, ((), ())), precision=highest, preferred_element_type=jnp.float32
    )


vmem = pl.BlockSpec(memory_space=pltpu.VMEM)
smem = pl.BlockSpec(memory_space=pltpu.SMEM)
anywhere = pl.BlockSpec(memory_space=pl.ANY)


def kernel(body, out_shape, in_specs, scratch, name, cost=0, out_specs=None, aliases=None):
    extra = {} if out_specs is None else {"out_specs": out_specs}
    return pl.pallas_call(
        body,
        out_shape=out_shape,
        input_output_aliases=aliases or {},
        **extra,
        in_specs=in_specs,
        scratch_shapes=scratch,
        compiler_params=pltpu.CompilerParams(vmem_limit_bytes=32 * 2**20),
        cost_estimate=pl.CostEstimate(flops=0, bytes_accessed=cost, transcendentals=0),
        name=name,
    )


def shape(*dims, dtype=jnp.float32):
    return jax.ShapeDtypeStruct(dims, dtype)


def split(value):
    high = value.astype(jnp.bfloat16)
    return high, (value - high.astype(jnp.float32)).astype(jnp.bfloat16)


def three_left(value):
    high, low = split(value)
    return jnp.concatenate([high, high, low], axis=1)


def three_right(value):
    high, low = split(value)
    return jnp.concatenate([high, low, high], axis=1)


def dot_three(a, b):
    return lax.dot_general(a, b, (((1,), (1,)), ((), ())), preferred_element_type=jnp.float32)


def factor_block(block):
    size = block.shape[0]
    lane = lax.broadcasted_iota(jnp.int32, (panel, size), 1)
    row = lax.broadcasted_iota(jnp.int32, (panel, size), 0)
    for first in range(0, size, panel):
        count = size - first
        now = block[first:, :]
        columns = [
            jnp.broadcast_to(now[:, first + k : first + k + 1], (count, size)) for k in range(panel)
        ]
        inside = (lane >= first) & (lane < first + panel)
        head = jnp.where(inside, jnp.where(lane - first == row, 1.0, 0.0), now[:panel])
        tail = None
        if count > panel:
            lane_below = lax.broadcasted_iota(jnp.int32, (count - panel, size), 1)
            inside_below = (lane_below >= first) & (lane_below < first + panel)
            tail = jnp.where(inside_below, 0.0, now[panel:])
        for j in range(panel):
            inverse = lax.rsqrt(columns[j][j : j + 1, :])
            multiplier = columns[j] * inverse
            for k in range(j + 1, panel):
                columns[k] = columns[k] - multiplier * (columns[k][j : j + 1, :] * inverse)
            pivot = head[j : j + 1, :] * inverse
            below = jnp.where(row > j, head - multiplier[:panel] * pivot, head)
            head = jnp.where(row == j, pivot, below)
            if tail is not None:
                tail = tail - multiplier[panel:] * pivot
        block[first : first + panel, :] = head
        if tail is not None:
            block[first + panel :, :] = tail


def place_gram(bits, shares, work):
    size = work.shape[0]
    count = size // lanes
    core, plane = bits[0], bits[1]
    stack = shares.pop()
    share = shares[0].shape[0]
    for flip_plane in range(2):
        for flip_core in range(2):
            at = pl.multiple_of(((plane ^ flip_plane) * 2 + (core ^ flip_core)) * share, 8)
            stack[pl.ds(at, share), :] = shares[flip_plane * 2 + flip_core][...]
    at = 0
    for j in range(count):
        for i in range(j, count):
            block = stack[at * lanes : (at + 1) * lanes, :]
            work[j * lanes : (j + 1) * lanes, i * lanes : (i + 1) * lanes] = block.T
            at += 1


def factor_step(b, work, out, block):
    size = work.shape[0]
    count = size // lanes
    row = lax.broadcasted_iota(jnp.int32, (lanes, lanes), 0)
    lower = row >= lax.broadcasted_iota(jnp.int32, (lanes, lanes), 1)
    rows = slice(b * lanes, (b + 1) * lanes)
    past = (b + 1) * lanes
    block[...] = work[rows, rows]
    factor_block(block)
    inverse = jnp.where(lower, block[...], 0.0)
    out[:, rows] = inverse
    if b:
        out[:, : b * lanes] = dot(inverse, work[rows, : b * lanes])
    if past < size:
        out[:, past:] = jnp.zeros((lanes, size - past), jnp.float32)
        upper = dot(inverse, work[rows, past:])
        own = out[:, :past]
        for i in range(b + 1, count):
            at = (i - b - 1) * lanes
            left = upper[:, at : at + lanes]
            below = slice(i * lanes, (i + 1) * lanes)
            work[below, i * lanes :] = work[below, i * lanes :] - dot(left, upper[:, at:], ((0,), (0,)))
            change = dot(left, own, ((0,), (0,)))
            if b:
                work[below, : b * lanes] = work[below, : b * lanes] - change[:, : b * lanes]
            work[below, b * lanes : past] = -change[:, b * lanes :]


def whole_kernel(gram, out, work, block):
    work[...] = gram[...]
    for b in range(work.shape[0] // lanes):
        factor_step(b, work, out.at[b * lanes : (b + 1) * lanes], block)


def inverse_factor(gram):
    size = gram.shape[0]
    return kernel(
        whole_kernel,
        jax.ShapeDtypeStruct((size, size), jnp.float32),
        [vmem],
        [pltpu.VMEM((size, size), jnp.float32), pltpu.VMEM((lanes, lanes), jnp.float32)],
        "inverse_factor",
    )(gram)


def first_kernel(bits, a, b, c, d, out, work, stack, block):
    place_gram(bits, [a, b, c, d, stack], work)
    factor_step(0, work, out, block)


def first_step(bits, shares, size):
    blocks = sum(x.shape[0] for x in shares)
    return kernel(
        first_kernel,
        [shape(lanes, size), shape(size, size)],
        [smem] + [vmem] * 4,
        [pltpu.VMEM((blocks, lanes), jnp.float32), pltpu.VMEM((lanes, lanes), jnp.float32)],
        "factor_first",
    )(bits, *shares)


def later_kernel(b, before, token, out, work, block):
    work[...] = before[...]
    factor_step(b, work, out, block)


def later_step(b, work, token):
    size = work.shape[0]
    return kernel(
        functools.partial(later_kernel, b),
        [shape(lanes, size), shape(size, size)],
        [vmem, anywhere],
        [pltpu.VMEM((lanes, lanes), jnp.float32)],
        "factor_later",
    )(work, token)


def share_norms(right_rows):
    squares = lax.psum(jnp.sum(right_rows * right_rows, axis=0), ("fsdp", "tensor"))
    return jnp.sqrt(squares + epsilon)


def any_mesh(momentum, gradient, right_basis):
    summed = momentum + gradient.astype(jnp.float32)
    left_raw = lax.psum(dot(summed, right_basis), "tensor")
    gram = lax.psum(dot(left_raw, left_raw, ((0,), (0,))), "fsdp")
    inverse = inverse_factor(gram)
    left = dot(left_raw, inverse, ((1,), (1,)))
    total_rows = left.shape[0] * lax.axis_size("fsdp")
    total_cols = summed.shape[1] * lax.axis_size("tensor")
    raw_rows = lax.psum_scatter(
        dot(summed, left_raw, ((0,), (0,))), "fsdp", scatter_dimension=0, tiled=True
    )
    right_rows = dot(raw_rows, inverse, ((1,), (1,)))
    column_norm = share_norms(right_rows)
    scaled_left = left * (math.sqrt(total_rows / total_cols) / column_norm)[None, :]
    raw = lax.all_gather(raw_rows, "fsdp", axis=0, tiled=True)
    product = dot(dot(left, inverse), raw, ((1,), (1,)))
    update = dot(dot(scaled_left, inverse), raw, ((1,), (1,))).astype(jnp.bfloat16)
    new_momentum = summed - 0.5 * product
    return (update, new_momentum, left * math.sqrt(total_rows), right_rows / column_norm[None, :])


def swap(value, axis, flip):
    return lax.ppermute(value, axis, [(i, i ^ flip) for i in range(lax.axis_size(axis))])


def split_kernel(bits, momentum, gradient, *pieces):
    width = pieces[0].shape[1]
    for k, piece in enumerate(pieces):
        at = pl.ds(pl.multiple_of((bits[2] ^ k) * width, lanes), width)
        piece[...] = momentum[:, at] + gradient[:, at].astype(jnp.float32)


def part_left_kernel(bits, basis, momentum, gradient, token, sent, kept, total):
    half = sent.shape[0]
    total[...] = dot(momentum[...] + gradient[...].astype(jnp.float32), basis[...])
    sent[...] = total[pl.ds(pl.multiple_of((1 - bits[0]) * half, 8), half), :]
    kept[...] = total[pl.ds(pl.multiple_of(bits[0] * half, 8), half), :]


def core_add_kernel(bits, kept, both, out):
    half = kept.shape[0]
    out[...] = kept[...] + both[pl.ds(pl.multiple_of((1 - bits[0]) * half, 8), half), :]


def add_kernel(*refs):
    refs[-1][...] = refs[0][...] + refs[1][...]


def add_after(a, b, *tokens):
    return kernel(
        add_kernel, shape(*a.shape), [vmem] * 2 + [anywhere] * len(tokens), [], "add_after"
    )(a, b, *tokens)


def gram_kernel(bits, *refs):
    parts, (sent, kept, rows, stack) = refs[:square], refs[square:]
    half, rank = parts[0].shape
    share = sent.shape[0]
    for k, part in enumerate(parts):
        rows[k * half : (k + 1) * half, :] = part[...]
    at = 0
    for first in range(0, rank, 2 * lanes):
        last = min(first + 2 * lanes, rank)
        product = dot(rows[:, first:], rows[:, first:last], ((0,), (0,)))
        for j in range(0, last - first, lanes):
            stack[at : at + rank - first - j, :] = product[j:, j : j + lanes]
            at += rank - first - j
    for out, core in ((kept, bits[0]), (sent, 1 - bits[0])):
        index = (2 * bits[1] + core) * 2 + bits[2] % 2
        out[...] = stack[pl.ds(pl.multiple_of(index * share, 8), share), :]


def raw_kernel(bits, token, *refs):
    mine, others, columns = refs[:square], refs[square : 2 * square], refs[2 * square : 3 * square]
    sent, kept, left, right, raw = refs[3 * square :]
    rows = columns[0].shape[0]
    half = rows // 2
    for k in range(square):
        left[k * rows : (k + 1) * rows, :] = columns[k][...]
        right[pl.ds(pl.multiple_of(k * rows + bits[0] * half, 8), half), :] = mine[k][...]
        right[pl.ds(pl.multiple_of(k * rows + (1 - bits[0]) * half, 8), half), :] = others[k][...]
    raw[...] = dot(left[...], right[...], ((0,), (0,)))
    count = kept.shape[0]
    kept[...] = raw[pl.ds(pl.multiple_of(bits[4] * count, 8), count), :]
    sent[...] = raw[pl.ds(pl.multiple_of((1 - bits[4]) * count, 8), count), :]


def left_kernel(scale, bits, mine, other, own, *refs):
    inverses, (left, left_scaled, inverse, own_right, rows) = refs[:-5], refs[-5:]
    half = mine.shape[0]
    for b, part in enumerate(inverses):
        inverse[b * lanes : (b + 1) * lanes, :] = part[...]
    rows[pl.ds(pl.multiple_of(bits[0] * half, 8), half), :] = mine[...]
    rows[pl.ds(pl.multiple_of((1 - bits[0]) * half, 8), half), :] = other[...]
    left[...] = dot(rows[...], inverse[...], ((1,), (1,)))
    left_scaled[...] = left[...] * scale
    own_right[...] = dot(own[...], inverse[...], ((1,), (1,)))


def norm_kernel(own_right, received, inverse, one, two, out, squares):
    right = dot(received[...], inverse[...], ((1,), (1,)))
    out[...] = right
    total = jnp.sum(right * right, axis=0, keepdims=True)
    squares[...] = total + jnp.sum(own_right[...] * own_right[...], axis=0, keepdims=True)


def with_row(rows, squares, out):
    count = rows.shape[0]
    out[:count, :] = rows[...]
    row = lax.broadcasted_iota(jnp.int32, (8, rows.shape[1]), 0)
    out[count:, :] = jnp.where(row == 0, squares[...], 0.0)


def pack_kernel(rows, squares, out):
    with_row(rows, squares, out)


def own_kernel(left, inverse, own_right, one, two, rights, splits, products):
    count = own_right.shape[0]
    rights[:count, :] = own_right[...]
    for k, part in enumerate((one, two)):
        at = slice((k + 1) * count, (k + 2) * count)
        rights[at, :] = dot(part[...], inverse[...], ((1,), (1,)))
    splits[...] = three_right(rights[...])
    product = dot_three(three_left(left[...]), splits[...])
    for k in range(3):
        products[k] = product[:, k * count : (k + 1) * count]


def columns_of(bits, k, width):
    return pl.ds(pl.multiple_of((bits[2] ^ k) * width, lanes), width)


def in_order(bits, mine, other):
    lower = jnp.concatenate([mine, other], axis=1)
    return jnp.where(bits[4] == 0, lower, jnp.concatenate([other, mine], axis=1))


def momentum_kernel(bits, left, rights, squares, products, *refs):
    pieces, received, (new_momentum, splits, first, second, ready, sent) = refs[:3], refs[3:6], refs[6:]
    width = pieces[0].shape[1]
    half = width // 2
    middle = half // 2
    with_row(rights.at[2 * half : 2 * half + middle], squares, first)
    with_row(rights.at[half + middle : 2 * half], squares, second)
    for k in range(3):
        splits[k * half : (k + 1) * half, :] = three_right(received[k][...])
    both = dot_three(three_left(left[...]), splits[...])
    copies = []
    for k in range(3):
        other = both[:, k * half : (k + 1) * half]
        ready[k] = pieces[k][...] - 0.5 * in_order(bits, products[k], other)
        target = new_momentum.at[:, columns_of(bits, k, width)]
        copies.append(pltpu.make_async_copy(ready.at[k], target, sent.at[k]))
        copies[k].start()
    for copy in copies:
        copy.wait()


def last_kernel(factor, bits, squares, left, rights, own_splits, splits, *refs):
    received, (first, second, piece, _, new_momentum, update, next_basis), scratch = (
        refs[:square],
        refs[square : square + 7],
        refs[square + 7 :],
    )
    last_right, last_splits, ready, scaled_ready, basis_ready, sent = scratch
    half, width = basis_ready.shape[0], piece.shape[1]
    middle = half // 2
    total = squares[...] + received[square - 1][half : half + 1, :]
    total = total + first[middle : middle + 1, :] + second[middle : middle + 1, :]
    norm = jnp.sqrt(total + epsilon)
    copies = []

    def send(source, target, index):
        copies.append(pltpu.make_async_copy(source, target, sent.at[index]))
        copies[-1].start()

    last_right[:middle, :] = first[:middle, :]
    last_right[middle:, :] = second[:middle, :]
    last_splits[:half, :] = three_right(last_right[...])
    last_splits[half:, :] = three_right(received[square - 1][:half, :])
    both = dot_three(three_left(left[...]), last_splits[...])
    ready[...] = piece[...] - 0.5 * in_order(bits, both[:, :half], both[:, half:])
    send(ready, new_momentum.at[:, columns_of(bits, square - 1, width)], square)
    for k in range(square):

        @pl.when((bits[3] // 2) ^ bits[2] == k)
        def _():
            mine = rights[k * half : (k + 1) * half, :] if k < square - 1 else last_right[...]
            mine = jnp.where(bits[3] % 2 == bits[4], mine, received[k][:half, :])
            basis_ready[...] = mine / norm

    send(basis_ready, next_basis, square + 1)
    scaled = three_left(left[...] * (factor / norm))
    for k in range(square):
        if k < square - 1:
            parts = slice(k * half, (k + 1) * half)
            mine = dot_three(scaled, own_splits[parts, :])
            other = dot_three(scaled, splits[parts, :])
        else:
            both = dot_three(scaled, last_splits[...])
            mine, other = both[:, :half], both[:, half:]
        scaled_ready[k] = in_order(bits, mine, other).astype(jnp.bfloat16)
        send(scaled_ready.at[k], update.at[:, columns_of(bits, k, width)], k)
    for copy in copies:
        copy.wait()


def in_squares(momentum, gradient, right_basis):
    device = lax.axis_index("fsdp")
    tensor = lax.axis_index("tensor")
    bits = jnp.stack([tensor % 2, tensor // 2, device % square, device, device // square])
    bits = bits.astype(jnp.int32)
    rows, cols = momentum.shape
    rank = right_basis.shape[1]
    half, width = rows // 2, cols // square
    total_rows = rows * lax.axis_size("fsdp")
    total_cols = cols * lax.axis_size("tensor")

    pieces = kernel(split_kernel, [shape(rows, width)] * square, [smem, vmem, vmem], [], "split_sum")(
        bits, momentum, gradient
    )
    columns = [pieces[0]] + [swap(pieces[k], "fsdp", k) for k in range(1, square)]

    sent, kept = kernel(
        part_left_kernel,
        [shape(half, rank)] * 2,
        [smem] + [vmem] * 3 + [anywhere],
        [pltpu.VMEM((rows, rank), jnp.float32)],
        "part_left",
    )(bits, right_basis, momentum, gradient, pieces[0])
    cores = [[i, i + 1] for i in range(0, lax.axis_size("tensor"), 2)]
    both = lax.all_gather(sent, "tensor", axis=0, tiled=True, axis_index_groups=cores)
    mine = kernel(core_add_kernel, shape(half, rank), [smem, vmem, vmem], [], "core_add")(
        bits, kept, both
    )
    mine = add_after(mine, swap(mine, "tensor", 2), *columns[1:])
    gathered = [mine] + [swap(mine, "fsdp", k) for k in range(1, square)]
    others = [swap(part, "tensor", 1) for part in gathered]

    count = rank // lanes
    stacked = count * (count + 1) // 2 * lanes
    share = stacked // 8
    gram_sent, gram_kept = kernel(
        gram_kernel,
        [shape(share, lanes)] * 2,
        [smem] + [vmem] * square,
        [pltpu.VMEM((square * half, rank), jnp.float32), pltpu.VMEM((stacked, lanes), jnp.float32)],
        "part_gram",
    )(bits, *gathered)
    part = gram_kept + swap(gram_sent, "tensor", 1)

    sent, kept = kernel(
        raw_kernel,
        [shape(width // 2, rank)] * 2,
        [smem, anywhere] + [vmem] * (3 * square),
        [
            pltpu.VMEM((square * rows, width), jnp.float32),
            pltpu.VMEM((square * rows, rank), jnp.float32),
            pltpu.VMEM((width, rank), jnp.float32),
        ],
        "part_raw",
    )(bits, part, *gathered, *others, *columns)

    part = add_after(part, swap(part, "fsdp", square), kept)
    chips = [[i, i + 1] for i in range(0, lax.axis_size("fsdp"), 2)]
    quarter = lax.all_gather(part, "fsdp", axis=0, tiled=True, axis_index_groups=chips)
    over_planes = swap(quarter, "tensor", 2)
    shares = [quarter, swap(quarter, "tensor", 1), over_planes, swap(over_planes, "tensor", 1)]

    factors = []
    out, work = first_step(bits, shares, rank)
    factors.append(out)
    token = out
    for b in range(1, count):
        if b == 1:
            own = add_after(kept, swap(sent, "fsdp", square), out)
            token = own
        out, work = later_step(b, work, token)
        factors.append(out)
    left, left_scaled, inverse, own_right = kernel(
        functools.partial(left_kernel, math.sqrt(total_rows)),
        [shape(rows, rank), shape(rows, rank), shape(rank, rank), shape(width // 2, rank)],
        [smem] + [vmem] * (3 + count),
        [pltpu.VMEM((rows, rank), jnp.float32)],
        "left",
    )(bits, mine, others[0], own, *factors)

    received = swap(own, "fsdp", square)
    beside = [swap(own, "fsdp", k) for k in (1, 2)]
    half_width = width // 2
    received_right, squares = kernel(
        norm_kernel,
        [shape(half_width, rank), shape(1, rank)],
        [vmem] * 3 + [anywhere] * 2,
        [],
        "norms",
    )(own_right, received, inverse, *beside)
    for flip in (1, 2):
        squares = squares + swap(squares, "tensor", flip)
    packed = kernel(pack_kernel, shape(half_width + 8, rank), [vmem] * 2, [], "pack")(
        received_right, squares
    )
    received_rows = [received_right] + [swap(received_right, "fsdp", k) for k in (1, 2)]
    received_rows += [swap(packed, "fsdp", 3)]

    rights, own_splits, products = kernel(
        own_kernel,
        [
            shape(3 * half_width, rank),
            shape(3 * half_width, 3 * rank, dtype=jnp.bfloat16),
            shape(3, rows, half_width),
        ],
        [vmem] * 5,
        [],
        "own_part",
        cost=2**24,
    )(left, inverse, own_right, *beside)

    new_momentum, splits, first, second = kernel(
        momentum_kernel,
        [
            shape(rows, cols),
            shape(3 * half_width, 3 * rank, dtype=jnp.bfloat16),
            shape(half_width // 2 + 8, rank),
            shape(half_width // 2 + 8, rank),
        ],
        [smem] + [vmem] * 10,
        [pltpu.VMEM((3, rows, width), jnp.float32), pltpu.SemaphoreType.DMA((3,))],
        "new_momentum",
        cost=2**24,
        out_specs=[anywhere] + [vmem] * 3,
    )(bits, left, rights, squares, products, *pieces[:3], *received_rows[:3])
    first, second = swap(first, "fsdp", 1), swap(second, "fsdp", 2)
    new_momentum, update, next_basis = kernel(
        functools.partial(last_kernel, math.sqrt(total_rows / total_cols)),
        [
            shape(rows, cols),
            shape(rows, cols, dtype=jnp.bfloat16),
            shape(cols // lax.axis_size("fsdp"), rank),
        ],
        [smem] + [vmem] * (8 + square) + [anywhere],
        [
            pltpu.VMEM((half_width, rank), jnp.float32),
            pltpu.VMEM((2 * half_width, 3 * rank), jnp.bfloat16),
            pltpu.VMEM((rows, width), jnp.float32),
            pltpu.VMEM((square, rows, width), jnp.bfloat16),
            pltpu.VMEM((half_width, rank), jnp.float32),
            pltpu.SemaphoreType.DMA((square + 2,)),
        ],
        "last",
        out_specs=[anywhere] * 3,
        aliases={9 + square: 0},
    )(
        *(bits, squares, left, rights, own_splits, splits, *received_rows),
        *(first, second, pieces[3], new_momentum),
    )
    return (update, new_momentum, left_scaled, next_basis)


def on_device(momentum, gradient, right_basis):
    rows, cols = momentum.shape
    pairs = lax.axis_size("fsdp") == 2 * square and lax.axis_size("tensor") == 4
    aligned = rows % 16 == 0 and cols % (square * lanes) == 0 and right_basis.shape[1] % lanes == 0
    plan = in_squares if pairs and aligned else any_mesh
    return plan(momentum, gradient, right_basis)


def solution(mesh):
    in_specs = (P("fsdp", "tensor"), P("fsdp", "tensor"), P("tensor", None))
    out_specs = (
        P("fsdp", "tensor"),
        P("fsdp", "tensor"),
        P("fsdp", None),
        P(("tensor", "fsdp"), None),
    )
    return jax.shard_map(
        on_device, mesh=mesh, in_specs=in_specs, out_specs=out_specs, check_vma=False
    )
```

```python
import functools
import math

import jax
import jax.numpy as jnp
from jax import lax
from jax.experimental import pallas as pl
from jax.experimental.pallas import tpu as pltpu
from jax.sharding import PartitionSpec as P

epsilon = 1e-06
highest = lax.Precision.HIGHEST
lanes = 128
panel = 8
square = 4


def dot(a, b, contract=((1,), (0,))):
    return lax.dot_general(
        a, b, (contract, ((), ())), precision=highest, preferred_element_type=jnp.float32
    )


vmem = pl.BlockSpec(memory_space=pltpu.VMEM)
smem = pl.BlockSpec(memory_space=pltpu.SMEM)
anywhere = pl.BlockSpec(memory_space=pl.ANY)


def kernel(body, out_shape, in_specs, scratch, name, cost=0, out_specs=None, aliases=None):
    extra = {} if out_specs is None else {"out_specs": out_specs}
    return pl.pallas_call(
        body,
        out_shape=out_shape,
        input_output_aliases=aliases or {},
        **extra,
        in_specs=in_specs,
        scratch_shapes=scratch,
        compiler_params=pltpu.CompilerParams(vmem_limit_bytes=32 * 2**20),
        cost_estimate=pl.CostEstimate(flops=0, bytes_accessed=cost, transcendentals=0),
        name=name,
    )


def shape(*dims, dtype=jnp.float32):
    return jax.ShapeDtypeStruct(dims, dtype)


def split(value):
    high = value.astype(jnp.bfloat16)
    return high, (value - high.astype(jnp.float32)).astype(jnp.bfloat16)


def three_left(value):
    high, low = split(value)
    return jnp.concatenate([high, high, low], axis=1)


def three_right(value):
    high, low = split(value)
    return jnp.concatenate([high, low, high], axis=1)


def dot_three(a, b):
    return lax.dot_general(a, b, (((1,), (1,)), ((), ())), preferred_element_type=jnp.float32)


def factor_block(block):
    size = block.shape[0]
    lane = lax.broadcasted_iota(jnp.int32, (panel, size), 1)
    row = lax.broadcasted_iota(jnp.int32, (panel, size), 0)
    for first in range(0, size, panel):
        count = size - first
        now = block[first:, :]
        columns = [
            jnp.broadcast_to(now[:, first + k : first + k + 1], (count, size)) for k in range(panel)
        ]
        inside = (lane >= first) & (lane < first + panel)
        head = jnp.where(inside, jnp.where(lane - first == row, 1.0, 0.0), now[:panel])
        tail = None
        if count > panel:
            lane_below = lax.broadcasted_iota(jnp.int32, (count - panel, size), 1)
            inside_below = (lane_below >= first) & (lane_below < first + panel)
            tail = jnp.where(inside_below, 0.0, now[panel:])
        for j in range(panel):
            inverse = lax.rsqrt(columns[j][j : j + 1, :])
            multiplier = columns[j] * inverse
            for k in range(j + 1, panel):
                columns[k] = columns[k] - multiplier * (columns[k][j : j + 1, :] * inverse)
            pivot = head[j : j + 1, :] * inverse
            below = jnp.where(row > j, head - multiplier[:panel] * pivot, head)
            head = jnp.where(row == j, pivot, below)
            if tail is not None:
                tail = tail - multiplier[panel:] * pivot
        block[first : first + panel, :] = head
        if tail is not None:
            block[first + panel :, :] = tail


def place_gram(bits, shares, work):
    size = work.shape[0]
    count = size // lanes
    core, plane = bits[0], bits[1]
    stack = shares.pop()
    share = shares[0].shape[0]
    for flip_plane in range(2):
        for flip_core in range(2):
            at = pl.multiple_of(((plane ^ flip_plane) * 2 + (core ^ flip_core)) * share, 8)
            stack[pl.ds(at, share), :] = shares[flip_plane * 2 + flip_core][...]
    at = 0
    for j in range(count):
        for i in range(j, count):
            block = stack[at * lanes : (at + 1) * lanes, :]
            work[j * lanes : (j + 1) * lanes, i * lanes : (i + 1) * lanes] = block.T
            at += 1


def factor_step(b, work, out, block):
    size = work.shape[0]
    count = size // lanes
    row = lax.broadcasted_iota(jnp.int32, (lanes, lanes), 0)
    lower = row >= lax.broadcasted_iota(jnp.int32, (lanes, lanes), 1)
    rows = slice(b * lanes, (b + 1) * lanes)
    past = (b + 1) * lanes
    block[...] = work[rows, rows]
    factor_block(block)
    inverse = jnp.where(lower, block[...], 0.0)
    out[:, rows] = inverse
    if b:
        out[:, : b * lanes] = dot(inverse, work[rows, : b * lanes])
    if past < size:
        out[:, past:] = jnp.zeros((lanes, size - past), jnp.float32)
        upper = dot(inverse, work[rows, past:])
        own = out[:, :past]
        for i in range(b + 1, count):
            at = (i - b - 1) * lanes
            left = upper[:, at : at + lanes]
            below = slice(i * lanes, (i + 1) * lanes)
            work[below, i * lanes :] = work[below, i * lanes :] - dot(left, upper[:, at:], ((0,), (0,)))
            change = dot(left, own, ((0,), (0,)))
            if b:
                work[below, : b * lanes] = work[below, : b * lanes] - change[:, : b * lanes]
            work[below, b * lanes : past] = -change[:, b * lanes :]


def whole_kernel(gram, out, work, block):
    work[...] = gram[...]
    for b in range(work.shape[0] // lanes):
        factor_step(b, work, out.at[b * lanes : (b + 1) * lanes], block)


def inverse_factor(gram):
    size = gram.shape[0]
    return kernel(
        whole_kernel,
        jax.ShapeDtypeStruct((size, size), jnp.float32),
        [vmem],
        [pltpu.VMEM((size, size), jnp.float32), pltpu.VMEM((lanes, lanes), jnp.float32)],
        "inverse_factor",
    )(gram)


def first_kernel(bits, a, b, c, d, out, work, stack, block):
    place_gram(bits, [a, b, c, d, stack], work)
    factor_step(0, work, out, block)


def first_step(bits, shares, size):
    blocks = sum(x.shape[0] for x in shares)
    return kernel(
        first_kernel,
        [shape(lanes, size), shape(size, size)],
        [smem] + [vmem] * 4,
        [pltpu.VMEM((blocks, lanes), jnp.float32), pltpu.VMEM((lanes, lanes), jnp.float32)],
        "factor_first",
    )(bits, *shares)


def later_kernel(b, before, token, out, work, block):
    work[...] = before[...]
    factor_step(b, work, out, block)


def later_step(b, work, token):
    size = work.shape[0]
    return kernel(
        functools.partial(later_kernel, b),
        [shape(lanes, size), shape(size, size)],
        [vmem, anywhere],
        [pltpu.VMEM((lanes, lanes), jnp.float32)],
        "factor_later",
    )(work, token)


def share_norms(right_rows):
    squares = lax.psum(jnp.sum(right_rows * right_rows, axis=0), ("fsdp", "tensor"))
    return jnp.sqrt(squares + epsilon)


def any_mesh(momentum, gradient, right_basis):
    summed = momentum + gradient.astype(jnp.float32)
    left_raw = lax.psum(dot(summed, right_basis), "tensor")
    gram = lax.psum(dot(left_raw, left_raw, ((0,), (0,))), "fsdp")
    inverse = inverse_factor(gram)
    left = dot(left_raw, inverse, ((1,), (1,)))
    total_rows = left.shape[0] * lax.axis_size("fsdp")
    total_cols = summed.shape[1] * lax.axis_size("tensor")
    raw_rows = lax.psum_scatter(
        dot(summed, left_raw, ((0,), (0,))), "fsdp", scatter_dimension=0, tiled=True
    )
    right_rows = dot(raw_rows, inverse, ((1,), (1,)))
    column_norm = share_norms(right_rows)
    scaled_left = left * (math.sqrt(total_rows / total_cols) / column_norm)[None, :]
    raw = lax.all_gather(raw_rows, "fsdp", axis=0, tiled=True)
    product = dot(dot(left, inverse), raw, ((1,), (1,)))
    update = dot(dot(scaled_left, inverse), raw, ((1,), (1,))).astype(jnp.bfloat16)
    new_momentum = summed - 0.5 * product
    return (update, new_momentum, left * math.sqrt(total_rows), right_rows / column_norm[None, :])


def swap(value, axis, flip):
    return lax.ppermute(value, axis, [(i, i ^ flip) for i in range(lax.axis_size(axis))])


def split_kernel(bits, momentum, gradient, *pieces):
    width = pieces[0].shape[1]
    for k, piece in enumerate(pieces):
        at = pl.ds(pl.multiple_of((bits[2] ^ k) * width, lanes), width)
        piece[...] = momentum[:, at] + gradient[:, at].astype(jnp.float32)


def part_left_kernel(bits, basis, momentum, gradient, token, sent, kept, total):
    half = sent.shape[0]
    total[...] = dot(momentum[...] + gradient[...].astype(jnp.float32), basis[...])
    sent[...] = total[pl.ds(pl.multiple_of((1 - bits[0]) * half, 8), half), :]
    kept[...] = total[pl.ds(pl.multiple_of(bits[0] * half, 8), half), :]


def core_add_kernel(bits, kept, both, out):
    half = kept.shape[0]
    out[...] = kept[...] + both[pl.ds(pl.multiple_of((1 - bits[0]) * half, 8), half), :]


def add_kernel(*refs):
    refs[-1][...] = refs[0][...] + refs[1][...]


def add_after(a, b, *tokens):
    return kernel(
        add_kernel, shape(*a.shape), [vmem] * 2 + [anywhere] * len(tokens), [], "add_after"
    )(a, b, *tokens)


def gram_kernel(bits, *refs):
    parts, (sent, kept, rows, stack) = refs[:square], refs[square:]
    half, rank = parts[0].shape
    share = sent.shape[0]
    for k, part in enumerate(parts):
        rows[k * half : (k + 1) * half, :] = part[...]
    at = 0
    for first in range(0, rank, 2 * lanes):
        last = min(first + 2 * lanes, rank)
        product = dot(rows[:, first:], rows[:, first:last], ((0,), (0,)))
        for j in range(0, last - first, lanes):
            stack[at : at + rank - first - j, :] = product[j:, j : j + lanes]
            at += rank - first - j
    for out, core in ((kept, bits[0]), (sent, 1 - bits[0])):
        index = (2 * bits[1] + core) * 2 + bits[2] % 2
        out[...] = stack[pl.ds(pl.multiple_of(index * share, 8), share), :]


def raw_kernel(bits, token, *refs):
    mine, others, columns = refs[:square], refs[square : 2 * square], refs[2 * square : 3 * square]
    sent, kept, left, right, raw = refs[3 * square :]
    rows = columns[0].shape[0]
    half = rows // 2
    for k in range(square):
        left[k * rows : (k + 1) * rows, :] = columns[k][...]
        right[pl.ds(pl.multiple_of(k * rows + bits[0] * half, 8), half), :] = mine[k][...]
        right[pl.ds(pl.multiple_of(k * rows + (1 - bits[0]) * half, 8), half), :] = others[k][...]
    raw[...] = dot(left[...], right[...], ((0,), (0,)))
    count = kept.shape[0]
    kept[...] = raw[pl.ds(pl.multiple_of(bits[4] * count, 8), count), :]
    sent[...] = raw[pl.ds(pl.multiple_of((1 - bits[4]) * count, 8), count), :]


def left_kernel(scale, bits, mine, other, own, *refs):
    inverses, (left, left_scaled, inverse, own_right, rows) = refs[:-5], refs[-5:]
    half = mine.shape[0]
    for b, part in enumerate(inverses):
        inverse[b * lanes : (b + 1) * lanes, :] = part[...]
    rows[pl.ds(pl.multiple_of(bits[0] * half, 8), half), :] = mine[...]
    rows[pl.ds(pl.multiple_of((1 - bits[0]) * half, 8), half), :] = other[...]
    left[...] = dot(rows[...], inverse[...], ((1,), (1,)))
    left_scaled[...] = left[...] * scale
    own_right[...] = dot(own[...], inverse[...], ((1,), (1,)))


def norm_kernel(own_right, received, inverse, one, two, out, squares):
    right = dot(received[...], inverse[...], ((1,), (1,)))
    out[...] = right
    total = jnp.sum(right * right, axis=0, keepdims=True)
    squares[...] = total + jnp.sum(own_right[...] * own_right[...], axis=0, keepdims=True)


def forward_kernel(one, two, squares, one_here, two_here, first, second):
    middle = second.shape[0]
    first[:middle, :] = two[:middle, :]
    row = lax.broadcasted_iota(jnp.int32, (8, two.shape[1]), 0)
    first[middle:, :] = jnp.where(row == 0, squares[...], 0.0)
    second[...] = one[middle:, :]


def own_kernel(left, inverse, own_right, one, two, rights, first, second, splits, products):
    count = own_right.shape[0]
    middle = count // 2
    rights[:count, :] = own_right[...]
    for k, part in enumerate((one, two)):
        at = slice((k + 1) * count, (k + 2) * count)
        rights[at, :] = dot(part[...], inverse[...], ((1,), (1,)))
    first[...] = rights[2 * count : 2 * count + middle, :]
    second[...] = rights[count + middle : 2 * count, :]
    splits[...] = three_right(rights[...])
    product = dot_three(three_left(left[...]), splits[...])
    for k in range(3):
        products[k] = product[:, k * count : (k + 1) * count]


def columns_of(bits, k, width):
    return pl.ds(pl.multiple_of((bits[2] ^ k) * width, lanes), width)


def in_order(bits, mine, other):
    lower = jnp.concatenate([mine, other], axis=1)
    return jnp.where(bits[4] == 0, lower, jnp.concatenate([other, mine], axis=1))


def momentum_kernel(bits, left, products, *refs):
    pieces, received, (new_momentum, splits, ready, sent) = refs[:3], refs[3:6], refs[6:]
    width = pieces[0].shape[1]
    half = width // 2
    for k in range(3):
        splits[k * half : (k + 1) * half, :] = three_right(received[k][...])
    both = dot_three(three_left(left[...]), splits[...])
    copies = []
    for k in range(3):
        other = both[:, k * half : (k + 1) * half]
        ready[k] = pieces[k][...] - 0.5 * in_order(bits, products[k], other)
        target = new_momentum.at[:, columns_of(bits, k, width)]
        copies.append(pltpu.make_async_copy(ready.at[k], target, sent.at[k]))
        copies[k].start()
    for copy in copies:
        copy.wait()


def last_kernel(factor, bits, squares, left, rights, own_splits, splits, *refs):
    received, (own_first, own_second, first, second, piece, _, new_momentum, update, next_basis), scratch = (
        refs[:3],
        refs[3:12],
        refs[12:],
    )
    last_own, last_received, last_splits, ready, scaled_ready, basis_ready, sent = scratch
    half, width = basis_ready.shape[0], piece.shape[1]
    middle = half // 2
    norm = jnp.sqrt(squares[...] + first[middle : middle + 1, :] + epsilon)
    copies = []

    def send(source, target, index):
        copies.append(pltpu.make_async_copy(source, target, sent.at[index]))
        copies[-1].start()

    last_own[:middle, :] = own_first[...]
    last_own[middle:, :] = own_second[...]
    last_received[:middle, :] = first[:middle, :]
    last_received[middle:, :] = second[...]
    last_splits[:half, :] = three_right(last_own[...])
    last_splits[half:, :] = three_right(last_received[...])
    both = dot_three(three_left(left[...]), last_splits[...])
    ready[...] = piece[...] - 0.5 * in_order(bits, both[:, :half], both[:, half:])
    send(ready, new_momentum.at[:, columns_of(bits, square - 1, width)], square)
    for k in range(square):

        @pl.when((bits[3] // 2) ^ bits[2] == k)
        def _():
            last = k == square - 1
            mine = last_own[...] if last else rights[k * half : (k + 1) * half, :]
            other = last_received[...] if last else received[k][...]
            basis_ready[...] = jnp.where(bits[3] % 2 == bits[4], mine, other) / norm

    send(basis_ready, next_basis, square + 1)
    scaled = three_left(left[...] * (factor / norm))
    for k in range(square):
        if k < square - 1:
            parts = slice(k * half, (k + 1) * half)
            mine = dot_three(scaled, own_splits[parts, :])
            other = dot_three(scaled, splits[parts, :])
        else:
            both = dot_three(scaled, last_splits[...])
            mine, other = both[:, :half], both[:, half:]
        scaled_ready[k] = in_order(bits, mine, other).astype(jnp.bfloat16)
        send(scaled_ready.at[k], update.at[:, columns_of(bits, k, width)], k)
    for copy in copies:
        copy.wait()


def in_squares(momentum, gradient, right_basis):
    device = lax.axis_index("fsdp")
    tensor = lax.axis_index("tensor")
    bits = jnp.stack([tensor % 2, tensor // 2, device % square, device, device // square])
    bits = bits.astype(jnp.int32)
    rows, cols = momentum.shape
    rank = right_basis.shape[1]
    half, width = rows // 2, cols // square
    total_rows = rows * lax.axis_size("fsdp")
    total_cols = cols * lax.axis_size("tensor")

    pieces = kernel(split_kernel, [shape(rows, width)] * square, [smem, vmem, vmem], [], "split_sum")(
        bits, momentum, gradient
    )
    columns = [pieces[0]] + [swap(pieces[k], "fsdp", k) for k in range(1, square)]

    sent, kept = kernel(
        part_left_kernel,
        [shape(half, rank)] * 2,
        [smem] + [vmem] * 3 + [anywhere],
        [pltpu.VMEM((rows, rank), jnp.float32)],
        "part_left",
    )(bits, right_basis, momentum, gradient, pieces[0])
    cores = [[i, i + 1] for i in range(0, lax.axis_size("tensor"), 2)]
    both = lax.all_gather(sent, "tensor", axis=0, tiled=True, axis_index_groups=cores)
    mine = kernel(core_add_kernel, shape(half, rank), [smem, vmem, vmem], [], "core_add")(
        bits, kept, both
    )
    mine = add_after(mine, swap(mine, "tensor", 2), *columns[1:])
    gathered = [mine] + [swap(mine, "fsdp", k) for k in range(1, square)]
    others = [swap(part, "tensor", 1) for part in gathered]

    count = rank // lanes
    stacked = count * (count + 1) // 2 * lanes
    share = stacked // 8
    gram_sent, gram_kept = kernel(
        gram_kernel,
        [shape(share, lanes)] * 2,
        [smem] + [vmem] * square,
        [pltpu.VMEM((square * half, rank), jnp.float32), pltpu.VMEM((stacked, lanes), jnp.float32)],
        "part_gram",
    )(bits, *gathered)
    part = gram_kept + swap(gram_sent, "tensor", 1)

    sent, kept = kernel(
        raw_kernel,
        [shape(width // 2, rank)] * 2,
        [smem, anywhere] + [vmem] * (3 * square),
        [
            pltpu.VMEM((square * rows, width), jnp.float32),
            pltpu.VMEM((square * rows, rank), jnp.float32),
            pltpu.VMEM((width, rank), jnp.float32),
        ],
        "part_raw",
    )(bits, part, *gathered, *others, *columns)

    part = add_after(part, swap(part, "fsdp", square), kept)
    chips = [[i, i + 1] for i in range(0, lax.axis_size("fsdp"), 2)]
    quarter = lax.all_gather(part, "fsdp", axis=0, tiled=True, axis_index_groups=chips)
    over_planes = swap(quarter, "tensor", 2)
    shares = [quarter, swap(quarter, "tensor", 1), over_planes, swap(over_planes, "tensor", 1)]

    factors = []
    out, work = first_step(bits, shares, rank)
    factors.append(out)
    token = out
    for b in range(1, count):
        if b == 1:
            own = add_after(kept, swap(sent, "fsdp", square), out)
            token = own
        out, work = later_step(b, work, token)
        factors.append(out)
    left, left_scaled, inverse, own_right = kernel(
        functools.partial(left_kernel, math.sqrt(total_rows)),
        [shape(rows, rank), shape(rows, rank), shape(rank, rank), shape(width // 2, rank)],
        [smem] + [vmem] * (3 + count),
        [pltpu.VMEM((rows, rank), jnp.float32)],
        "left",
    )(bits, mine, others[0], own, *factors)

    received = swap(own, "fsdp", square)
    beside = [swap(own, "fsdp", k) for k in (1, 2)]
    half_width = width // 2
    received_right, squares = kernel(
        norm_kernel,
        [shape(half_width, rank), shape(1, rank)],
        [vmem] * 3 + [anywhere] * 2,
        [],
        "norms",
    )(own_right, received, inverse, *beside)
    received_rows = [received_right] + [swap(received_right, "fsdp", k) for k in (1, 2)]
    for axis, flip in (("tensor", 1), ("tensor", 2), ("fsdp", 2)):
        squares = squares + swap(squares, axis, flip)

    half_rows = shape(half_width // 2, rank)
    rights, own_first, own_second, own_splits, products = kernel(
        own_kernel,
        [
            shape(3 * half_width, rank),
            half_rows,
            half_rows,
            shape(3 * half_width, 3 * rank, dtype=jnp.bfloat16),
            shape(3, rows, half_width),
        ],
        [vmem] * 5,
        [],
        "own_part",
        cost=2**24,
    )(left, inverse, own_right, *beside)
    own_first, own_second = swap(own_first, "fsdp", 1), swap(own_second, "fsdp", 2)
    first, second = kernel(
        forward_kernel,
        [shape(half_width // 2 + 8, rank), half_rows],
        [vmem] * 3 + [anywhere] * 2,
        [],
        "forward",
    )(received_rows[1], received_rows[2], squares, own_first, own_second)
    first, second = swap(first, "fsdp", 1), swap(second, "fsdp", 2)

    new_momentum, splits = kernel(
        momentum_kernel,
        [shape(rows, cols), shape(3 * half_width, 3 * rank, dtype=jnp.bfloat16)],
        [smem] + [vmem] * 8,
        [pltpu.VMEM((3, rows, width), jnp.float32), pltpu.SemaphoreType.DMA((3,))],
        "new_momentum",
        cost=2**24,
        out_specs=[anywhere, vmem],
    )(bits, left, products, *pieces[:3], *received_rows)
    new_momentum, update, next_basis = kernel(
        functools.partial(last_kernel, math.sqrt(total_rows / total_cols)),
        [
            shape(rows, cols),
            shape(rows, cols, dtype=jnp.bfloat16),
            shape(cols // lax.axis_size("fsdp"), rank),
        ],
        [smem] + [vmem] * 13 + [anywhere],
        [
            pltpu.VMEM((half_width, rank), jnp.float32),
            pltpu.VMEM((half_width, rank), jnp.float32),
            pltpu.VMEM((2 * half_width, 3 * rank), jnp.bfloat16),
            pltpu.VMEM((rows, width), jnp.float32),
            pltpu.VMEM((square, rows, width), jnp.bfloat16),
            pltpu.VMEM((half_width, rank), jnp.float32),
            pltpu.SemaphoreType.DMA((square + 2,)),
        ],
        "last",
        out_specs=[anywhere] * 3,
        aliases={14: 0},
    )(
        *(bits, squares, left, rights, own_splits, splits, *received_rows),
        *(own_first, own_second, first, second, pieces[3], new_momentum),
    )
    return (update, new_momentum, left_scaled, next_basis)


def on_device(momentum, gradient, right_basis):
    rows, cols = momentum.shape
    pairs = lax.axis_size("fsdp") == 2 * square and lax.axis_size("tensor") == 4
    aligned = rows % 16 == 0 and cols % (square * lanes) == 0 and right_basis.shape[1] % lanes == 0
    plan = in_squares if pairs and aligned else any_mesh
    return plan(momentum, gradient, right_basis)


def solution(mesh):
    in_specs = (P("fsdp", "tensor"), P("fsdp", "tensor"), P("tensor", None))
    out_specs = (
        P("fsdp", "tensor"),
        P("fsdp", "tensor"),
        P("fsdp", None),
        P(("tensor", "fsdp"), None),
    )
    return jax.shard_map(
        on_device, mesh=mesh, in_specs=in_specs, out_specs=out_specs, check_vma=False
    )
```

```python
import functools
import math

import jax
import jax.numpy as jnp
from jax import lax
from jax.experimental import pallas as pl
from jax.experimental.pallas import tpu as pltpu
from jax.sharding import PartitionSpec as P

epsilon = 1e-06
highest = lax.Precision.HIGHEST
lanes = 128
panel = 8
square = 4


def dot(a, b, contract=((1,), (0,))):
    return lax.dot_general(
        a, b, (contract, ((), ())), precision=highest, preferred_element_type=jnp.float32
    )


vmem = pl.BlockSpec(memory_space=pltpu.VMEM)
smem = pl.BlockSpec(memory_space=pltpu.SMEM)
anywhere = pl.BlockSpec(memory_space=pl.ANY)


def kernel(body, out_shape, in_specs, scratch, name, cost=0, out_specs=None, aliases=None):
    extra = {} if out_specs is None else {"out_specs": out_specs}
    return pl.pallas_call(
        body,
        out_shape=out_shape,
        input_output_aliases=aliases or {},
        **extra,
        in_specs=in_specs,
        scratch_shapes=scratch,
        compiler_params=pltpu.CompilerParams(vmem_limit_bytes=32 * 2**20),
        cost_estimate=pl.CostEstimate(flops=0, bytes_accessed=cost, transcendentals=0),
        name=name,
    )


def shape(*dims, dtype=jnp.float32):
    return jax.ShapeDtypeStruct(dims, dtype)


def split(value):
    high = value.astype(jnp.bfloat16)
    return high, (value - high.astype(jnp.float32)).astype(jnp.bfloat16)


def three_left(value):
    high, low = split(value)
    return jnp.concatenate([high, high, low], axis=1)


def three_right(value):
    high, low = split(value)
    return jnp.concatenate([high, low, high], axis=1)


def dot_three(a, b):
    return lax.dot_general(a, b, (((1,), (1,)), ((), ())), preferred_element_type=jnp.float32)


def factor_block(block):
    size = block.shape[0]
    lane = lax.broadcasted_iota(jnp.int32, (panel, size), 1)
    row = lax.broadcasted_iota(jnp.int32, (panel, size), 0)
    for first in range(0, size, panel):
        count = size - first
        now = block[first:, :]
        columns = [
            jnp.broadcast_to(now[:, first + k : first + k + 1], (count, size)) for k in range(panel)
        ]
        inside = (lane >= first) & (lane < first + panel)
        head = jnp.where(inside, jnp.where(lane - first == row, 1.0, 0.0), now[:panel])
        tail = None
        if count > panel:
            lane_below = lax.broadcasted_iota(jnp.int32, (count - panel, size), 1)
            inside_below = (lane_below >= first) & (lane_below < first + panel)
            tail = jnp.where(inside_below, 0.0, now[panel:])
        for j in range(panel):
            inverse = lax.rsqrt(columns[j][j : j + 1, :])
            multiplier = columns[j] * inverse
            for k in range(j + 1, panel):
                columns[k] = columns[k] - multiplier * (columns[k][j : j + 1, :] * inverse)
            pivot = head[j : j + 1, :] * inverse
            below = jnp.where(row > j, head - multiplier[:panel] * pivot, head)
            head = jnp.where(row == j, pivot, below)
            if tail is not None:
                tail = tail - multiplier[panel:] * pivot
        block[first : first + panel, :] = head
        if tail is not None:
            block[first + panel :, :] = tail


def place_gram(bits, shares, work):
    size = work.shape[0]
    count = size // lanes
    core, plane = bits[0], bits[1]
    stack = shares.pop()
    share = shares[0].shape[0]
    for flip_plane in range(2):
        for flip_core in range(2):
            at = pl.multiple_of(((plane ^ flip_plane) * 2 + (core ^ flip_core)) * share, 8)
            stack[pl.ds(at, share), :] = shares[flip_plane * 2 + flip_core][...]
    at = 0
    for j in range(count):
        for i in range(j, count):
            block = stack[at * lanes : (at + 1) * lanes, :]
            work[j * lanes : (j + 1) * lanes, i * lanes : (i + 1) * lanes] = block.T
            at += 1


def factor_step(b, work, out, block):
    size = work.shape[0]
    count = size // lanes
    row = lax.broadcasted_iota(jnp.int32, (lanes, lanes), 0)
    lower = row >= lax.broadcasted_iota(jnp.int32, (lanes, lanes), 1)
    rows = slice(b * lanes, (b + 1) * lanes)
    past = (b + 1) * lanes
    block[...] = work[rows, rows]
    factor_block(block)
    inverse = jnp.where(lower, block[...], 0.0)
    out[:, rows] = inverse
    if b:
        out[:, : b * lanes] = dot(inverse, work[rows, : b * lanes])
    if past < size:
        out[:, past:] = jnp.zeros((lanes, size - past), jnp.float32)
        upper = dot(inverse, work[rows, past:])
        own = out[:, :past]
        for i in range(b + 1, count):
            at = (i - b - 1) * lanes
            left = upper[:, at : at + lanes]
            below = slice(i * lanes, (i + 1) * lanes)
            work[below, i * lanes :] = work[below, i * lanes :] - dot(left, upper[:, at:], ((0,), (0,)))
            change = dot(left, own, ((0,), (0,)))
            if b:
                work[below, : b * lanes] = work[below, : b * lanes] - change[:, : b * lanes]
            work[below, b * lanes : past] = -change[:, b * lanes :]


def whole_kernel(gram, out, work, block):
    work[...] = gram[...]
    for b in range(work.shape[0] // lanes):
        factor_step(b, work, out.at[b * lanes : (b + 1) * lanes], block)


def inverse_factor(gram):
    size = gram.shape[0]
    return kernel(
        whole_kernel,
        jax.ShapeDtypeStruct((size, size), jnp.float32),
        [vmem],
        [pltpu.VMEM((size, size), jnp.float32), pltpu.VMEM((lanes, lanes), jnp.float32)],
        "inverse_factor",
    )(gram)


def first_kernel(bits, a, b, c, d, out, work, stack, block):
    place_gram(bits, [a, b, c, d, stack], work)
    factor_step(0, work, out, block)


def first_step(bits, shares, size):
    blocks = sum(x.shape[0] for x in shares)
    return kernel(
        first_kernel,
        [shape(lanes, size), shape(size, size)],
        [smem] + [vmem] * 4,
        [pltpu.VMEM((blocks, lanes), jnp.float32), pltpu.VMEM((lanes, lanes), jnp.float32)],
        "factor_first",
    )(bits, *shares)


def later_kernel(before, first, own, inverse, own_right, squares, work, block):
    work[...] = before[...]
    inverse[:lanes, :] = first[...]
    for b in range(1, work.shape[0] // lanes):
        factor_step(b, work, inverse.at[b * lanes : (b + 1) * lanes], block)
    own_right[...] = dot(own[...], inverse[...], ((1,), (1,)))
    squares[...] = jnp.sum(own_right[...] * own_right[...], axis=0, keepdims=True)


def later_steps(work, first, own):
    size = work.shape[0]
    return kernel(
        later_kernel,
        [shape(size, size), shape(*own.shape), shape(1, size)],
        [vmem] * 3,
        [pltpu.VMEM((size, size), jnp.float32), pltpu.VMEM((lanes, lanes), jnp.float32)],
        "factor_later",
    )(work, first, own)


def share_norms(right_rows):
    squares = lax.psum(jnp.sum(right_rows * right_rows, axis=0), ("fsdp", "tensor"))
    return jnp.sqrt(squares + epsilon)


def any_mesh(momentum, gradient, right_basis):
    summed = momentum + gradient.astype(jnp.float32)
    left_raw = lax.psum(dot(summed, right_basis), "tensor")
    gram = lax.psum(dot(left_raw, left_raw, ((0,), (0,))), "fsdp")
    inverse = inverse_factor(gram)
    left = dot(left_raw, inverse, ((1,), (1,)))
    total_rows = left.shape[0] * lax.axis_size("fsdp")
    total_cols = summed.shape[1] * lax.axis_size("tensor")
    raw_rows = lax.psum_scatter(
        dot(summed, left_raw, ((0,), (0,))), "fsdp", scatter_dimension=0, tiled=True
    )
    right_rows = dot(raw_rows, inverse, ((1,), (1,)))
    column_norm = share_norms(right_rows)
    scaled_left = left * (math.sqrt(total_rows / total_cols) / column_norm)[None, :]
    raw = lax.all_gather(raw_rows, "fsdp", axis=0, tiled=True)
    product = dot(dot(left, inverse), raw, ((1,), (1,)))
    update = dot(dot(scaled_left, inverse), raw, ((1,), (1,))).astype(jnp.bfloat16)
    new_momentum = summed - 0.5 * product
    return (update, new_momentum, left * math.sqrt(total_rows), right_rows / column_norm[None, :])


def swap(value, axis, flip):
    return lax.ppermute(value, axis, [(i, i ^ flip) for i in range(lax.axis_size(axis))])


def split_kernel(bits, momentum, gradient, *pieces):
    width = pieces[0].shape[1]
    for k, piece in enumerate(pieces):
        at = pl.ds(pl.multiple_of((bits[2] ^ k) * width, lanes), width)
        piece[...] = momentum[:, at] + gradient[:, at].astype(jnp.float32)


def part_left_kernel(bits, basis, momentum, gradient, token, sent, kept, total):
    half = sent.shape[0]
    total[...] = dot(momentum[...] + gradient[...].astype(jnp.float32), basis[...])
    sent[...] = total[pl.ds(pl.multiple_of((1 - bits[0]) * half, 8), half), :]
    kept[...] = total[pl.ds(pl.multiple_of(bits[0] * half, 8), half), :]


def core_add_kernel(bits, kept, both, out):
    half = kept.shape[0]
    out[...] = kept[...] + both[pl.ds(pl.multiple_of((1 - bits[0]) * half, 8), half), :]


def add_kernel(*refs):
    refs[-1][...] = refs[0][...] + refs[1][...]


def add_after(a, b, *tokens):
    return kernel(
        add_kernel, shape(*a.shape), [vmem] * 2 + [anywhere] * len(tokens), [], "add_after"
    )(a, b, *tokens)


def gram_kernel(bits, *refs):
    parts, (sent, kept, rows, stack) = refs[:square], refs[square:]
    half, rank = parts[0].shape
    share = sent.shape[0]
    for k, part in enumerate(parts):
        rows[k * half : (k + 1) * half, :] = part[...]
    at = 0
    for first in range(0, rank, 2 * lanes):
        last = min(first + 2 * lanes, rank)
        product = dot(rows[:, first:], rows[:, first:last], ((0,), (0,)))
        for j in range(0, last - first, lanes):
            stack[at : at + rank - first - j, :] = product[j:, j : j + lanes]
            at += rank - first - j
    for out, core in ((kept, bits[0]), (sent, 1 - bits[0])):
        index = (2 * bits[1] + core) * 2 + bits[2] % 2
        out[...] = stack[pl.ds(pl.multiple_of(index * share, 8), share), :]


def raw_kernel(bits, token, *refs):
    mine, others, columns = refs[:square], refs[square : 2 * square], refs[2 * square : 3 * square]
    sent, kept, left, right, raw = refs[3 * square :]
    rows = columns[0].shape[0]
    half = rows // 2
    for k in range(square):
        left[k * rows : (k + 1) * rows, :] = columns[k][...]
        right[pl.ds(pl.multiple_of(k * rows + bits[0] * half, 8), half), :] = mine[k][...]
        right[pl.ds(pl.multiple_of(k * rows + (1 - bits[0]) * half, 8), half), :] = others[k][...]
    raw[...] = dot(left[...], right[...], ((0,), (0,)))
    count = kept.shape[0]
    kept[...] = raw[pl.ds(pl.multiple_of(bits[4] * count, 8), count), :]
    sent[...] = raw[pl.ds(pl.multiple_of((1 - bits[4]) * count, 8), count), :]


def norm_kernel(inverse, before, one, two, received, out, squares):
    right = dot(received[...], inverse[...], ((1,), (1,)))
    out[...] = right
    squares[...] = before[...] + jnp.sum(right * right, axis=0, keepdims=True)


def beside_kernel(inverse, one, two, squares, rights, first, second):
    count = one.shape[0]
    middle = count // 2
    rights[:count, :] = dot(one[...], inverse[...], ((1,), (1,)))
    rights[count:, :] = dot(two[...], inverse[...], ((1,), (1,)))
    first[...] = rights[count : count + middle, :]
    with_row(rights.at[middle:count], squares[...], second)


def with_row(rows, value, out):
    count = rows.shape[0]
    out[:count, :] = rows[...]
    row = lax.broadcasted_iota(jnp.int32, (8, rows.shape[1]), 0)
    out[count:, :] = jnp.where(row == 0, value, 0.0)


def left_kernel(bits, mine, other, inverse, left, rows):
    half = mine.shape[0]
    rows[pl.ds(pl.multiple_of(bits[0] * half, 8), half), :] = mine[...]
    rows[pl.ds(pl.multiple_of((1 - bits[0]) * half, 8), half), :] = other[...]
    left[...] = dot(rows[...], inverse[...], ((1,), (1,)))


def forward_kernel(one, two, squares, own_second, left, own_first, first, second, total):
    middle = second.shape[0]
    total[...] = squares[...] + own_second[middle : middle + 1, :]
    with_row(two.at[:middle], total[...], first)
    second[...] = one[middle:, :]


def columns_of(bits, k, width):
    return pl.ds(pl.multiple_of((bits[2] ^ k) * width, lanes), width)


def in_order(bits, mine, other):
    lower = jnp.concatenate([mine, other], axis=1)
    return jnp.where(bits[4] == 0, lower, jnp.concatenate([other, mine], axis=1))


def momentum_kernel(scale, bits, left, own_right, rights, *refs):
    pieces, received, refs = refs[:3], refs[3:6], refs[6:]
    new_momentum, left_scaled, own_splits, splits, ready, left_ready, sent = refs
    left_ready[...] = left[...] * scale
    copies = [pltpu.make_async_copy(left_ready, left_scaled, sent.at[3])]
    copies[0].start()
    width = pieces[0].shape[1]
    half = width // 2
    own_splits[:half, :] = three_right(own_right[...])
    own_splits[half:, :] = three_right(rights[...])
    for k in range(3):
        splits[k * half : (k + 1) * half, :] = three_right(received[k][...])
    scaled = three_left(left[...])
    for k in range(3):
        at = slice(k * half, (k + 1) * half)
        mine, other = dot_three(scaled, own_splits[at, :]), dot_three(scaled, splits[at, :])
        ready[k] = pieces[k][...] - 0.5 * in_order(bits, mine, other)
        target = new_momentum.at[:, columns_of(bits, k, width)]
        copies.append(pltpu.make_async_copy(ready.at[k], target, sent.at[k]))
        copies[-1].start()
    for copy in copies:
        copy.wait()


def last_kernel(factor, bits, squares, left, own_right, rights, own_splits, splits, *refs):
    received, (own_first, own_second, first, second, piece, _, new_momentum, update, next_basis), scratch = (
        refs[:3],
        refs[3:12],
        refs[12:],
    )
    last_own, last_received, last_splits, ready, scaled_ready, basis_ready, sent = scratch
    half, width = basis_ready.shape[0], piece.shape[1]
    middle = half // 2
    norm = jnp.sqrt(squares[...] + first[middle : middle + 1, :] + epsilon)
    copies = []

    def send(source, target, index):
        copies.append(pltpu.make_async_copy(source, target, sent.at[index]))
        copies[-1].start()

    last_own[:middle, :] = own_first[...]
    last_own[middle:, :] = own_second[:middle, :]
    last_received[:middle, :] = first[:middle, :]
    last_received[middle:, :] = second[...]
    last_splits[:half, :] = three_right(last_own[...])
    last_splits[half:, :] = three_right(last_received[...])
    both = dot_three(three_left(left[...]), last_splits[...])
    ready[...] = piece[...] - 0.5 * in_order(bits, both[:, :half], both[:, half:])
    send(ready, new_momentum.at[:, columns_of(bits, square - 1, width)], square)
    for k in range(square):

        @pl.when((bits[3] // 2) ^ bits[2] == k)
        def _():
            beside = [rights[i * half : (i + 1) * half, :] for i in range(2)]
            mine = [own_right[...], *beside, last_own[...]][k]
            other = last_received[...] if k == square - 1 else received[k][...]
            basis_ready[...] = jnp.where(bits[3] % 2 == bits[4], mine, other) / norm

    send(basis_ready, next_basis, square + 1)
    scaled = three_left(left[...] * (factor / norm))
    for k in range(square):
        if k < square - 1:
            parts = slice(k * half, (k + 1) * half)
            mine = dot_three(scaled, own_splits[parts, :])
            other = dot_three(scaled, splits[parts, :])
        else:
            both = dot_three(scaled, last_splits[...])
            mine, other = both[:, :half], both[:, half:]
        scaled_ready[k] = in_order(bits, mine, other).astype(jnp.bfloat16)
        send(scaled_ready.at[k], update.at[:, columns_of(bits, k, width)], k)
    for copy in copies:
        copy.wait()


def in_squares(momentum, gradient, right_basis):
    device = lax.axis_index("fsdp")
    tensor = lax.axis_index("tensor")
    bits = jnp.stack([tensor % 2, tensor // 2, device % square, device, device // square])
    bits = bits.astype(jnp.int32)
    rows, cols = momentum.shape
    rank = right_basis.shape[1]
    half, width = rows // 2, cols // square
    total_rows = rows * lax.axis_size("fsdp")
    total_cols = cols * lax.axis_size("tensor")

    pieces = kernel(split_kernel, [shape(rows, width)] * square, [smem, vmem, vmem], [], "split_sum")(
        bits, momentum, gradient
    )
    columns = [pieces[0]] + [swap(pieces[k], "fsdp", k) for k in range(1, square)]

    sent, kept = kernel(
        part_left_kernel,
        [shape(half, rank)] * 2,
        [smem] + [vmem] * 3 + [anywhere],
        [pltpu.VMEM((rows, rank), jnp.float32)],
        "part_left",
    )(bits, right_basis, momentum, gradient, pieces[0])
    cores = [[i, i + 1] for i in range(0, lax.axis_size("tensor"), 2)]
    both = lax.all_gather(sent, "tensor", axis=0, tiled=True, axis_index_groups=cores)
    mine = kernel(core_add_kernel, shape(half, rank), [smem, vmem, vmem], [], "core_add")(
        bits, kept, both
    )
    mine = add_after(mine, swap(mine, "tensor", 2), *columns[1:])
    gathered = [mine] + [swap(mine, "fsdp", k) for k in range(1, square)]
    others = [swap(part, "tensor", 1) for part in gathered]

    count = rank // lanes
    stacked = count * (count + 1) // 2 * lanes
    share = stacked // 8
    gram_sent, gram_kept = kernel(
        gram_kernel,
        [shape(share, lanes)] * 2,
        [smem] + [vmem] * square,
        [pltpu.VMEM((square * half, rank), jnp.float32), pltpu.VMEM((stacked, lanes), jnp.float32)],
        "part_gram",
    )(bits, *gathered)
    part = gram_kept + swap(gram_sent, "tensor", 1)

    sent, kept = kernel(
        raw_kernel,
        [shape(width // 2, rank)] * 2,
        [smem, anywhere] + [vmem] * (3 * square),
        [
            pltpu.VMEM((square * rows, width), jnp.float32),
            pltpu.VMEM((square * rows, rank), jnp.float32),
            pltpu.VMEM((width, rank), jnp.float32),
        ],
        "part_raw",
    )(bits, part, *gathered, *others, *columns)

    part = add_after(part, swap(part, "fsdp", square), kept)
    chips = [[i, i + 1] for i in range(0, lax.axis_size("fsdp"), 2)]
    quarter = lax.all_gather(part, "fsdp", axis=0, tiled=True, axis_index_groups=chips)
    over_planes = swap(quarter, "tensor", 2)
    shares = [quarter, swap(quarter, "tensor", 1), over_planes, swap(over_planes, "tensor", 1)]

    first_block, work = first_step(bits, shares, rank)
    own = add_after(kept, swap(sent, "fsdp", square), first_block)

    half_width = width // 2
    received = swap(own, "fsdp", square)
    beside = [swap(own, "fsdp", k) for k in (1, 2)]
    inverse, own_right, squares = later_steps(work, first_block, own)
    received_right, squares = kernel(
        norm_kernel,
        [shape(half_width, rank), shape(1, rank)],
        [vmem] * 2 + [anywhere] * 2 + [vmem],
        [],
        "norms",
    )(inverse, squares, *beside, received)
    received_rows = [received_right] + [swap(received_right, "fsdp", k) for k in (1, 2)]
    for flip in (1, 2):
        squares = squares + swap(squares, "tensor", flip)

    half_rows = shape(half_width // 2, rank)
    with_norms = shape(half_width // 2 + 8, rank)
    rights, own_first, own_second = kernel(
        beside_kernel,
        [shape(2 * half_width, rank), half_rows, with_norms],
        [vmem] * 4,
        [],
        "beside",
    )(inverse, *beside, squares)
    own_first, own_second = swap(own_first, "fsdp", 1), swap(own_second, "fsdp", 2)
    left = kernel(
        left_kernel,
        shape(rows, rank),
        [smem] + [vmem] * 3,
        [pltpu.VMEM((rows, rank), jnp.float32)],
        "left",
        cost=2**23,
    )(bits, mine, others[0], inverse)
    first, second, squares = kernel(
        forward_kernel,
        [with_norms, half_rows, shape(1, rank)],
        [vmem] * 4 + [anywhere] * 2,
        [],
        "forward",
    )(received_rows[1], received_rows[2], squares, own_second, left, own_first)
    first, second = swap(first, "fsdp", 1), swap(second, "fsdp", 2)

    splits_shape = shape(3 * half_width, 3 * rank, dtype=jnp.bfloat16)
    new_momentum, left_scaled, own_splits, splits = kernel(
        functools.partial(momentum_kernel, math.sqrt(total_rows)),
        [shape(rows, cols), shape(rows, rank), splits_shape, splits_shape],
        [smem] + [vmem] * 9,
        [
            pltpu.VMEM((3, rows, width), jnp.float32),
            pltpu.VMEM((rows, rank), jnp.float32),
            pltpu.SemaphoreType.DMA((4,)),
        ],
        "new_momentum",
        cost=2**24,
        out_specs=[anywhere] * 2 + [vmem] * 2,
    )(bits, left, own_right, rights, *pieces[:3], *received_rows)
    new_momentum, update, next_basis = kernel(
        functools.partial(last_kernel, math.sqrt(total_rows / total_cols)),
        [
            shape(rows, cols),
            shape(rows, cols, dtype=jnp.bfloat16),
            shape(cols // lax.axis_size("fsdp"), rank),
        ],
        [smem] + [vmem] * 14 + [anywhere],
        [
            pltpu.VMEM((half_width, rank), jnp.float32),
            pltpu.VMEM((half_width, rank), jnp.float32),
            pltpu.VMEM((2 * half_width, 3 * rank), jnp.bfloat16),
            pltpu.VMEM((rows, width), jnp.float32),
            pltpu.VMEM((square, rows, width), jnp.bfloat16),
            pltpu.VMEM((half_width, rank), jnp.float32),
            pltpu.SemaphoreType.DMA((square + 2,)),
        ],
        "last",
        out_specs=[anywhere] * 3,
        aliases={15: 0},
    )(
        *(bits, squares, left, own_right, rights, own_splits, splits, *received_rows),
        *(own_first, own_second, first, second, pieces[3], new_momentum),
    )
    return (update, new_momentum, left_scaled, next_basis)


def on_device(momentum, gradient, right_basis):
    rows, cols = momentum.shape
    pairs = lax.axis_size("fsdp") == 2 * square and lax.axis_size("tensor") == 4
    aligned = rows % 16 == 0 and cols % (square * lanes) == 0 and right_basis.shape[1] % lanes == 0
    plan = in_squares if pairs and aligned else any_mesh
    return plan(momentum, gradient, right_basis)


def solution(mesh):
    in_specs = (P("fsdp", "tensor"), P("fsdp", "tensor"), P("tensor", None))
    out_specs = (
        P("fsdp", "tensor"),
        P("fsdp", "tensor"),
        P("fsdp", None),
        P(("tensor", "fsdp"), None),
    )
    return jax.shard_map(
        on_device, mesh=mesh, in_specs=in_specs, out_specs=out_specs, check_vma=False
    )
```

```python
import functools
import math

import jax
import jax.numpy as jnp
from jax import lax
from jax.experimental import pallas as pl
from jax.experimental.pallas import tpu as pltpu
from jax.sharding import PartitionSpec as P

epsilon = 1e-06
highest = lax.Precision.HIGHEST
lanes = 128
panel = 8
square = 4


def dot(a, b, contract=((1,), (0,))):
    return lax.dot_general(
        a, b, (contract, ((), ())), precision=highest, preferred_element_type=jnp.float32
    )


vmem = pl.BlockSpec(memory_space=pltpu.VMEM)
smem = pl.BlockSpec(memory_space=pltpu.SMEM)
anywhere = pl.BlockSpec(memory_space=pl.ANY)


def kernel(body, out_shape, in_specs, scratch, name, cost=0, out_specs=None, aliases=None):
    extra = {} if out_specs is None else {"out_specs": out_specs}
    return pl.pallas_call(
        body,
        out_shape=out_shape,
        input_output_aliases=aliases or {},
        **extra,
        in_specs=in_specs,
        scratch_shapes=scratch,
        compiler_params=pltpu.CompilerParams(vmem_limit_bytes=32 * 2**20),
        cost_estimate=pl.CostEstimate(flops=0, bytes_accessed=cost, transcendentals=0),
        name=name,
    )


def shape(*dims, dtype=jnp.float32):
    return jax.ShapeDtypeStruct(dims, dtype)


def split(value):
    high = value.astype(jnp.bfloat16)
    return high, (value - high.astype(jnp.float32)).astype(jnp.bfloat16)


def three_left(value):
    high, low = split(value)
    return jnp.concatenate([high, high, low], axis=1)


def three_right(value):
    high, low = split(value)
    return jnp.concatenate([high, low, high], axis=1)


def dot_three(a, b):
    return lax.dot_general(a, b, (((1,), (1,)), ((), ())), preferred_element_type=jnp.float32)


def factor_block(block):
    size = block.shape[0]
    lane = lax.broadcasted_iota(jnp.int32, (panel, size), 1)
    row = lax.broadcasted_iota(jnp.int32, (panel, size), 0)
    for first in range(0, size, panel):
        count = size - first
        now = block[first:, :]
        columns = [
            jnp.broadcast_to(now[:, first + k : first + k + 1], (count, size)) for k in range(panel)
        ]
        inside = (lane >= first) & (lane < first + panel)
        head = jnp.where(inside, jnp.where(lane - first == row, 1.0, 0.0), now[:panel])
        tail = None
        if count > panel:
            lane_below = lax.broadcasted_iota(jnp.int32, (count - panel, size), 1)
            inside_below = (lane_below >= first) & (lane_below < first + panel)
            tail = jnp.where(inside_below, 0.0, now[panel:])
        for j in range(panel):
            inverse = lax.rsqrt(columns[j][j : j + 1, :])
            multiplier = columns[j] * inverse
            for k in range(j + 1, panel):
                columns[k] = columns[k] - multiplier * (columns[k][j : j + 1, :] * inverse)
            pivot = head[j : j + 1, :] * inverse
            below = jnp.where(row > j, head - multiplier[:panel] * pivot, head)
            head = jnp.where(row == j, pivot, below)
            if tail is not None:
                tail = tail - multiplier[panel:] * pivot
        block[first : first + panel, :] = head
        if tail is not None:
            block[first + panel :, :] = tail


def place_gram(bits, shares, work):
    size = work.shape[0]
    count = size // lanes
    core, plane = bits[0], bits[1]
    stack = shares.pop()
    share = shares[0].shape[0]
    for flip_plane in range(2):
        for flip_core in range(2):
            at = pl.multiple_of(((plane ^ flip_plane) * 2 + (core ^ flip_core)) * share, 8)
            stack[pl.ds(at, share), :] = shares[flip_plane * 2 + flip_core][...]
    at = 0
    for j in range(count):
        for i in range(j, count):
            block = stack[at * lanes : (at + 1) * lanes, :]
            work[j * lanes : (j + 1) * lanes, i * lanes : (i + 1) * lanes] = block.T
            at += 1


def factor_step(b, work, out, block):
    size = work.shape[0]
    count = size // lanes
    row = lax.broadcasted_iota(jnp.int32, (lanes, lanes), 0)
    lower = row >= lax.broadcasted_iota(jnp.int32, (lanes, lanes), 1)
    rows = slice(b * lanes, (b + 1) * lanes)
    past = (b + 1) * lanes
    block[...] = work[rows, rows]
    factor_block(block)
    inverse = jnp.where(lower, block[...], 0.0)
    out[:, rows] = inverse
    if b:
        out[:, : b * lanes] = dot(inverse, work[rows, : b * lanes])
    if past < size:
        out[:, past:] = jnp.zeros((lanes, size - past), jnp.float32)
        upper = dot(inverse, work[rows, past:])
        own = out[:, :past]
        for i in range(b + 1, count):
            at = (i - b - 1) * lanes
            left = upper[:, at : at + lanes]
            below = slice(i * lanes, (i + 1) * lanes)
            work[below, i * lanes :] = work[below, i * lanes :] - dot(left, upper[:, at:], ((0,), (0,)))
            change = dot(left, own, ((0,), (0,)))
            if b:
                work[below, : b * lanes] = work[below, : b * lanes] - change[:, : b * lanes]
            work[below, b * lanes : past] = -change[:, b * lanes :]


def whole_kernel(gram, out, work, block):
    work[...] = gram[...]
    for b in range(work.shape[0] // lanes):
        factor_step(b, work, out.at[b * lanes : (b + 1) * lanes], block)


def inverse_factor(gram):
    size = gram.shape[0]
    return kernel(
        whole_kernel,
        jax.ShapeDtypeStruct((size, size), jnp.float32),
        [vmem],
        [pltpu.VMEM((size, size), jnp.float32), pltpu.VMEM((lanes, lanes), jnp.float32)],
        "inverse_factor",
    )(gram)


def first_kernel(bits, a, b, c, d, out, work, stack, block):
    place_gram(bits, [a, b, c, d, stack], work)
    factor_step(0, work, out, block)


def first_step(bits, shares, size):
    blocks = sum(x.shape[0] for x in shares)
    return kernel(
        first_kernel,
        [shape(lanes, size), shape(size, size)],
        [smem] + [vmem] * 4,
        [pltpu.VMEM((blocks, lanes), jnp.float32), pltpu.VMEM((lanes, lanes), jnp.float32)],
        "factor_first",
    )(bits, *shares)


def later_kernel(before, first, own, inverse, own_right, squares, work, block):
    work[...] = before[...]
    inverse[:lanes, :] = first[...]
    for b in range(1, work.shape[0] // lanes):
        factor_step(b, work, inverse.at[b * lanes : (b + 1) * lanes], block)
    own_right[...] = dot(own[...], inverse[...], ((1,), (1,)))
    squares[...] = jnp.sum(own_right[...] * own_right[...], axis=0, keepdims=True)


def later_steps(work, first, own):
    size = work.shape[0]
    return kernel(
        later_kernel,
        [shape(size, size), shape(*own.shape), shape(1, size)],
        [vmem] * 3,
        [pltpu.VMEM((size, size), jnp.float32), pltpu.VMEM((lanes, lanes), jnp.float32)],
        "factor_later",
    )(work, first, own)


def share_norms(right_rows):
    squares = lax.psum(jnp.sum(right_rows * right_rows, axis=0), ("fsdp", "tensor"))
    return jnp.sqrt(squares + epsilon)


def any_mesh(momentum, gradient, right_basis):
    summed = momentum + gradient.astype(jnp.float32)
    left_raw = lax.psum(dot(summed, right_basis), "tensor")
    gram = lax.psum(dot(left_raw, left_raw, ((0,), (0,))), "fsdp")
    inverse = inverse_factor(gram)
    left = dot(left_raw, inverse, ((1,), (1,)))
    total_rows = left.shape[0] * lax.axis_size("fsdp")
    total_cols = summed.shape[1] * lax.axis_size("tensor")
    raw_rows = lax.psum_scatter(
        dot(summed, left_raw, ((0,), (0,))), "fsdp", scatter_dimension=0, tiled=True
    )
    right_rows = dot(raw_rows, inverse, ((1,), (1,)))
    column_norm = share_norms(right_rows)
    scaled_left = left * (math.sqrt(total_rows / total_cols) / column_norm)[None, :]
    raw = lax.all_gather(raw_rows, "fsdp", axis=0, tiled=True)
    product = dot(dot(left, inverse), raw, ((1,), (1,)))
    update = dot(dot(scaled_left, inverse), raw, ((1,), (1,))).astype(jnp.bfloat16)
    new_momentum = summed - 0.5 * product
    return (update, new_momentum, left * math.sqrt(total_rows), right_rows / column_norm[None, :])


def swap(value, axis, flip):
    return lax.ppermute(value, axis, [(i, i ^ flip) for i in range(lax.axis_size(axis))])


def split_kernel(bits, momentum, gradient, *pieces):
    width = pieces[0].shape[1]
    for k, piece in enumerate(pieces):
        at = pl.ds(pl.multiple_of((bits[2] ^ k) * width, lanes), width)
        piece[...] = momentum[:, at] + gradient[:, at].astype(jnp.float32)


def part_left_kernel(bits, basis, momentum, gradient, token, sent, kept, total):
    half = sent.shape[0]
    total[...] = dot(momentum[...] + gradient[...].astype(jnp.float32), basis[...])
    sent[...] = total[pl.ds(pl.multiple_of((1 - bits[0]) * half, 8), half), :]
    kept[...] = total[pl.ds(pl.multiple_of(bits[0] * half, 8), half), :]


def core_add_kernel(bits, kept, both, out):
    half = kept.shape[0]
    out[...] = kept[...] + both[pl.ds(pl.multiple_of((1 - bits[0]) * half, 8), half), :]


def add_kernel(*refs):
    refs[-1][...] = refs[0][...] + refs[1][...]


def add_after(a, b, *tokens):
    return kernel(
        add_kernel, shape(*a.shape), [vmem] * 2 + [anywhere] * len(tokens), [], "add_after"
    )(a, b, *tokens)


def gram_kernel(bits, *refs):
    parts, (sent, kept, rows, stack) = refs[:square], refs[square:]
    half, rank = parts[0].shape
    share = sent.shape[0]
    for k, part in enumerate(parts):
        rows[k * half : (k + 1) * half, :] = part[...]
    at = 0
    for first in range(0, rank, 2 * lanes):
        last = min(first + 2 * lanes, rank)
        product = dot(rows[:, first:], rows[:, first:last], ((0,), (0,)))
        for j in range(0, last - first, lanes):
            stack[at : at + rank - first - j, :] = product[j:, j : j + lanes]
            at += rank - first - j
    for out, core in ((kept, bits[0]), (sent, 1 - bits[0])):
        index = (2 * bits[1] + core) * 2 + bits[2] % 2
        out[...] = stack[pl.ds(pl.multiple_of(index * share, 8), share), :]


def raw_kernel(bits, token, *refs):
    mine, others, columns = refs[:square], refs[square : 2 * square], refs[2 * square : 3 * square]
    sent, kept, left, right, raw = refs[3 * square :]
    rows = columns[0].shape[0]
    half = rows // 2
    for k in range(square):
        left[k * rows : (k + 1) * rows, :] = columns[k][...]
        right[pl.ds(pl.multiple_of(k * rows + bits[0] * half, 8), half), :] = mine[k][...]
        right[pl.ds(pl.multiple_of(k * rows + (1 - bits[0]) * half, 8), half), :] = others[k][...]
    raw[...] = dot(left[...], right[...], ((0,), (0,)))
    count = kept.shape[0]
    kept[...] = raw[pl.ds(pl.multiple_of(bits[4] * count, 8), count), :]
    sent[...] = raw[pl.ds(pl.multiple_of((1 - bits[4]) * count, 8), count), :]


def norm_kernel(inverse, before, one, two, received, out, squares):
    right = dot(received[...], inverse[...], ((1,), (1,)))
    out[...] = right
    squares[...] = before[...] + jnp.sum(right * right, axis=0, keepdims=True)


def beside_kernel(inverse, one, two, token, rights, first, second):
    count = one.shape[0]
    middle = count // 2
    rights[:count, :] = dot(one[...], inverse[...], ((1,), (1,)))
    rights[count:, :] = dot(two[...], inverse[...], ((1,), (1,)))
    for out, at in ((first, count), (second, middle)):
        out[:middle, :] = rights[at : at + middle, :]
        out[middle:, :] = jnp.zeros((out.shape[0] - middle, out.shape[1]), jnp.float32)


def with_row(rows, value, out):
    count = rows.shape[0]
    out[:count, :] = rows[...]
    row = lax.broadcasted_iota(jnp.int32, (8, rows.shape[1]), 0)
    out[count:, :] = jnp.where(row == 0, value, 0.0)


def left_kernel(bits, mine, other, inverse, left, rows):
    half = mine.shape[0]
    rows[pl.ds(pl.multiple_of(bits[0] * half, 8), half), :] = mine[...]
    rows[pl.ds(pl.multiple_of((1 - bits[0]) * half, 8), half), :] = other[...]
    left[...] = dot(rows[...], inverse[...], ((1,), (1,)))


def forward_kernel(one, two, squares, first, second):
    middle = second.shape[0]
    with_row(two.at[:middle], squares[...], first)
    second[...] = one[middle:, :]


def columns_of(bits, k, width):
    return pl.ds(pl.multiple_of((bits[2] ^ k) * width, lanes), width)


def in_order(bits, mine, other):
    lower = jnp.concatenate([mine, other], axis=1)
    return jnp.where(bits[4] == 0, lower, jnp.concatenate([other, mine], axis=1))


def momentum_kernel(scale, bits, left, own_right, rights, *refs):
    pieces, received, refs = refs[:3], refs[3:6], refs[6:]
    new_momentum, left_scaled, own_splits, splits, ready, left_ready, sent = refs
    left_ready[...] = left[...] * scale
    copies = [pltpu.make_async_copy(left_ready, left_scaled, sent.at[3])]
    copies[0].start()
    width = pieces[0].shape[1]
    half = width // 2
    own_splits[:half, :] = three_right(own_right[...])
    own_splits[half:, :] = three_right(rights[...])
    for k in range(3):
        splits[k * half : (k + 1) * half, :] = three_right(received[k][...])
    scaled = three_left(left[...])
    for k in range(3):
        at = slice(k * half, (k + 1) * half)
        mine, other = dot_three(scaled, own_splits[at, :]), dot_three(scaled, splits[at, :])
        ready[k] = pieces[k][...] - 0.5 * in_order(bits, mine, other)
        target = new_momentum.at[:, columns_of(bits, k, width)]
        copies.append(pltpu.make_async_copy(ready.at[k], target, sent.at[k]))
        copies[-1].start()
    for copy in copies:
        copy.wait()


def last_kernel(factor, bits, squares, left, own_right, rights, own_splits, splits, *refs):
    received, (first, second, own_first, own_second, piece, _, new_momentum, update, next_basis), scratch = (
        refs[:3],
        refs[3:12],
        refs[12:],
    )
    last_own, last_received, last_splits, ready, scaled_ready, basis_ready, sent = scratch
    half, width = basis_ready.shape[0], piece.shape[1]
    middle = half // 2
    norm = jnp.sqrt(squares[...] + first[middle : middle + 1, :] + epsilon)
    copies = []

    def send(source, target, index):
        copies.append(pltpu.make_async_copy(source, target, sent.at[index]))
        copies[-1].start()

    last_own[:middle, :] = own_first[:middle, :]
    last_own[middle:, :] = own_second[:middle, :]
    last_received[:middle, :] = first[:middle, :]
    last_received[middle:, :] = second[...]
    last_splits[:half, :] = three_right(last_own[...])
    last_splits[half:, :] = three_right(last_received[...])
    both = dot_three(three_left(left[...]), last_splits[...])
    ready[...] = piece[...] - 0.5 * in_order(bits, both[:, :half], both[:, half:])
    send(ready, new_momentum.at[:, columns_of(bits, square - 1, width)], square)
    for k in range(square):

        @pl.when((bits[3] // 2) ^ bits[2] == k)
        def _():
            beside = [rights[i * half : (i + 1) * half, :] for i in range(2)]
            mine = [own_right[...], *beside, last_own[...]][k]
            other = last_received[...] if k == square - 1 else received[k][...]
            basis_ready[...] = jnp.where(bits[3] % 2 == bits[4], mine, other) / norm

    send(basis_ready, next_basis, square + 1)
    scaled = three_left(left[...] * (factor / norm))
    for k in range(square):
        if k < square - 1:
            parts = slice(k * half, (k + 1) * half)
            mine = dot_three(scaled, own_splits[parts, :])
            other = dot_three(scaled, splits[parts, :])
        else:
            both = dot_three(scaled, last_splits[...])
            mine, other = both[:, :half], both[:, half:]
        scaled_ready[k] = in_order(bits, mine, other).astype(jnp.bfloat16)
        send(scaled_ready.at[k], update.at[:, columns_of(bits, k, width)], k)
    for copy in copies:
        copy.wait()


def in_squares(momentum, gradient, right_basis):
    device = lax.axis_index("fsdp")
    tensor = lax.axis_index("tensor")
    bits = jnp.stack([tensor % 2, tensor // 2, device % square, device, device // square])
    bits = bits.astype(jnp.int32)
    rows, cols = momentum.shape
    rank = right_basis.shape[1]
    half, width = rows // 2, cols // square
    total_rows = rows * lax.axis_size("fsdp")
    total_cols = cols * lax.axis_size("tensor")

    pieces = kernel(split_kernel, [shape(rows, width)] * square, [smem, vmem, vmem], [], "split_sum")(
        bits, momentum, gradient
    )
    columns = [pieces[0]] + [swap(pieces[k], "fsdp", k) for k in range(1, square)]

    sent, kept = kernel(
        part_left_kernel,
        [shape(half, rank)] * 2,
        [smem] + [vmem] * 3 + [anywhere],
        [pltpu.VMEM((rows, rank), jnp.float32)],
        "part_left",
    )(bits, right_basis, momentum, gradient, pieces[0])
    cores = [[i, i + 1] for i in range(0, lax.axis_size("tensor"), 2)]
    both = lax.all_gather(sent, "tensor", axis=0, tiled=True, axis_index_groups=cores)
    mine = kernel(core_add_kernel, shape(half, rank), [smem, vmem, vmem], [], "core_add")(
        bits, kept, both
    )
    mine = add_after(mine, swap(mine, "tensor", 2), *columns[1:])
    gathered = [mine] + [swap(mine, "fsdp", k) for k in range(1, square)]
    others = [swap(part, "tensor", 1) for part in gathered]

    count = rank // lanes
    stacked = count * (count + 1) // 2 * lanes
    share = stacked // 8
    gram_sent, gram_kept = kernel(
        gram_kernel,
        [shape(share, lanes)] * 2,
        [smem] + [vmem] * square,
        [pltpu.VMEM((square * half, rank), jnp.float32), pltpu.VMEM((stacked, lanes), jnp.float32)],
        "part_gram",
    )(bits, *gathered)
    part = gram_kept + swap(gram_sent, "tensor", 1)

    sent, kept = kernel(
        raw_kernel,
        [shape(width // 2, rank)] * 2,
        [smem, anywhere] + [vmem] * (3 * square),
        [
            pltpu.VMEM((square * rows, width), jnp.float32),
            pltpu.VMEM((square * rows, rank), jnp.float32),
            pltpu.VMEM((width, rank), jnp.float32),
        ],
        "part_raw",
    )(bits, part, *gathered, *others, *columns)

    part = add_after(part, swap(part, "fsdp", square), kept)
    chips = [[i, i + 1] for i in range(0, lax.axis_size("fsdp"), 2)]
    quarter = lax.all_gather(part, "fsdp", axis=0, tiled=True, axis_index_groups=chips)
    over_planes = swap(quarter, "tensor", 2)
    shares = [quarter, swap(quarter, "tensor", 1), over_planes, swap(over_planes, "tensor", 1)]

    first_block, work = first_step(bits, shares, rank)
    own = add_after(kept, swap(sent, "fsdp", square), first_block)

    half_width = width // 2
    received = swap(own, "fsdp", square)
    beside = [swap(own, "fsdp", k) for k in (1, 2)]
    inverse, own_right, squares = later_steps(work, first_block, own)
    received_right, squares = kernel(
        norm_kernel,
        [shape(half_width, rank), shape(1, rank)],
        [vmem] * 2 + [anywhere] * 2 + [vmem],
        [],
        "norms",
    )(inverse, squares, *beside, received)
    received_rows = [received_right] + [swap(received_right, "fsdp", k) for k in (1, 2)]
    for flip in (1, 2):
        squares = squares + swap(squares, "tensor", flip)

    half_rows = shape(half_width // 2, rank)
    with_norms = shape(half_width // 2 + 8, rank)
    padded = shape(half_width // 2 + 8, rank)
    rights, own_first, own_second = kernel(
        beside_kernel,
        [shape(2 * half_width, rank), padded, padded],
        [vmem] * 3 + [anywhere],
        [],
        "beside",
    )(inverse, *beside, squares)
    own_first, own_second = swap(own_first, "fsdp", 1), swap(own_second, "fsdp", 2)
    squares = squares + swap(squares, "fsdp", 2)
    left = kernel(
        left_kernel,
        shape(rows, rank),
        [smem] + [vmem] * 3,
        [pltpu.VMEM((rows, rank), jnp.float32)],
        "left",
        cost=2**23,
    )(bits, mine, others[0], inverse)
    first, second = kernel(
        forward_kernel, [with_norms, half_rows], [vmem] * 3, [], "forward"
    )(received_rows[1], received_rows[2], squares)
    first, second = swap(first, "fsdp", 1), swap(second, "fsdp", 2)

    splits_shape = shape(3 * half_width, 3 * rank, dtype=jnp.bfloat16)
    new_momentum, left_scaled, own_splits, splits = kernel(
        functools.partial(momentum_kernel, math.sqrt(total_rows)),
        [shape(rows, cols), shape(rows, rank), splits_shape, splits_shape],
        [smem] + [vmem] * 9,
        [
            pltpu.VMEM((3, rows, width), jnp.float32),
            pltpu.VMEM((rows, rank), jnp.float32),
            pltpu.SemaphoreType.DMA((4,)),
        ],
        "new_momentum",
        cost=2**24,
        out_specs=[anywhere] * 2 + [vmem] * 2,
    )(bits, left, own_right, rights, *pieces[:3], *received_rows)
    new_momentum, update, next_basis = kernel(
        functools.partial(last_kernel, math.sqrt(total_rows / total_cols)),
        [
            shape(rows, cols),
            shape(rows, cols, dtype=jnp.bfloat16),
            shape(cols // lax.axis_size("fsdp"), rank),
        ],
        [smem] + [vmem] * 14 + [anywhere],
        [
            pltpu.VMEM((half_width, rank), jnp.float32),
            pltpu.VMEM((half_width, rank), jnp.float32),
            pltpu.VMEM((2 * half_width, 3 * rank), jnp.bfloat16),
            pltpu.VMEM((rows, width), jnp.float32),
            pltpu.VMEM((square, rows, width), jnp.bfloat16),
            pltpu.VMEM((half_width, rank), jnp.float32),
            pltpu.SemaphoreType.DMA((square + 2,)),
        ],
        "last",
        out_specs=[anywhere] * 3,
        aliases={15: 0},
    )(
        *(bits, squares, left, own_right, rights, own_splits, splits, *received_rows),
        *(first, second, own_first, own_second, pieces[3], new_momentum),
    )
    return (update, new_momentum, left_scaled, next_basis)


def on_device(momentum, gradient, right_basis):
    rows, cols = momentum.shape
    pairs = lax.axis_size("fsdp") == 2 * square and lax.axis_size("tensor") == 4
    aligned = rows % 16 == 0 and cols % (square * lanes) == 0 and right_basis.shape[1] % lanes == 0
    plan = in_squares if pairs and aligned else any_mesh
    return plan(momentum, gradient, right_basis)


def solution(mesh):
    in_specs = (P("fsdp", "tensor"), P("fsdp", "tensor"), P("tensor", None))
    out_specs = (
        P("fsdp", "tensor"),
        P("fsdp", "tensor"),
        P("fsdp", None),
        P(("tensor", "fsdp"), None),
    )
    return jax.shard_map(
        on_device, mesh=mesh, in_specs=in_specs, out_specs=out_specs, check_vma=False
    )
```

```python
import functools
import math

import jax
import jax.numpy as jnp
from jax import lax
from jax.experimental import pallas as pl
from jax.experimental.pallas import tpu as pltpu
from jax.sharding import PartitionSpec as P

epsilon = 1e-06
highest = lax.Precision.HIGHEST
lanes = 128
panel = 8
square = 4


def dot(a, b, contract=((1,), (0,))):
    return lax.dot_general(
        a, b, (contract, ((), ())), precision=highest, preferred_element_type=jnp.float32
    )


vmem = pl.BlockSpec(memory_space=pltpu.VMEM)
smem = pl.BlockSpec(memory_space=pltpu.SMEM)
anywhere = pl.BlockSpec(memory_space=pl.ANY)


def kernel(body, out_shape, in_specs, scratch, name, cost=0, out_specs=None, aliases=None):
    extra = {} if out_specs is None else {"out_specs": out_specs}
    return pl.pallas_call(
        body,
        out_shape=out_shape,
        input_output_aliases=aliases or {},
        **extra,
        in_specs=in_specs,
        scratch_shapes=scratch,
        compiler_params=pltpu.CompilerParams(vmem_limit_bytes=32 * 2**20),
        cost_estimate=pl.CostEstimate(flops=0, bytes_accessed=cost, transcendentals=0),
        name=name,
    )


def shape(*dims, dtype=jnp.float32):
    return jax.ShapeDtypeStruct(dims, dtype)


def split(value):
    high = value.astype(jnp.bfloat16)
    return high, (value - high.astype(jnp.float32)).astype(jnp.bfloat16)


def three_left(value):
    high, low = split(value)
    return jnp.concatenate([high, high, low], axis=1)


def three_right(value):
    high, low = split(value)
    return jnp.concatenate([high, low, high], axis=1)


def dot_three(a, b):
    return lax.dot_general(a, b, (((1,), (1,)), ((), ())), preferred_element_type=jnp.float32)


def factor_block(block):
    size = block.shape[0]
    lane = lax.broadcasted_iota(jnp.int32, (panel, size), 1)
    row = lax.broadcasted_iota(jnp.int32, (panel, size), 0)
    for first in range(0, size, panel):
        count = size - first
        now = block[first:, :]
        columns = [
            jnp.broadcast_to(now[:, first + k : first + k + 1], (count, size)) for k in range(panel)
        ]
        inside = (lane >= first) & (lane < first + panel)
        head = jnp.where(inside, jnp.where(lane - first == row, 1.0, 0.0), now[:panel])
        tail = None
        if count > panel:
            lane_below = lax.broadcasted_iota(jnp.int32, (count - panel, size), 1)
            inside_below = (lane_below >= first) & (lane_below < first + panel)
            tail = jnp.where(inside_below, 0.0, now[panel:])
        for j in range(panel):
            inverse = lax.rsqrt(columns[j][j : j + 1, :])
            multiplier = columns[j] * inverse
            for k in range(j + 1, panel):
                columns[k] = columns[k] - multiplier * (columns[k][j : j + 1, :] * inverse)
            pivot = head[j : j + 1, :] * inverse
            below = jnp.where(row > j, head - multiplier[:panel] * pivot, head)
            head = jnp.where(row == j, pivot, below)
            if tail is not None:
                tail = tail - multiplier[panel:] * pivot
        block[first : first + panel, :] = head
        if tail is not None:
            block[first + panel :, :] = tail


def place_gram(bits, shares, work):
    size = work.shape[0]
    count = size // lanes
    core, plane = bits[0], bits[1]
    stack = shares.pop()
    share = shares[0].shape[0]
    for flip_plane in range(2):
        for flip_core in range(2):
            at = pl.multiple_of(((plane ^ flip_plane) * 2 + (core ^ flip_core)) * share, 8)
            stack[pl.ds(at, share), :] = shares[flip_plane * 2 + flip_core][...]
    at = 0
    for j in range(count):
        for i in range(j, count):
            block = stack[at * lanes : (at + 1) * lanes, :]
            work[j * lanes : (j + 1) * lanes, i * lanes : (i + 1) * lanes] = block.T
            at += 1


def factor_step(b, work, out, block):
    size = work.shape[0]
    count = size // lanes
    row = lax.broadcasted_iota(jnp.int32, (lanes, lanes), 0)
    lower = row >= lax.broadcasted_iota(jnp.int32, (lanes, lanes), 1)
    rows = slice(b * lanes, (b + 1) * lanes)
    past = (b + 1) * lanes
    block[...] = work[rows, rows]
    factor_block(block)
    inverse = jnp.where(lower, block[...], 0.0)
    out[:, rows] = inverse
    if b:
        out[:, : b * lanes] = dot(inverse, work[rows, : b * lanes])
    if past < size:
        out[:, past:] = jnp.zeros((lanes, size - past), jnp.float32)
        upper = dot(inverse, work[rows, past:])
        own = out[:, :past]
        for i in range(b + 1, count):
            at = (i - b - 1) * lanes
            left = upper[:, at : at + lanes]
            below = slice(i * lanes, (i + 1) * lanes)
            work[below, i * lanes :] = work[below, i * lanes :] - dot(left, upper[:, at:], ((0,), (0,)))
            change = dot(left, own, ((0,), (0,)))
            if b:
                work[below, : b * lanes] = work[below, : b * lanes] - change[:, : b * lanes]
            work[below, b * lanes : past] = -change[:, b * lanes :]


def whole_kernel(gram, out, work, block):
    work[...] = gram[...]
    for b in range(work.shape[0] // lanes):
        factor_step(b, work, out.at[b * lanes : (b + 1) * lanes], block)


def inverse_factor(gram):
    size = gram.shape[0]
    return kernel(
        whole_kernel,
        jax.ShapeDtypeStruct((size, size), jnp.float32),
        [vmem],
        [pltpu.VMEM((size, size), jnp.float32), pltpu.VMEM((lanes, lanes), jnp.float32)],
        "inverse_factor",
    )(gram)


def first_kernel(bits, a, b, c, d, out, work, stack, block):
    place_gram(bits, [a, b, c, d, stack], work)
    factor_step(0, work, out, block)


def first_step(bits, shares, size):
    blocks = sum(x.shape[0] for x in shares)
    return kernel(
        first_kernel,
        [shape(lanes, size), shape(size, size)],
        [smem] + [vmem] * 4,
        [pltpu.VMEM((blocks, lanes), jnp.float32), pltpu.VMEM((lanes, lanes), jnp.float32)],
        "factor_first",
    )(bits, *shares)


def later_kernel(before, first, own, inverse, own_right, squares, work, block):
    work[...] = before[...]
    inverse[:lanes, :] = first[...]
    for b in range(1, work.shape[0] // lanes):
        factor_step(b, work, inverse.at[b * lanes : (b + 1) * lanes], block)
    own_right[...] = dot(own[...], inverse[...], ((1,), (1,)))
    squares[...] = jnp.sum(own_right[...] * own_right[...], axis=0, keepdims=True)


def later_steps(work, first, own):
    size = work.shape[0]
    return kernel(
        later_kernel,
        [shape(size, size), shape(*own.shape), shape(1, size)],
        [vmem] * 3,
        [pltpu.VMEM((size, size), jnp.float32), pltpu.VMEM((lanes, lanes), jnp.float32)],
        "factor_later",
    )(work, first, own)


def share_norms(right_rows):
    squares = lax.psum(jnp.sum(right_rows * right_rows, axis=0), ("fsdp", "tensor"))
    return jnp.sqrt(squares + epsilon)


def any_mesh(momentum, gradient, right_basis):
    summed = momentum + gradient.astype(jnp.float32)
    left_raw = lax.psum(dot(summed, right_basis), "tensor")
    gram = lax.psum(dot(left_raw, left_raw, ((0,), (0,))), "fsdp")
    inverse = inverse_factor(gram)
    left = dot(left_raw, inverse, ((1,), (1,)))
    total_rows = left.shape[0] * lax.axis_size("fsdp")
    total_cols = summed.shape[1] * lax.axis_size("tensor")
    raw_rows = lax.psum_scatter(
        dot(summed, left_raw, ((0,), (0,))), "fsdp", scatter_dimension=0, tiled=True
    )
    right_rows = dot(raw_rows, inverse, ((1,), (1,)))
    column_norm = share_norms(right_rows)
    scaled_left = left * (math.sqrt(total_rows / total_cols) / column_norm)[None, :]
    raw = lax.all_gather(raw_rows, "fsdp", axis=0, tiled=True)
    product = dot(dot(left, inverse), raw, ((1,), (1,)))
    update = dot(dot(scaled_left, inverse), raw, ((1,), (1,))).astype(jnp.bfloat16)
    new_momentum = summed - 0.5 * product
    return (update, new_momentum, left * math.sqrt(total_rows), right_rows / column_norm[None, :])


def swap(value, axis, flip):
    return lax.ppermute(value, axis, [(i, i ^ flip) for i in range(lax.axis_size(axis))])


def split_kernel(bits, momentum, gradient, *pieces):
    width = pieces[0].shape[1]
    for k, piece in enumerate(pieces):
        at = pl.ds(pl.multiple_of((bits[2] ^ k) * width, lanes), width)
        piece[...] = momentum[:, at] + gradient[:, at].astype(jnp.float32)


def part_left_kernel(bits, basis, momentum, gradient, token, sent, kept, total):
    half = sent.shape[0]
    total[...] = dot(momentum[...] + gradient[...].astype(jnp.float32), basis[...])
    sent[...] = total[pl.ds(pl.multiple_of((1 - bits[0]) * half, 8), half), :]
    kept[...] = total[pl.ds(pl.multiple_of(bits[0] * half, 8), half), :]


def core_add_kernel(bits, kept, both, out):
    half = kept.shape[0]
    out[...] = kept[...] + both[pl.ds(pl.multiple_of((1 - bits[0]) * half, 8), half), :]


def add_kernel(*refs):
    refs[-1][...] = refs[0][...] + refs[1][...]


def add_after(a, b, *tokens):
    return kernel(
        add_kernel, shape(*a.shape), [vmem] * 2 + [anywhere] * len(tokens), [], "add_after"
    )(a, b, *tokens)


def gram_kernel(bits, *refs):
    parts, (sent, kept, rows, stack) = refs[:square], refs[square:]
    half, rank = parts[0].shape
    share = sent.shape[0]
    for k, part in enumerate(parts):
        rows[k * half : (k + 1) * half, :] = part[...]
    at = 0
    for first in range(0, rank, 2 * lanes):
        last = min(first + 2 * lanes, rank)
        product = dot(rows[:, first:], rows[:, first:last], ((0,), (0,)))
        for j in range(0, last - first, lanes):
            stack[at : at + rank - first - j, :] = product[j:, j : j + lanes]
            at += rank - first - j
    for out, core in ((kept, bits[0]), (sent, 1 - bits[0])):
        index = (2 * bits[1] + core) * 2 + bits[2] % 2
        out[...] = stack[pl.ds(pl.multiple_of(index * share, 8), share), :]


def raw_kernel(bits, token, *refs):
    mine, others, columns = refs[:square], refs[square : 2 * square], refs[2 * square : 3 * square]
    sent, kept, left, right, raw = refs[3 * square :]
    rows = columns[0].shape[0]
    half = rows // 2
    for k in range(square):
        left[k * rows : (k + 1) * rows, :] = columns[k][...]
        right[pl.ds(pl.multiple_of(k * rows + bits[0] * half, 8), half), :] = mine[k][...]
        right[pl.ds(pl.multiple_of(k * rows + (1 - bits[0]) * half, 8), half), :] = others[k][...]
    raw[...] = dot(left[...], right[...], ((0,), (0,)))
    count = kept.shape[0]
    kept[...] = raw[pl.ds(pl.multiple_of(bits[4] * count, 8), count), :]
    sent[...] = raw[pl.ds(pl.multiple_of((1 - bits[4]) * count, 8), count), :]


def norm_kernel(inverse, before, one, two, received, out, squares):
    right = dot(received[...], inverse[...], ((1,), (1,)))
    out[...] = right
    squares[...] = before[...] + jnp.sum(right * right, axis=0, keepdims=True)


def beside_kernel(inverse, one, two, token, rights, first, second):
    count = one.shape[0]
    middle = count // 2
    rights[:count, :] = dot(one[...], inverse[...], ((1,), (1,)))
    rights[count:, :] = dot(two[...], inverse[...], ((1,), (1,)))
    for out, at in ((first, count), (second, middle)):
        out[:middle, :] = rights[at : at + middle, :]
        out[middle:, :] = jnp.zeros((out.shape[0] - middle, out.shape[1]), jnp.float32)


def with_row(rows, value, out):
    count = rows.shape[0]
    out[:count, :] = rows[...]
    row = lax.broadcasted_iota(jnp.int32, (8, rows.shape[1]), 0)
    out[count:, :] = jnp.where(row == 0, value, 0.0)


def left_kernel(bits, mine, other, inverse, left, rows):
    half = mine.shape[0]
    rows[pl.ds(pl.multiple_of(bits[0] * half, 8), half), :] = mine[...]
    rows[pl.ds(pl.multiple_of((1 - bits[0]) * half, 8), half), :] = other[...]
    left[...] = dot(rows[...], inverse[...], ((1,), (1,)))


def forward_kernel(one, two, squares, first, second):
    middle = second.shape[0]
    with_row(two.at[:middle], squares[...], first)
    second[...] = one[middle:, :]


def columns_of(bits, k, width):
    return pl.ds(pl.multiple_of((bits[2] ^ k) * width, lanes), width)


def in_order(bits, mine, other):
    lower = jnp.concatenate([mine, other], axis=1)
    return jnp.where(bits[4] == 0, lower, jnp.concatenate([other, mine], axis=1))


def momentum_kernel(scale, bits, left, own_right, rights, *refs):
    pieces, received, refs = refs[:3], refs[3:6], refs[6:]
    new_momentum, left_scaled, own_splits, splits, ready, left_ready, sent = refs
    left_ready[...] = left[...] * scale
    copies = [pltpu.make_async_copy(left_ready, left_scaled, sent.at[3])]
    copies[0].start()
    width = pieces[0].shape[1]
    half = width // 2
    own_splits[:half, :] = three_right(own_right[...])
    own_splits[half:, :] = three_right(rights[...])
    for k in range(3):
        splits[k * half : (k + 1) * half, :] = three_right(received[k][...])
    scaled = three_left(left[...])
    for k in range(3):
        at = slice(k * half, (k + 1) * half)
        mine, other = dot_three(scaled, own_splits[at, :]), dot_three(scaled, splits[at, :])
        ready[k] = pieces[k][...] - 0.5 * in_order(bits, mine, other)
        target = new_momentum.at[:, columns_of(bits, k, width)]
        copies.append(pltpu.make_async_copy(ready.at[k], target, sent.at[k]))
        copies[-1].start()
    for copy in copies:
        copy.wait()


def diagonal_kernel(left, one, two, rights, splits, product):
    middle = rights.shape[0] // 2
    rights[:middle, :] = one[:middle, :]
    rights[middle:, :] = two[:middle, :]
    splits[...] = three_right(rights[...])
    product[...] = dot_three(three_left(left[...]), splits[...])


def last_kernel(factor, bits, squares, left, own_right, rights, own_splits, splits, *refs):
    received, refs = refs[:3], refs[3:]
    first, second, last_own, own_last_splits, last_product, piece, _ = refs[:7]
    new_momentum, update, next_basis = refs[7:10]
    last_received, last_splits, ready, scaled_ready, basis_ready, sent = refs[10:]
    half, width = basis_ready.shape[0], piece.shape[1]
    middle = half // 2
    norm = jnp.sqrt(squares[...] + first[middle : middle + 1, :] + epsilon)
    copies = []

    def send(source, target, index):
        copies.append(pltpu.make_async_copy(source, target, sent.at[index]))
        copies[-1].start()

    last_received[:middle, :] = first[:middle, :]
    last_received[middle:, :] = second[...]
    last_splits[...] = three_right(last_received[...])
    other = dot_three(three_left(left[...]), last_splits[...])
    ready[...] = piece[...] - 0.5 * in_order(bits, last_product[...], other)
    send(ready, new_momentum.at[:, columns_of(bits, square - 1, width)], square)
    for k in range(square):

        @pl.when((bits[3] // 2) ^ bits[2] == k)
        def _():
            beside = [rights[i * half : (i + 1) * half, :] for i in range(2)]
            mine = [own_right[...], *beside, last_own[...]][k]
            other = last_received[...] if k == square - 1 else received[k][...]
            basis_ready[...] = jnp.where(bits[3] % 2 == bits[4], mine, other) / norm

    send(basis_ready, next_basis, square + 1)
    scaled = three_left(left[...] * (factor / norm))
    for k in range(square):
        if k < square - 1:
            parts = slice(k * half, (k + 1) * half)
            mine = dot_three(scaled, own_splits[parts, :])
            other = dot_three(scaled, splits[parts, :])
        else:
            mine = dot_three(scaled, own_last_splits[...])
            other = dot_three(scaled, last_splits[...])
        scaled_ready[k] = in_order(bits, mine, other).astype(jnp.bfloat16)
        send(scaled_ready.at[k], update.at[:, columns_of(bits, k, width)], k)
    for copy in copies:
        copy.wait()


def in_squares(momentum, gradient, right_basis):
    device = lax.axis_index("fsdp")
    tensor = lax.axis_index("tensor")
    bits = jnp.stack([tensor % 2, tensor // 2, device % square, device, device // square])
    bits = bits.astype(jnp.int32)
    rows, cols = momentum.shape
    rank = right_basis.shape[1]
    half, width = rows // 2, cols // square
    total_rows = rows * lax.axis_size("fsdp")
    total_cols = cols * lax.axis_size("tensor")

    pieces = kernel(split_kernel, [shape(rows, width)] * square, [smem, vmem, vmem], [], "split_sum")(
        bits, momentum, gradient
    )
    columns = [pieces[0]] + [swap(pieces[k], "fsdp", k) for k in range(1, square)]

    sent, kept = kernel(
        part_left_kernel,
        [shape(half, rank)] * 2,
        [smem] + [vmem] * 3 + [anywhere],
        [pltpu.VMEM((rows, rank), jnp.float32)],
        "part_left",
    )(bits, right_basis, momentum, gradient, pieces[0])
    cores = [[i, i + 1] for i in range(0, lax.axis_size("tensor"), 2)]
    both = lax.all_gather(sent, "tensor", axis=0, tiled=True, axis_index_groups=cores)
    mine = kernel(core_add_kernel, shape(half, rank), [smem, vmem, vmem], [], "core_add")(
        bits, kept, both
    )
    mine = add_after(mine, swap(mine, "tensor", 2), *columns[1:])
    gathered = [mine] + [swap(mine, "fsdp", k) for k in range(1, square)]
    others = [swap(part, "tensor", 1) for part in gathered]

    count = rank // lanes
    stacked = count * (count + 1) // 2 * lanes
    share = stacked // 8
    gram_sent, gram_kept = kernel(
        gram_kernel,
        [shape(share, lanes)] * 2,
        [smem] + [vmem] * square,
        [pltpu.VMEM((square * half, rank), jnp.float32), pltpu.VMEM((stacked, lanes), jnp.float32)],
        "part_gram",
    )(bits, *gathered)
    part = gram_kept + swap(gram_sent, "tensor", 1)

    sent, kept = kernel(
        raw_kernel,
        [shape(width // 2, rank)] * 2,
        [smem, anywhere] + [vmem] * (3 * square),
        [
            pltpu.VMEM((square * rows, width), jnp.float32),
            pltpu.VMEM((square * rows, rank), jnp.float32),
            pltpu.VMEM((width, rank), jnp.float32),
        ],
        "part_raw",
    )(bits, part, *gathered, *others, *columns)

    part = add_after(part, swap(part, "fsdp", square), kept)
    chips = [[i, i + 1] for i in range(0, lax.axis_size("fsdp"), 2)]
    quarter = lax.all_gather(part, "fsdp", axis=0, tiled=True, axis_index_groups=chips)
    over_planes = swap(quarter, "tensor", 2)
    shares = [quarter, swap(quarter, "tensor", 1), over_planes, swap(over_planes, "tensor", 1)]

    first_block, work = first_step(bits, shares, rank)
    own = add_after(kept, swap(sent, "fsdp", square), first_block)

    half_width = width // 2
    received = swap(own, "fsdp", square)
    beside = [swap(own, "fsdp", k) for k in (1, 2)]
    inverse, own_right, squares = later_steps(work, first_block, own)
    received_right, squares = kernel(
        norm_kernel,
        [shape(half_width, rank), shape(1, rank)],
        [vmem] * 2 + [anywhere] * 2 + [vmem],
        [],
        "norms",
    )(inverse, squares, *beside, received)
    received_rows = [received_right] + [swap(received_right, "fsdp", k) for k in (1, 2)]
    for flip in (1, 2):
        squares = squares + swap(squares, "tensor", flip)

    half_rows = shape(half_width // 2, rank)
    with_norms = shape(half_width // 2 + 8, rank)
    padded = shape(half_width // 2 + 8, rank)
    rights, own_first, own_second = kernel(
        beside_kernel,
        [shape(2 * half_width, rank), padded, padded],
        [vmem] * 3 + [anywhere],
        [],
        "beside",
    )(inverse, *beside, squares)
    own_first, own_second = swap(own_first, "fsdp", 1), swap(own_second, "fsdp", 2)
    squares = squares + swap(squares, "fsdp", 2)
    left = kernel(
        left_kernel,
        shape(rows, rank),
        [smem] + [vmem] * 3,
        [pltpu.VMEM((rows, rank), jnp.float32)],
        "left",
        cost=2**23,
    )(bits, mine, others[0], inverse)
    first, second = kernel(
        forward_kernel, [with_norms, half_rows], [vmem] * 3, [], "forward"
    )(received_rows[1], received_rows[2], squares)
    first, second = swap(first, "fsdp", 1), swap(second, "fsdp", 2)

    splits_shape = shape(3 * half_width, 3 * rank, dtype=jnp.bfloat16)
    new_momentum, left_scaled, own_splits, splits = kernel(
        functools.partial(momentum_kernel, math.sqrt(total_rows)),
        [shape(rows, cols), shape(rows, rank), splits_shape, splits_shape],
        [smem] + [vmem] * 9,
        [
            pltpu.VMEM((3, rows, width), jnp.float32),
            pltpu.VMEM((rows, rank), jnp.float32),
            pltpu.SemaphoreType.DMA((4,)),
        ],
        "new_momentum",
        cost=2**24,
        out_specs=[anywhere] * 2 + [vmem] * 2,
    )(bits, left, own_right, rights, *pieces[:3], *received_rows)
    last_own = kernel(
        diagonal_kernel,
        [
            shape(half_width, rank),
            shape(half_width, 3 * rank, dtype=jnp.bfloat16),
            shape(rows, half_width),
        ],
        [vmem] * 3,
        [],
        "diagonal",
    )(left, own_first, own_second)
    new_momentum, update, next_basis = kernel(
        functools.partial(last_kernel, math.sqrt(total_rows / total_cols)),
        [
            shape(rows, cols),
            shape(rows, cols, dtype=jnp.bfloat16),
            shape(cols // lax.axis_size("fsdp"), rank),
        ],
        [smem] + [vmem] * 15 + [anywhere],
        [
            pltpu.VMEM((half_width, rank), jnp.float32),
            pltpu.VMEM((half_width, 3 * rank), jnp.bfloat16),
            pltpu.VMEM((rows, width), jnp.float32),
            pltpu.VMEM((square, rows, width), jnp.bfloat16),
            pltpu.VMEM((half_width, rank), jnp.float32),
            pltpu.SemaphoreType.DMA((square + 2,)),
        ],
        "last",
        out_specs=[anywhere] * 3,
        aliases={16: 0},
    )(
        *(bits, squares, left, own_right, rights, own_splits, splits, *received_rows),
        *(first, second, *last_own, pieces[3], new_momentum),
    )
    return (update, new_momentum, left_scaled, next_basis)


def on_device(momentum, gradient, right_basis):
    rows, cols = momentum.shape
    pairs = lax.axis_size("fsdp") == 2 * square and lax.axis_size("tensor") == 4
    aligned = rows % 16 == 0 and cols % (square * lanes) == 0 and right_basis.shape[1] % lanes == 0
    plan = in_squares if pairs and aligned else any_mesh
    return plan(momentum, gradient, right_basis)


def solution(mesh):
    in_specs = (P("fsdp", "tensor"), P("fsdp", "tensor"), P("tensor", None))
    out_specs = (
        P("fsdp", "tensor"),
        P("fsdp", "tensor"),
        P("fsdp", None),
        P(("tensor", "fsdp"), None),
    )
    return jax.shard_map(
        on_device, mesh=mesh, in_specs=in_specs, out_specs=out_specs, check_vma=False
    )
```
